32 devices in a mesh: slab: 8 (over z, x), chan: 4 (over y, core).
Axes of the slice: x: 2, y: 2, z: 4, core: 2. Of those that a mesh axis runs over, the one named last changes fastest.
Arguments:
- stream_speed_field: bfloat16 [3, 8, 8, 8, 16384], P(None, None, None, None, ('slab', 'chan')), may hold values from -6 to 6
- liquid_to_solid_element: int32 [16384], P(('slab', 'chan')), may hold values from 0 to 16383, as said below
- previous_panel_warmth: float32 [8, 8, 8, 8, 2048], P(None, None, None, 'chan', 'slab'), may hold values from -6 to 6
- pointwise_energy_source: float32 [8, 8, 8, 8, 2048], P(None, None, None, 'chan', 'slab'), may hold values from -6 to 6
- coked_element_flags: int32 [8, 2048], P('chan', 'slab'), may hold values from 0 to 1, as said below
- coking_thickness_plies: int32 [8, 2048], P('chan', 'slab'), may hold values from 1 to 8
Outputs:
- stepped_stream_speed: bfloat16 [3, 8, 8, 8, 16384], P(None, None, None, None, ('slab', 'chan'))
- solved_panel_warmth: float32 [8, 8, 8, 8, 2048], P(None, None, None, 'chan', 'slab')
The draws below stay inside these ranges and needn't reach their ends.
Inputs may be any that keep to these rules, and one draw needn't show every extreme that they name: `liquid_to_solid_element`: A permutation of the element numbers. Element n belongs to thermal device n // 512 (devices numbered slab first, then chan) at local position n % 512. The fluid device f holds 256 elements of thermal device f and at most 128 of each of the thermal devices f + 1, f - 1 and f + 4 (modulo the number of devices), none of any other; these three counts are the same for every f, and one of them is 128. `coked_element_flags`: at most 192 flagged elements among one thermal device's elements, and exactly 192 on some device.
All inputs are finite; a program needn't handle non-finite values.
Results may differ from the reference program's by a relative error of at most 0.005.
Values may be sent and summed in bfloat16 or wider, within the bound.
No kernel may reach another device: no remote copies, remote signals or barrier semaphores. Data moves between devices by JAX's collectives and lax.ppermute only.
A program may use at most 128 MiB of HBM per device.

```python
import jax
import jax.numpy as jnp
import numpy as np
from jax import lax

A_DEV = 256
L_DEV = 2
ITERS = 5
E_DEV = 512
HALF = 256
CAP = 128
DEP_CAP = 192
LENGTHWISE_TOTAL = 2048
CROSSWISE_TOTAL = 8
E_TOTAL = 16384
N_SLAB = 8
N_CHAN = 4


def shuffled(seed_key):
    return jax.random.permutation(seed_key, E_DEV).astype(jnp.int32)


def draw_liquid_to_solid_element(key, part):
    device_total = N_SLAB * N_CHAN
    split_value = jax.random.randint(jax.random.fold_in(key, 1), (), 1, CAP).astype(jnp.int32)
    rotation = jax.random.randint(jax.random.fold_in(key, 2), (), 0, 3)
    triple = jnp.stack([jnp.int32(CAP), split_value, jnp.int32(CAP) - split_value])
    triple = jnp.roll(triple, rotation)
    positions = jnp.arange(E_DEV, dtype=jnp.int32)
    offset_group = (positions >= HALF).astype(jnp.int32) + (positions >= HALF + triple[0]).astype(jnp.int32) + (positions >= HALF + triple[0] + triple[1]).astype(jnp.int32)
    shift_table = jnp.array([0, 1, device_total - 1, N_CHAN], jnp.int32)
    shifts = shift_table[offset_group]
    senders = jnp.arange(device_total, dtype=jnp.int32)[:, None]
    target_dev = (senders + shifts[None, :]) % device_total
    receive_order = jax.vmap(shuffled)(jax.random.split(jax.random.fold_in(key, 3), device_total))
    send_order = jax.vmap(shuffled)(jax.random.split(jax.random.fold_in(key, 4), device_total))
    values = target_dev * E_DEV + receive_order[target_dev, positions[None, :]]
    mapping = jnp.zeros((device_total, E_DEV), jnp.int32).at[senders, send_order].set(values)
    return mapping.reshape(-1)


def draw_coked_element_flags(key, part):
    device_total = N_SLAB * N_CHAN
    counts = jax.random.randint(jax.random.fold_in(key, 21), (device_total,), E_DEV // 16, 3 * E_DEV // 16)
    busiest = jax.random.randint(jax.random.fold_in(key, 22), (), 0, device_total)
    counts = jnp.where(jnp.arange(device_total) == busiest, DEP_CAP, counts)
    ranking = jax.vmap(shuffled)(jax.random.split(jax.random.fold_in(key, 23), device_total))
    flag_grid = (ranking < counts[:, None]).astype(jnp.int32)
    flag_grid = flag_grid.reshape(N_SLAB, N_CHAN, L_DEV, A_DEV).transpose(1, 2, 0, 3)
    return flag_grid.reshape(CROSSWISE_TOTAL, LENGTHWISE_TOTAL)


def set_ends(values, stream_key, least, top_value):
    longest = values.shape.index(max(values.shape))
    spots = []
    for shift in (0, 1):
        where = [jax.random.randint(jax.random.fold_in(stream_key, axis), (), 0, length) for axis, length in enumerate(values.shape)]
        where[longest] = (where[longest] + shift) % values.shape[longest]
        spots.append(tuple(where))
    return values.at[spots[0]].set(least).at[spots[1]].set(top_value)


def steps_of(own_key, dims, cuts, smallest, top_value):
    def one(axis_at, parts):
        draws = jax.random.uniform(jax.random.fold_in(jax.random.fold_in(own_key, 6), axis_at), (parts,), jnp.float32, smallest / len(cuts), top_value / len(cuts))
        return jnp.repeat(jnp.exp(draws), dims[axis_at] // parts).reshape((-1,) + (1,) * (len(dims) - axis_at - 1))

    loudness = one(*cuts[0])
    for cut in cuts[1:]:
        loudness = loudness * one(*cut)
    return loudness


def centred(own_key, dims, width, limit, pieces=(), kind=jnp.bfloat16):
    drawn = jax.random.normal(own_key, dims, jnp.float32) * width
    if len(pieces) > 0:
        drawn = steps_of(own_key, dims, pieces, -0.22, 0.18) * drawn
    return jnp.clip(drawn, min=-limit, max=limit).astype(kind)


def setup_inputs(seed: int = 0) -> dict:
    arg_keys = jax.random.split(jax.random.key(seed), 7)
    return {
        "stream_speed_field": centred(arg_keys[0], (3, 8, 8, 8, E_TOTAL), 1.0, 6.0, ((4, 32),)),
        "liquid_to_solid_element": draw_liquid_to_solid_element(jax.random.fold_in(arg_keys[6], 71), 0),
        "previous_panel_warmth": centred(arg_keys[2], (8, 8, 8, CROSSWISE_TOTAL, LENGTHWISE_TOTAL), 1.0, 6.0, ((3, 4), (4, 8)), jnp.float32),
        "pointwise_energy_source": centred(arg_keys[3], (8, 8, 8, CROSSWISE_TOTAL, LENGTHWISE_TOTAL), 1.0, 6.0, ((3, 4), (4, 8)), jnp.float32),
        "coked_element_flags": draw_coked_element_flags(jax.random.fold_in(arg_keys[6], 71), 0),
        "coking_thickness_plies": set_ends(jax.random.randint(arg_keys[5], (CROSSWISE_TOTAL, LENGTHWISE_TOTAL), 1, 9), jax.random.fold_in(arg_keys[5], 1), 1, 8).astype(jnp.int32),
    }


highest = lax.Precision.HIGHEST
coolant_throughput = 0.05
time_step = 0.01
viscosity = 0.02
cross_gain = 0.4
layer_damp = 0.25
forward_forms = ("ir,rst...->ist...", "js,rst...->rjt...", "kt,rst...->rsk...")
backward_forms = ("ir,ist...->rst...", "js,rjt...->rst...", "kt,rsk...->rst...")
fluid_forms = ("ir,crste->ciste", "js,crste->crjte", "kt,crste->crske")


def gll_tables():
    points = np.array([-1.0, -0.8717401485096066, -0.5917001814331423, -0.2092992179024789, 0.2092992179024789, 0.5917001814331423, 0.8717401485096066, 1.0])
    weights = np.array([1.0 / 28.0, 0.2107042271435061, 0.3411226924835044, 0.4124587946587038, 0.4124587946587038, 0.3411226924835044, 0.2107042271435061, 1.0 / 28.0])
    lower_poly = np.ones(8)
    upper_poly = points.copy()
    for degree in range(1, 7):
        next_poly = ((2 * degree + 1) * points * upper_poly - degree * lower_poly) / (degree + 1)
        lower_poly = upper_poly
        upper_poly = next_poly
    gaps_matrix = points[:, None] - points[None, :] + np.eye(8)
    derivative = upper_poly[:, None] / (upper_poly[None, :] * gaps_matrix)
    derivative = derivative * (1.0 - np.eye(8))
    derivative[0, 0] = -14.0
    derivative[7, 7] = 14.0
    return jnp.asarray(derivative, jnp.float32), jnp.asarray(weights, jnp.float32)


def forward(matrix, field, conjugate_update_vector):
    return jnp.einsum(forward_forms[conjugate_update_vector], matrix, field, precision=highest)


def backward(matrix, field, conjugate_update_vector):
    return jnp.einsum(backward_forms[conjugate_update_vector], matrix, field, precision=highest)


def fluid_update(velocity_block, matrix):
    velocity_now = velocity_block.astype(jnp.float32)
    gradients = [jnp.einsum(fluid_forms[conjugate_update_vector], matrix, velocity_now, precision=highest) for conjugate_update_vector in range(3)]
    convect = velocity_now[0:1] * gradients[0] + velocity_now[1:2] * gradients[1] + velocity_now[2:3] * gradients[2]
    laplace = jnp.einsum(fluid_forms[0], matrix, gradients[0], precision=highest)
    laplace = laplace + jnp.einsum(fluid_forms[1], matrix, gradients[1], precision=highest)
    laplace = laplace + jnp.einsum(fluid_forms[2], matrix, gradients[2], precision=highest)
    updated = velocity_now + time_step * (viscosity * laplace - convect)
    return updated.astype(jnp.bfloat16)


def conductivity_of(stepped_stream_speed):
    faster = stepped_stream_speed.astype(jnp.float32)
    return (1.0 + 0.5 * (faster[0] * faster[0] + faster[1] * faster[1] + faster[2] * faster[2])).astype(jnp.bfloat16)


def local_operator(field, weighted_kappa, cross_el, matrix, integration_factor):
    gradients = [forward(matrix, field, conjugate_update_vector) for conjugate_update_vector in range(3)]
    summed = coolant_throughput * integration_factor * field
    summed = summed + backward(matrix, weighted_kappa * gradients[0], 0)
    summed = summed + backward(matrix, weighted_kappa * gradients[1], 1)
    summed = summed + backward(matrix, weighted_kappa * gradients[2], 2)
    mixed = backward(matrix, weighted_kappa * gradients[1], 0) + backward(matrix, weighted_kappa * gradients[0], 1)
    return summed + cross_el * mixed


def collect_assembled_points(field):
    shared = field[7, :, :, :, :-1] + field[0, :, :, :, 1:]
    field = field.at[7, :, :, :, :-1].set(shared).at[0, :, :, :, 1:].set(shared)
    shared = field[:, 7, :, :-1, :] + field[:, 0, :, 1:, :]
    field = field.at[:, 7, :, :-1, :].set(shared).at[:, 0, :, 1:, :].set(shared)
    return field


def multiplicity(count_l, count_a, first_l, first_a, total_l, total_a):
    node_index = jnp.arange(8, dtype=jnp.int32)
    axial_pos = first_a + jnp.arange(count_a, dtype=jnp.int32)
    lateral_pos = first_l + jnp.arange(count_l, dtype=jnp.int32)
    along_axial = 1 + ((node_index[:, None] == 0) & (axial_pos[None, :] > 0)).astype(jnp.int32) + ((node_index[:, None] == 7) & (axial_pos[None, :] < total_a - 1)).astype(jnp.int32)
    along_lateral = 1 + ((node_index[:, None] == 0) & (lateral_pos[None, :] > 0)).astype(jnp.int32) + ((node_index[:, None] == 7) & (lateral_pos[None, :] < total_l - 1)).astype(jnp.int32)
    return (along_axial[:, None, None, None, :] * along_lateral[None, :, None, :, None]).astype(jnp.float32)


def reference(stream_speed_field, liquid_to_solid_element, previous_panel_warmth, pointwise_energy_source, coked_element_flags, coking_thickness_plies):
    matrix, node_gll = gll_tables()
    integration_factor = (node_gll[:, None, None] * node_gll[None, :, None] * node_gll[None, None, :])[:, :, :, None, None]
    device_total = N_SLAB * N_CHAN
    blocks = stream_speed_field.reshape(3, 8, 8, 8, device_total, E_DEV).transpose(4, 0, 1, 2, 3, 5)

    def per_block(velocity_block):
        next_block = fluid_update(velocity_block, matrix)
        return next_block, conductivity_of(next_block)

    next_blocks, cond_blocks = lax.map(per_block, blocks)
    stepped_stream_speed = next_blocks.transpose(1, 2, 3, 4, 0, 5).reshape(3, 8, 8, 8, E_TOTAL)
    cond_flat = cond_blocks.transpose(1, 2, 3, 0, 4).reshape(512, E_TOTAL)
    moved = jnp.zeros((512, E_TOTAL), jnp.bfloat16).at[:, liquid_to_solid_element].set(cond_flat)
    moved = moved.reshape(8, 8, 8, N_SLAB, N_CHAN, L_DEV, A_DEV).transpose(0, 1, 2, 4, 5, 3, 6).reshape(8, 8, 8, CROSSWISE_TOTAL, LENGTHWISE_TOTAL)
    layer_float = coking_thickness_plies.astype(jnp.float32)
    flag_float = coked_element_flags.astype(jnp.float32)
    damping = jnp.where(coked_element_flags == 1, 1.0 / (1.0 + layer_damp * layer_float), jnp.ones_like(layer_float))
    kappa = moved.astype(jnp.float32) * damping
    weighted_kappa = integration_factor * kappa
    cross_el = cross_gain * flag_float * layer_float / (layer_float + 1.0)
    inv_mult = 1.0 / multiplicity(CROSSWISE_TOTAL, LENGTHWISE_TOTAL, 0, 0, CROSSWISE_TOTAL, LENGTHWISE_TOTAL)

    def apply_operator(field):
        return collect_assembled_points(local_operator(field, weighted_kappa, cross_el, matrix, integration_factor))

    source_vector = collect_assembled_points(integration_factor * (coolant_throughput * previous_panel_warmth + pointwise_energy_source))
    solved_panel_warmth = jnp.zeros_like(source_vector)
    residual = source_vector
    conjugate_update_vector = source_vector
    norm_now = jnp.sum(residual * residual * inv_mult)
    for number in range(ITERS):
        applied = apply_operator(conjugate_update_vector)
        conjugate_alpha_factor = norm_now / jnp.sum(conjugate_update_vector * applied * inv_mult)
        solved_panel_warmth = solved_panel_warmth + conjugate_alpha_factor * conjugate_update_vector
        residual = residual - conjugate_alpha_factor * applied
        norm_next = jnp.sum(residual * residual * inv_mult)
        conjugate_update_vector = residual + (norm_next / norm_now) * conjugate_update_vector
        norm_now = norm_next
    return stepped_stream_speed, solved_panel_warmth
```

```python
import functools

import jax
import jax.numpy as jnp
import numpy as np
from jax import lax
from jax.experimental import pallas as pl
from jax.experimental.pallas import tpu as pltpu
from jax.sharding import PartitionSpec as P

ITERS = 5
LANES = 128
RIM = 8
KRYLOV_SCALE = 1.0 / 256.0

highest = lax.Precision.HIGHEST
f32 = jnp.float32
bf16 = jnp.bfloat16
coolant_throughput = 0.05
time_step = 0.01
viscosity = 0.02
cross_gain = 0.4
layer_damp = 0.25

NT = (((1,), (1,)), ((), ()))
TN = (((0,), (0,)), ((), ()))


def gll_tables():
    points = np.array(
        [
            -1.0,
            -0.8717401485096066,
            -0.5917001814331423,
            -0.2092992179024789,
            0.2092992179024789,
            0.5917001814331423,
            0.8717401485096066,
            1.0,
        ]
    )
    weights = np.array(
        [
            1.0 / 28.0,
            0.2107042271435061,
            0.3411226924835044,
            0.4124587946587038,
            0.4124587946587038,
            0.3411226924835044,
            0.2107042271435061,
            1.0 / 28.0,
        ]
    )
    lower_poly = np.ones(8)
    upper_poly = points.copy()
    for degree in range(1, 7):
        next_poly = ((2 * degree + 1) * points * upper_poly - degree * lower_poly) / (degree + 1)
        lower_poly = upper_poly
        upper_poly = next_poly
    gaps_matrix = points[:, None] - points[None, :] + np.eye(8)
    derivative = upper_poly[:, None] / (upper_poly[None, :] * gaps_matrix)
    derivative = derivative * (1.0 - np.eye(8))
    derivative[0, 0] = -14.0
    derivative[7, 7] = 14.0
    return derivative, weights


DERIV, GLL_W = gll_tables()
DERIV = DERIV.astype(np.float32).astype(np.float64)
GLL_W = GLL_W.astype(np.float32).astype(np.float64)


def split_hi_lo(matrix):
    high = np.asarray(matrix, np.float32).astype(jnp.bfloat16)
    low = (np.asarray(matrix, np.float64) - high.astype(np.float64)).astype(np.float32)
    return high, low.astype(jnp.bfloat16)


def line_matrices():
    out = []
    for matrix in (DERIV, DERIV.T):
        high, low = split_hi_lo(np.kron(np.eye(32), matrix))
        out.append(np.concatenate([high, low, high], 1))
    return out


def fluid_matrices():
    eye8 = np.eye(8)
    square = DERIV @ DERIV
    first = np.kron(DERIV, np.eye(64))
    laplace = (
        np.kron(square, np.eye(64))
        + np.kron(np.kron(eye8, square), eye8)
        + np.kron(np.eye(64), square)
    )
    second = np.kron(np.kron(np.eye(4), DERIV), eye8)
    third = np.kron(np.eye(32), DERIV)
    return [np.concatenate(split_hi_lo(m), 1) for m in (first, laplace, second, third)]


def along(matrix, line):
    even = [line[j] + line[7 - j] for j in range(4)]
    odd = [line[j] - line[7 - j] for j in range(4)]
    result = [None] * 8
    for i in range(4):
        p = sum(float(0.5 * (matrix[i, j] + matrix[i, 7 - j])) * even[j] for j in range(4))
        q = sum(float(0.5 * (matrix[i, j] - matrix[i, 7 - j])) * odd[j] for j in range(4))
        result[i] = p + q
        result[7 - i] = q - p
    return result


def lane_index(rows=8):
    return lax.broadcasted_iota(jnp.int32, (rows, LANES), 1)


def vmem(shape, dtype=f32):
    return pltpu.VMEM(shape, dtype)


def call(kernel, out_shape, *args, smem=0, scratch=(), cost=None, limit=48, **kw):
    specs = [pl.BlockSpec(memory_space=pltpu.SMEM)] * smem
    specs += [pl.BlockSpec(memory_space=pltpu.VMEM)] * (len(args) - smem)
    outs = [pl.BlockSpec(memory_space=pltpu.VMEM) for _ in out_shape]
    return pl.pallas_call(
        kernel,
        in_specs=specs,
        out_specs=outs,
        out_shape=out_shape,
        scratch_shapes=scratch,
        cost_estimate=cost,
        compiler_params=pltpu.CompilerParams(vmem_limit_bytes=limit * 1024 * 1024),
        **kw,
    )(*args)


def weight_rows(wt):
    return [[float(GLL_W[r] * GLL_W[s]) * wt for s in range(8)] for r in range(8)]


def sel_matrix(l, first_lane):
    row = lax.broadcasted_iota(jnp.int32, (2 * RIM, LANES), 0)
    lane = lax.broadcasted_iota(jnp.int32, (2 * RIM, LANES), 1)
    return ((row - l * RIM + first_lane == lane) & (row >= l * RIM) & (row < (l + 1) * RIM)).astype(f32)


def place_matrix(first_lane):
    row = lax.broadcasted_iota(jnp.int32, (2 * RIM, LANES), 0)
    lane = lax.broadcasted_iota(jnp.int32, (2 * RIM, LANES), 1)
    target = jnp.where(row < RIM, row + first_lane, row - RIM + first_lane + LANES // 2)
    return (target == lane).astype(f32)


def send_rims(tile_rows, na):
    behind = sum(
        lax.dot_general(sel_matrix(l, 0), tile_rows(l * na), NT, precision=highest, preferred_element_type=f32)
        for l in range(2)
    )
    ahead = sum(
        lax.dot_general(
            sel_matrix(l, LANES - RIM), tile_rows(l * na + na - 1), NT, precision=highest, preferred_element_type=f32
        )
        for l in range(2)
    )
    return behind, ahead


def place_rims(from_ahead, from_behind):
    a = lax.dot_general(from_ahead, place_matrix(0), TN, precision=highest, preferred_element_type=f32)
    b = lax.dot_general(
        from_behind, place_matrix(LANES // 2 - RIM), TN, precision=highest, preferred_element_type=f32
    )
    return a + b


def source_kernel(na, p_ref, q_ref, dc_ref, wt_ref, z_ref, behind_ref, ahead_ref):
    rows = weight_rows(wt_ref[...])
    step = 2 * na
    for r in range(8):
        for s in range(8):
            base = (r * 8 + s) * 8 * step
            for l in range(2):
                for at in range(na):
                    pick = pl.ds(base + at * 2 + l, 8, stride=step)
                    z_ref[l * na + at, r, s] = rows[r][s] * (coolant_throughput * p_ref[pick, :] + q_ref[pick, :])

    def tile_rows(j):
        cols = pl.ds(j * LANES, LANES)
        extra = [
            jnp.broadcast_to(dc_ref[0:1, cols], (8, LANES)),
            jnp.broadcast_to(dc_ref[1:2, cols], (8, LANES)),
            jnp.zeros((LANES - 16, LANES), f32),
        ]
        return jnp.concatenate([z_ref[j].reshape(512, LANES)] + extra, 0)

    behind, ahead = send_rims(tile_rows, na)
    behind_ref[...] = behind
    ahead_ref[...] = ahead


def assemble(na, y, lo_ref, hi_ref):
    ghost = 2 * na
    lane = lane_index()
    first = lane == 0
    last = lane == LANES - 1
    half = LANES // 2
    roll = pltpu.roll
    for s in range(8):
        far = [y[j, 7, s] for j in range(ghost + 1)]
        near = [y[j, 0, s] for j in range(ghost + 1)]
        right = [roll(f, 1, 1) for f in far]
        left = [roll(f, LANES - 1, 1) for f in near]
        far_half = [roll(far[na * 2 - 1], half + 1, 1), roll(far[ghost], half + 1, 1)]
        near_half = [roll(near[0], half - 1, 1), roll(near[ghost], half - 1, 1)]
        for l in range(2):
            for at in range(na):
                j = l * na + at
                if at > 0:
                    carry = right[j - 1]
                else:
                    carry = far_half[1] if l == 0 else right[ghost]
                y[j, 0, s] = near[j] + jnp.where(first, carry, right[j])
                if at < na - 1:
                    carry = left[j + 1]
                else:
                    carry = left[ghost] if l == 0 else near_half[1]
                y[j, 7, s] = far[j] + jnp.where(last, carry, left[j])
        from_left = jnp.where(first, right[na - 1], jnp.where(lane == half, far_half[0], right[ghost]))
        y[ghost, 0, s] = near[ghost] + from_left
        from_right = jnp.where(last, left[na], jnp.where(lane == half - 1, near_half[0], left[ghost]))
        y[ghost, 7, s] = far[ghost] + from_right
    low = lane < half
    for r in range(8):
        for at in range(na):
            shared = y[at, r, 7] + y[na + at, r, 0]
            y[at, r, 7] = shared
            y[na + at, r, 0] = shared
            lo_ref[at, r] = y[at, r, 0]
            hi_ref[at, r] = y[na + at, r, 7]
        upper = y[ghost, r, 7]
        lower = y[ghost, r, 0]
        new_upper = upper + jnp.where(low, roll(lower, half, 1), 0.0)
        new_lower = lower + jnp.where(low, 0.0, roll(upper, half, 1))
        y[ghost, r, 7] = new_upper
        y[ghost, r, 0] = new_lower
        lo_ref[na, r] = jnp.where(low, new_lower, 0.0)
        hi_ref[na, r] = jnp.where(low, roll(new_upper, half, 1), 0.0)


def faces_out(parity, lo, hi, a_ref, b_ref):
    even = parity == 0
    a_ref[...] = jnp.where(even, hi[...], lo[...])
    b_ref[...] = jnp.where(even, lo[...], hi[...])


def add_faces(na, parity, v, a_ref, b_ref):
    even = parity == 0
    ghost = 2 * na
    for r in range(8):
        for at in range(na + 1):
            a, b = a_ref[at, r], b_ref[at, r]
            upper = jnp.where(even, a, b)
            lower = jnp.where(even, b, a)
            if at < na:
                v[at, r, 0] = v[at, r, 0] + lower
                v[na + at, r, 7] = v[na + at, r, 7] + upper
            else:
                v[ghost, r, 0] = v[ghost, r, 0] + lower
                v[ghost, r, 7] = v[ghost, r, 7] + pltpu.roll(upper, LANES // 2, 1)


def source_assembly_kernel(
    na, par_ref, z_ref, from_ahead, from_behind, dc_ref, y_ref, cr_ref, a_ref, b_ref, lo, hi
):
    ghost = 2 * na
    y_ref[0:ghost] = z_ref[...]
    tile = place_rims(from_ahead[...], from_behind[...])
    y_ref[ghost] = tile[:512].reshape(8, 8, 8, LANES)
    for j in range(ghost):
        cr_ref[j] = jnp.broadcast_to(dc_ref[1:2, j * LANES : (j + 1) * LANES], (8, LANES))
    cr_ref[ghost] = tile[520:528]
    assemble(na, y_ref, lo, hi)
    faces_out(par_ref[0], lo, hi, a_ref, b_ref)


def fluid_kernel(
    chan, total, me_ref, u_ref, l2s_ref, k1_ref, kl_ref, k2_ref, k3_ref, out_ref, own_ref, s1_ref, s2_ref, s3_ref, c_ref
):
    i = pl.program_id(0)
    width = u_ref.shape[-1]
    u = u_ref[...].astype(f32)
    ub = [u[c].reshape(512, width).astype(bf16) for c in range(3)]
    uf = [x.astype(f32) for x in ub]

    def whole(k_ref, x):
        return jnp.dot(k_ref[...], jnp.concatenate([x, x], 0), preferred_element_type=f32)

    def halves(k_ref, x):
        parts = []
        for h in range(2):
            part = x[h * 256 : (h + 1) * 256]
            parts.append(jnp.dot(k_ref[...], jnp.concatenate([part, part], 0), preferred_element_type=f32))
        return jnp.concatenate(parts, 0)

    speed = None
    for c in range(3):
        convect = uf[0] * whole(k1_ref, ub[c]) + uf[1] * halves(k2_ref, ub[c]) + uf[2] * halves(k3_ref, ub[c])
        new = (uf[c] + time_step * (viscosity * whole(kl_ref, ub[c]) - convect)).astype(bf16)
        out_ref[c] = new.reshape(8, 8, 8, width)
        new = new.astype(f32)
        speed = new * new if speed is None else speed + new * new
    c_ref[i, 0:512] = (1.0 + 0.5 * speed).astype(bf16)

    @pl.when(i == pl.num_programs(0) - 1)
    def _():
        elements = l2s_ref.shape[-1]
        cond = jnp.concatenate([c_ref[k, 0:512] for k in range(c_ref.shape[0])], 1)
        l2s = l2s_ref[...]
        if elements & (elements - 1) == 0:
            owner = lax.shift_right_logical(l2s, elements.bit_length() - 1)
            slot = l2s & (elements - 1)
        else:
            owner = l2s // elements
            slot = l2s - owner * elements
        ahead = owner - me_ref[0]
        ahead = jnp.where(ahead < 0, ahead + total, ahead)
        group = jnp.where(ahead == 1, 1, jnp.where(ahead == total - 1, 2, jnp.where(ahead == chan, 3, 0)))
        place = lax.broadcasted_iota(jnp.int32, (elements, elements), 0)
        keep = ((place == slot) & (group == 0)).astype(f32).astype(bf16)
        own_ref[...] = lax.dot_general(cond, keep, NT, preferred_element_type=f32).astype(bf16)
        kinds = lax.broadcasted_iota(jnp.int32, (16, elements), 0)
        marks = (kinds == group).astype(f32).astype(bf16)
        before = lax.broadcasted_iota(jnp.int32, (elements, elements), 0) < lax.broadcasted_iota(
            jnp.int32, (elements, elements), 1
        )
        rank = jnp.dot(marks, before.astype(f32).astype(bf16), preferred_element_type=f32).astype(jnp.int32)
        high = lax.shift_right_logical(slot, 5)
        codes = jnp.concatenate(
            [jnp.broadcast_to(high, (8, elements)), jnp.broadcast_to(slot - high * 32, (8, elements))], 0
        )
        tagged = jnp.concatenate([cond, codes.astype(f32).astype(bf16)], 0)
        room = s1_ref.shape[-1]
        position = lax.broadcasted_iota(jnp.int32, (room, elements), 0)
        for g, ref in ((1, s1_ref), (2, s2_ref), (3, s3_ref)):
            take = ((position == rank[g : g + 1]) & (group == g)).astype(f32).astype(bf16)
            ref[...] = lax.dot_general(tagged, take, NT, preferred_element_type=f32).astype(bf16)


def unpack_kernel(na, own_ref, r1_ref, r2_ref, r3_ref, dc_ref, wt_ref, wk_ref, behind_ref, ahead_ref):
    rows = weight_rows(wt_ref[...] * KRYLOV_SCALE)
    got = jnp.concatenate([r[0:512] for r in (r1_ref, r2_ref, r3_ref)], 1)
    tags = [r[512:528].astype(f32) for r in (r1_ref, r2_ref, r3_ref)]
    slots = [(t[0:1] * 32.0 + t[8:9]).astype(jnp.int32) for t in tags]
    slot = jnp.concatenate(slots, 1)
    for j in range(2 * na):
        place = lax.broadcasted_iota(jnp.int32, (LANES, slot.shape[1]), 0) + j * LANES
        put = (place == slot).astype(f32).astype(bf16)
        cols = slice(j * LANES, (j + 1) * LANES)
        moved = own_ref[:, cols].astype(f32) + lax.dot_general(got, put, NT, preferred_element_type=f32)
        kappa = (moved * dc_ref[0:1, cols]).reshape(8, 8, 8, LANES)
        for r in range(8):
            for s in range(8):
                wk_ref[j, r, s] = rows[r][s] * kappa[r, s]
    behind, ahead = send_rims(lambda j: wk_ref[j].reshape(512, LANES), na)
    behind_ref[...] = behind
    ahead_ref[...] = ahead


def lines_t(k_ref, x):
    x = x.reshape(2, 256, LANES)
    x = jnp.concatenate([x[0], x[1]], 1)
    high = x.astype(bf16)
    low = (x - high.astype(f32)).astype(bf16)
    y = jnp.dot(k_ref[...], jnp.concatenate([high, high, low], 0), preferred_element_type=f32)
    return y[:, :LANES].reshape(4, 8, 8, LANES), y[:, LANES:].reshape(4, 8, 8, LANES)


def squares(v, j, other, iw_ref):
    sums = {}
    for r in range(8):
        for s in range(8):
            key = (0 if r == 0 else 2 if r == 7 else 1, 0 if s == 0 else 2 if s == 7 else 1)
            x = v[j, r, s]
            pair = (x * x,) if other is None else (x * x, x * other[j, r, s])
            old = sums.get((key, r))
            sums[(key, r)] = pair if old is None else tuple(a + b for a, b in zip(old, pair))
    total = None
    for (key, _), pair in sums.items():
        weight = iw_ref[j, key[0] * 3 + key[1]]
        pair = tuple(weight * a for a in pair)
        total = pair if total is None else tuple(a + b for a, b in zip(total, pair))
    return total


def gradient_r(v, j, g):
    for s in range(8):
        for r, value in enumerate(along(DERIV, [v[j, r, s] for r in range(8)])):
            g[r, s] = value


def apply_tile(v, j, wk, jk, c, wt, kf_ref, kb_ref, y, g):
    gradient_r(v, j, g)
    base = weight_rows(wt * (coolant_throughput * KRYLOV_SCALE))
    for r in range(8):
        second = along(DERIV, [v[j, r, s] for s in range(8)])
        flux = []
        for s in range(8):
            first = g[r, s]
            k = wk[jk, r, s]
            flux.append(k * (second[s] + c * first))
            g[r, s] = k * (first + c * second[s])
        for s, value in enumerate(along(DERIV.T, flux)):
            y[j, r, s] = value + base[r][s] * v[j, r, s]
    for s in range(8):
        for r, value in enumerate(along(DERIV.T, [g[r, s] for r in range(8)])):
            y[j, r, s] = y[j, r, s] + value
    front, back = lines_t(kf_ref, v[j])
    third = jnp.concatenate([wk[jk, 0:4] * front, wk[jk, 4:8] * back], 0)
    front, back = lines_t(kb_ref, third)
    y[j, 0:4] = y[j, 0:4] + front
    y[j, 4:8] = y[j, 4:8] + back


def step_kernel(na, first, *refs):
    refs = list(refs)
    par_ref, y_in, a_in, b_in, wk_ref = refs[:5]
    del refs[:5]
    if first:
        from_ahead, from_behind = refs[:2]
        del refs[:2]
        prev = None
    else:
        wkg_ref, prev = refs[:2]
        del refs[:2]
    cr_ref, wt_ref, iw_ref, kf_ref, kb_ref, v, y, a_out, b_out, dots = refs[:10]
    del refs[:10]
    if first:
        wkg_ref = refs.pop(0)
    g, lo, hi = refs
    ghost = 2 * na
    parity = par_ref[0]
    if first:
        wkg_ref[0] = place_rims(from_ahead[...], from_behind[...]).reshape(8, 8, 8, LANES)
    v[...] = y_in[...]
    add_faces(na, parity, v, a_in, b_in)
    wt = wt_ref[...]
    dots[...] = jnp.zeros_like(dots)

    def own(j, carry):
        for k, value in enumerate(squares(v, j, prev, iw_ref)):
            dots[k] += value
        apply_tile(v, j, wk_ref, j, cr_ref[j], wt, kf_ref, kb_ref, y, g)
        return carry

    lax.fori_loop(0, ghost, own, 0)
    apply_tile(v, ghost, wkg_ref, 0, cr_ref[ghost], wt, kf_ref, kb_ref, y, g)
    assemble(na, y, lo, hi)
    faces_out(parity, lo, hi, a_out, b_out)


def last_kernel(na, par_ref, y_in, a_in, b_in, wk_ref, prev, cr_ref, wt_ref, iw_ref, kf_ref, d0, d1, d2, d3, v, all_dots, dots, g):
    ghost = 2 * na
    v[...] = y_in[...]
    add_faces(na, par_ref[0], v, a_in, b_in)
    wt = wt_ref[...]
    dots[...] = jnp.zeros_like(dots)

    def own(j, carry):
        for k, value in enumerate(squares(v, j, prev, iw_ref)):
            dots[k] += value
        gradient_r(v, j, g)
        c = 2.0 * cr_ref[j]
        base = weight_rows(wt * (coolant_throughput * KRYLOV_SCALE))
        front, back = lines_t(kf_ref, v[j])
        total = None
        for r in range(8):
            second = along(DERIV, [v[j, r, s] for s in range(8)])
            line = None
            for s in range(8):
                one, two = g[r, s], second[s]
                three = front[r, s] if r < 4 else back[r - 4, s]
                x = v[j, r, s]
                term = base[r][s] * x * x + wk_ref[j, r, s] * (one * (one + c * two) + two * two + three * three)
                line = term if line is None else line + term
            total = line if total is None else total + line
        dots[2] += total
        return carry

    lax.fori_loop(0, ghost, own, 0)
    lane = lane_index(1)
    rows = [d0[0], d1[1], d1[0], d2[1], d2[0], d3[1], d3[0], dots[1], dots[0], dots[2]]
    out = jnp.zeros((1, LANES), f32)
    for k, row in enumerate(rows):
        out = jnp.where(lane == k, jnp.sum(jnp.sum(row, 0, keepdims=True), 1, keepdims=True), out)
    all_dots[...] = jnp.broadcast_to(out[None], all_dots.shape)


def combine_kernel(na, m_ref, v0, v1, v2, v3, v4, out_ref):
    sums = jnp.sum(m_ref[:, 0, :], 0, keepdims=True)
    lane = lane_index(1)
    m = [jnp.sum(jnp.where(lane == k, sums, 0.0), 1, keepdims=True) for k in range(2 * ITERS)]
    n = ITERS
    low = [[None] * n for _ in range(n)]
    diag = [None] * n
    for j in range(n):
        acc = [m[i + j + 1] for i in range(n)]
        for k in range(j):
            scaled = low[j][k] * diag[k]
            for i in range(j, n):
                acc[i] = acc[i] - low[i][k] * scaled
        diag[j] = acc[j]
        for i in range(j + 1, n):
            low[i][j] = acc[i] / acc[j]
    z = []
    for i in range(n):
        value = m[i]
        for k in range(i):
            value = value - low[i][k] * z[k]
        z.append(value)
    c = [z[i] / diag[i] for i in range(n)]
    for i in reversed(range(n)):
        for k in range(i + 1, n):
            c[i] = c[i] - low[k][i] * c[k]
    c = [jnp.broadcast_to(x * KRYLOV_SCALE, (8, LANES)) for x in c]
    step = 2 * na
    vs = (v0, v1, v2, v3, v4)
    for r in range(8):
        for s in range(8):
            base = (r * 8 + s) * 8 * step
            for l in range(2):
                for at in range(na):
                    x = None
                    for coef, v in zip(c, vs):
                        term = coef * v[l * na + at, r, s]
                        x = term if x is None else x + term
                    out_ref[pl.ds(base + at * 2 + l, 8, stride=step), :] = x


def shift(x, axis, by):
    n = lax.axis_size(axis)
    return lax.ppermute(x, axis, [(i, i + by) for i in range(n) if 0 <= i + by < n])


def swap(x, axis, start):
    n = lax.axis_size(axis)
    pairs = [(i, i + 1) for i in range(start, n - 1, 2)]
    return lax.ppermute(x, axis, pairs + [(j, i) for i, j in pairs])


def around(x, by):
    n = lax.axis_size("slab") * lax.axis_size("chan")
    return lax.ppermute(x, ("slab", "chan"), [(i, (i + by) % n) for i in range(n)])


def product_weights(count_l, count_a):
    slab, chan = lax.axis_index("slab"), lax.axis_index("chan")
    axial = slab * count_a + jnp.arange(count_a)
    lateral = chan * count_l + jnp.arange(count_l)
    last_a = lax.axis_size("slab") * count_a - 1
    last_l = lax.axis_size("chan") * count_l - 1
    half = lambda cond: jnp.where(cond, 0.5, 1.0).astype(f32)
    along_a = jnp.stack([half(axial > 0), jnp.ones(count_a, f32), half(axial < last_a)])
    along_l = jnp.stack([half(lateral > 0), jnp.ones(count_l, f32), half(lateral < last_l)])
    weights = along_a[:, None, None, :] * along_l[None, :, :, None]
    weights = weights.reshape(9, -1, LANES).transpose(1, 0, 2)
    return jnp.broadcast_to(weights[:, :, None, :], weights.shape[:2] + (8, LANES))


def on_device(
    stream_speed_field,
    liquid_to_solid_element,
    previous_panel_warmth,
    pointwise_energy_source,
    coked_element_flags,
    coking_thickness_plies,
):
    count_l, count_a = coked_element_flags.shape
    assert count_l == 2 and count_a % LANES == 0
    elements = count_l * count_a
    na = count_a // LANES
    tiles = count_l * na
    chan = lax.axis_size("chan")
    total = lax.axis_size("slab") * chan
    me = (lax.axis_index("slab") * chan + lax.axis_index("chan")).astype(jnp.int32).reshape(1)
    parity = (lax.axis_index("chan") % 2).astype(jnp.int32).reshape(1)

    wt = jnp.asarray(np.broadcast_to(GLL_W[:, None], (8, LANES)), f32)
    kf, kb = (jnp.asarray(k) for k in line_matrices())
    k1, kl, k2, k3 = (jnp.asarray(k) for k in fluid_matrices())

    layers = coking_thickness_plies.astype(f32)
    flags = coked_element_flags.astype(f32)
    damping = jnp.where(coked_element_flags == 1, 1.0 / (1.0 + layer_damp * layers), jnp.ones_like(layers))
    cross = cross_gain * flags * layers / (layers + 1.0)
    dc = jnp.stack([damping.reshape(elements), cross.reshape(elements)])
    iw = product_weights(count_l, count_a)

    def as_rows(x):
        x = x.reshape(8, 8, 8, count_l, na, LANES).transpose(0, 1, 2, 4, 3, 5)
        return x.reshape(512 * tiles, LANES)

    field = (tiles, 8, 8, 8, LANES)
    whole = (tiles + 1, 8, 8, 8, LANES)
    face = (na + 1, 8, 8, LANES)
    shape = lambda s, d=f32: jax.ShapeDtypeStruct(s, d)
    z, behind, ahead = call(
        functools.partial(source_kernel, na),
        [shape(field), shape((2 * RIM, 640)), shape((2 * RIM, 640))],
        as_rows(previous_panel_warmth),
        as_rows(pointwise_energy_source),
        dc,
        wt,
    )
    from_ahead = shift(behind, "slab", -1)
    from_behind = shift(ahead, "slab", 1)

    split = 4
    width = elements // split
    room = elements // 4
    out = pl.pallas_call(
        functools.partial(fluid_kernel, chan, total),
        grid=(split,),
        in_specs=[
            pl.BlockSpec(memory_space=pltpu.SMEM),
            pl.BlockSpec((3, 8, 8, 8, width), lambda i: (0, 0, 0, 0, i)),
        ]
        + [pl.BlockSpec(memory_space=pltpu.VMEM)] * 5,
        out_specs=[pl.BlockSpec((3, 8, 8, 8, width), lambda i: (0, 0, 0, 0, i))]
        + [pl.BlockSpec(memory_space=pltpu.VMEM)] * 4,
        out_shape=[shape(stream_speed_field.shape, bf16), shape((512, elements), bf16)]
        + [shape((528, room), bf16)] * 3,
        scratch_shapes=[pltpu.VMEM((split, 512, width), bf16)],
        compiler_params=pltpu.CompilerParams(vmem_limit_bytes=48 * 1024 * 1024),
    )(me, stream_speed_field, liquid_to_solid_element.reshape(1, elements), k1, kl, k2, k3)
    stepped, own, *outgoing = out

    scratch_faces = [pltpu.VMEM(face, f32)] * 2
    y, cr, a, b = call(
        functools.partial(source_assembly_kernel, na),
        [shape(whole), shape((tiles + 1, 8, LANES)), shape(face), shape(face)],
        parity,
        z,
        from_ahead,
        from_behind,
        dc,
        smem=1,
        scratch=scratch_faces,
    )
    received = [around(x, by) for x, by in zip(outgoing, (1, -1, chan))]
    a, b = swap(a, "chan", 0), swap(b, "chan", 1)

    wk, behind, ahead = call(
        functools.partial(unpack_kernel, na),
        [shape(field), shape((2 * RIM, 512)), shape((2 * RIM, 512))],
        own,
        *received,
        dc,
        wt,
    )
    wk_ahead = shift(behind, "slab", -1)
    wk_behind = shift(ahead, "slab", 1)

    basis, products = [], []
    wkg = None
    for number in range(ITERS - 1):
        first = number == 0
        extra = (wk_ahead, wk_behind) if first else (wkg, basis[-1])
        outs = [shape(whole), shape(whole), shape(face), shape(face), shape((2, 8, LANES))]
        if first:
            outs.append(shape((1, 8, 8, 8, LANES)))
        got = call(
            functools.partial(step_kernel, na, first),
            outs,
            parity,
            y,
            a,
            b,
            wk,
            *extra,
            cr,
            wt,
            iw,
            kf,
            kb,
            smem=1,
            scratch=[pltpu.VMEM((8, 8, 8, LANES), f32)] + scratch_faces,
        )
        if first:
            wkg = got[5]
        v, y, a, b, dots = got[:5]
        basis.append(v)
        products.append(dots)
        a, b = swap(a, "chan", 0), swap(b, "chan", 1)
    v, sums = call(
        functools.partial(last_kernel, na),
        [shape(whole), shape((total, 1, LANES))],
        parity,
        y,
        a,
        b,
        wk,
        basis[-1],
        cr,
        wt,
        iw,
        kf,
        *products,
        smem=1,
        scratch=[pltpu.VMEM((3, 8, LANES), f32), pltpu.VMEM((8, 8, 8, LANES), f32)],
    )
    basis.append(v)
    sums = lax.all_to_all(sums, ("slab", "chan"), 0, 0)
    (x,) = call(functools.partial(combine_kernel, na), [shape((512 * tiles, LANES))], sums, *basis)
    x = x.reshape(8, 8, 8, na, count_l, LANES).transpose(0, 1, 2, 4, 3, 5)
    return stepped, x.reshape(8, 8, 8, count_l, count_a)


def solution(mesh):
    in_specs = (
        P(None, None, None, None, ("slab", "chan")),
        P(("slab", "chan")),
        P(None, None, None, "chan", "slab"),
        P(None, None, None, "chan", "slab"),
        P("chan", "slab"),
        P("chan", "slab"),
    )
    out_specs = (P(None, None, None, None, ("slab", "chan")), P(None, None, None, "chan", "slab"))
    return jax.shard_map(
        on_device, mesh=mesh, in_specs=in_specs, out_specs=out_specs, check_vma=False
    )
```

```python
import functools

import jax
import jax.numpy as jnp
import numpy as np
from jax import lax
from jax.experimental import pallas as pl
from jax.experimental.pallas import tpu as pltpu
from jax.sharding import PartitionSpec as P

ITERS = 5
LANES = 128
RIM = 8
KRYLOV_SCALE = 1.0 / 256.0

highest = lax.Precision.HIGHEST
f32 = jnp.float32
bf16 = jnp.bfloat16
coolant_throughput = 0.05
time_step = 0.01
viscosity = 0.02
cross_gain = 0.4
layer_damp = 0.25

NT = (((1,), (1,)), ((), ()))
TN = (((0,), (0,)), ((), ()))


def gll_tables():
    points = np.array(
        [
            -1.0,
            -0.8717401485096066,
            -0.5917001814331423,
            -0.2092992179024789,
            0.2092992179024789,
            0.5917001814331423,
            0.8717401485096066,
            1.0,
        ]
    )
    weights = np.array(
        [
            1.0 / 28.0,
            0.2107042271435061,
            0.3411226924835044,
            0.4124587946587038,
            0.4124587946587038,
            0.3411226924835044,
            0.2107042271435061,
            1.0 / 28.0,
        ]
    )
    lower_poly = np.ones(8)
    upper_poly = points.copy()
    for degree in range(1, 7):
        next_poly = ((2 * degree + 1) * points * upper_poly - degree * lower_poly) / (degree + 1)
        lower_poly = upper_poly
        upper_poly = next_poly
    gaps_matrix = points[:, None] - points[None, :] + np.eye(8)
    derivative = upper_poly[:, None] / (upper_poly[None, :] * gaps_matrix)
    derivative = derivative * (1.0 - np.eye(8))
    derivative[0, 0] = -14.0
    derivative[7, 7] = 14.0
    return derivative, weights


DERIV, GLL_W = gll_tables()
DERIV = DERIV.astype(np.float32).astype(np.float64)
GLL_W = GLL_W.astype(np.float32).astype(np.float64)


def split_hi_lo(matrix):
    high = np.asarray(matrix, np.float32).astype(jnp.bfloat16)
    low = (np.asarray(matrix, np.float64) - high.astype(np.float64)).astype(np.float32)
    return high, low.astype(jnp.bfloat16)


def line_matrices():
    out = []
    for matrix in (DERIV, DERIV.T):
        high, low = split_hi_lo(np.kron(np.eye(16), matrix))
        upper = np.concatenate([high, high], 1)
        out.append(np.concatenate([upper, np.concatenate([low, np.zeros_like(low)], 1)], 0))
    return out


def fluid_matrix():
    eye8 = np.eye(8)
    square = DERIV @ DERIV
    second = np.kron(DERIV, eye8)
    third = np.kron(eye8, DERIV)
    curve = np.kron(square, eye8) + np.kron(eye8, square)
    return np.concatenate([np.concatenate(split_hi_lo(np.kron(np.eye(2), m)), 1) for m in (second, third, curve)], 0)


def halves_of(line):
    return [line[j] + line[7 - j] for j in range(4)], [line[j] - line[7 - j] for j in range(4)]


def combined(matrix, parts, sign):
    even, odd = parts
    result = [None] * 8
    for i in range(4):
        p = sum(float(0.5 * (matrix[i, j] + matrix[i, 7 - j])) * even[j] for j in range(4))
        q = sum(float(0.5 * (matrix[i, j] - matrix[i, 7 - j])) * odd[j] for j in range(4))
        result[i] = p + q
        result[7 - i] = q - p if sign < 0 else p - q
    return result


def along(matrix, line):
    return combined(matrix, halves_of(line), -1)


def lane_index(rows=8):
    return lax.broadcasted_iota(jnp.int32, (rows, LANES), 1)


def vmem(shape, dtype=f32):
    return pltpu.VMEM(shape, dtype)


def call(kernel, out_shape, *args, smem=0, scratch=(), limit=48, **kw):
    specs = [pl.BlockSpec(memory_space=pltpu.SMEM)] * smem
    specs += [pl.BlockSpec(memory_space=pltpu.VMEM)] * (len(args) - smem)
    outs = [pl.BlockSpec(memory_space=pltpu.VMEM) for _ in out_shape]
    return pl.pallas_call(
        kernel,
        in_specs=specs,
        out_specs=outs,
        out_shape=out_shape,
        scratch_shapes=scratch,
        compiler_params=pltpu.CompilerParams(vmem_limit_bytes=limit * 1024 * 1024),
        **kw,
    )(*args)


def weight_rows(wt):
    return [[float(GLL_W[r] * GLL_W[s]) * wt for s in range(8)] for r in range(8)]


def sel_matrix(l, first_lane):
    row = lax.broadcasted_iota(jnp.int32, (2 * RIM, LANES), 0)
    lane = lax.broadcasted_iota(jnp.int32, (2 * RIM, LANES), 1)
    return ((row - l * RIM + first_lane == lane) & (row >= l * RIM) & (row < (l + 1) * RIM)).astype(f32)


def place_matrix(first_lane):
    row = lax.broadcasted_iota(jnp.int32, (2 * RIM, LANES), 0)
    lane = lax.broadcasted_iota(jnp.int32, (2 * RIM, LANES), 1)
    target = jnp.where(row < RIM, row + first_lane, row - RIM + first_lane + LANES // 2)
    return (target == lane).astype(f32)


def send_rims(tile_rows, na):
    behind = sum(
        lax.dot_general(sel_matrix(l, 0), tile_rows(l * na), NT, precision=highest, preferred_element_type=f32)
        for l in range(2)
    )
    ahead = sum(
        lax.dot_general(
            sel_matrix(l, LANES - RIM), tile_rows(l * na + na - 1), NT, precision=highest, preferred_element_type=f32
        )
        for l in range(2)
    )
    return behind, ahead


def place_rims(from_ahead, from_behind):
    a = lax.dot_general(from_ahead, place_matrix(0), TN, precision=highest, preferred_element_type=f32)
    b = lax.dot_general(
        from_behind, place_matrix(LANES // 2 - RIM), TN, precision=highest, preferred_element_type=f32
    )
    return a + b


def source_kernel(na, par_ref, p_ref, q_ref, wt_ref, z_ref, a_ref, b_ref):
    rows = weight_rows(wt_ref[...])
    step = 2 * na
    for r in range(8):
        for s in range(8):
            base = (r * 8 + s) * 8 * step
            for l in range(2):
                for at in range(na):
                    pick = pl.ds(base + at * 2 + l, 8, stride=step)
                    z_ref[l * na + at, r, s] = rows[r][s] * (coolant_throughput * p_ref[pick, :] + q_ref[pick, :])
    for r in range(8):
        for at in range(na):
            shared = z_ref[at, r, 7] + z_ref[na + at, r, 0]
            z_ref[at, r, 7] = shared
            z_ref[na + at, r, 0] = shared
            send_faces(par_ref, (at, r), z_ref[at, r, 0], z_ref[na + at, r, 7], a_ref, b_ref)


def rim_kernel(na, par_ref, z_in, a_ref, b_ref, dc_ref, z_ref, behind_ref, ahead_ref):
    z_ref[...] = z_in[...]
    for r in range(8):
        for at in range(na):
            lower, upper = got_faces(par_ref, (at, r), a_ref, b_ref)
            z_ref[at, r, 0] = z_ref[at, r, 0] + lower
            z_ref[na + at, r, 7] = z_ref[na + at, r, 7] + upper

    def tile_rows(j):
        cross = jnp.broadcast_to(dc_ref[1:2, j * LANES : (j + 1) * LANES], (LANES, LANES))
        return jnp.concatenate([z_ref[j].reshape(512, LANES), cross], 0)

    behind_ref[...], ahead_ref[...] = send_rims(tile_rows, na)


def send_faces(par_ref, at, lower, upper, a_ref, b_ref):
    even = par_ref[0] == 0
    lower = jnp.where(par_ref[1] > 0, lower, 0.0)
    upper = jnp.where(par_ref[2] > 0, upper, 0.0)
    a_ref[at] = jnp.where(even, upper, lower)
    b_ref[at] = jnp.where(even, lower, upper)


def got_faces(par_ref, at, a_ref, b_ref):
    even = par_ref[0] == 0
    a, b = a_ref[at], b_ref[at]
    return jnp.where(even, b, a), jnp.where(even, a, b)


def assemble_axial(na, y):
    ghost = 2 * na
    lane = lane_index()
    first = lane == 0
    last = lane == LANES - 1
    half = LANES // 2
    roll = pltpu.roll
    for s in range(8):
        far = [y[j, 7, s] for j in range(ghost + 1)]
        near = [y[j, 0, s] for j in range(ghost + 1)]
        right = [roll(f, 1, 1) for f in far]
        left = [roll(f, LANES - 1, 1) for f in near]
        far_half = [roll(far[na * 2 - 1], half + 1, 1), roll(far[ghost], half + 1, 1)]
        near_half = [roll(near[0], half - 1, 1), roll(near[ghost], half - 1, 1)]
        for l in range(2):
            for at in range(na):
                j = l * na + at
                if at > 0:
                    carry = right[j - 1]
                else:
                    carry = far_half[1] if l == 0 else right[ghost]
                y[j, 0, s] = near[j] + jnp.where(first, carry, right[j])
                if at < na - 1:
                    carry = left[j + 1]
                else:
                    carry = left[ghost] if l == 0 else near_half[1]
                y[j, 7, s] = far[j] + jnp.where(last, carry, left[j])
        from_left = jnp.where(first, right[na - 1], jnp.where(lane == half, far_half[0], right[ghost]))
        y[ghost, 0, s] = near[ghost] + from_left
        from_right = jnp.where(last, left[na], jnp.where(lane == half - 1, near_half[0], left[ghost]))
        y[ghost, 7, s] = far[ghost] + from_right


def assemble_lateral(na, par_ref, y, a_ref, b_ref):
    ghost = 2 * na
    half = LANES // 2
    low = lane_index() < half
    for r in range(8):
        for at in range(na):
            shared = y[at, r, 7] + y[na + at, r, 0]
            y[at, r, 7] = shared
            y[na + at, r, 0] = shared
            send_faces(par_ref, (at, r), y[at, r, 0], y[na + at, r, 7], a_ref, b_ref)
        upper = y[ghost, r, 7]
        lower = y[ghost, r, 0]
        new_upper = upper + jnp.where(low, pltpu.roll(lower, half, 1), 0.0)
        new_lower = lower + jnp.where(low, 0.0, pltpu.roll(upper, half, 1))
        y[ghost, r, 7] = new_upper
        y[ghost, r, 0] = new_lower
        to_lower = jnp.where(low, new_lower, 0.0)
        to_upper = jnp.where(low, pltpu.roll(new_upper, half, 1), 0.0)
        send_faces(par_ref, (na, r), to_lower, to_upper, a_ref, b_ref)


def add_faces(na, par_ref, v, a_ref, b_ref):
    ghost = 2 * na
    for r in range(8):
        for at in range(na + 1):
            lower, upper = got_faces(par_ref, (at, r), a_ref, b_ref)
            if at < na:
                v[at, r, 0] = v[at, r, 0] + lower
                v[na + at, r, 7] = v[na + at, r, 7] + upper
            else:
                v[ghost, r, 0] = v[ghost, r, 0] + lower
                v[ghost, r, 7] = v[ghost, r, 7] + pltpu.roll(upper, LANES // 2, 1)


def fluid_kernel(
    chan, total, me_ref, u_ref, l2s_ref, k_ref, out_ref, own_ref, s1_ref, s2_ref, s3_ref, c_ref, t_ref
):
    i = pl.program_id(0)
    k = k_ref[...]
    square = DERIV @ DERIV
    for c in range(3):
        for s in range(8):
            parts = halves_of([u_ref[c, r, s].astype(f32) for r in range(8)])
            slope = combined(DERIV, parts, -1)
            curve = combined(square, parts, 1)
            for r in range(8):
                t_ref[c, r, s] = viscosity * curve[r] - u_ref[0, r, s].astype(f32) * slope[r]
    for p in range(2):
        speed = [None] * 4
        for c in range(3):
            x = u_ref[c, 4 * p : 4 * p + 4].astype(f32).reshape(2, 128, LANES)
            x = jnp.concatenate([x[0], x[1]], 1).astype(bf16)
            y = jnp.dot(k, jnp.concatenate([x, x], 0), preferred_element_type=f32)
            for h in range(2):
                part = y[:, h * LANES : (h + 1) * LANES].reshape(3, 2, 8, 8, LANES)
                for q in range(2):
                    r = 4 * p + 2 * h + q
                    second, third, curve = part[0, q], part[1, q], part[2, q]
                    u2, u3 = u_ref[1, r].astype(f32), u_ref[2, r].astype(f32)
                    rate = t_ref[c, r] + viscosity * curve - u2 * second - u3 * third
                    new = (u_ref[c, r].astype(f32) + time_step * rate).astype(bf16)
                    out_ref[c, r] = new
                    new = new.astype(f32)
                    old = speed[2 * h + q]
                    speed[2 * h + q] = new * new if old is None else old + new * new
        for n, value in enumerate(speed):
            r = 4 * p + n
            c_ref[i, r * 64 : (r + 1) * 64] = (1.0 + 0.5 * value).astype(bf16).reshape(64, LANES)

    @pl.when(i == pl.num_programs(0) - 1)
    def _():
        elements = l2s_ref.shape[-1]
        cond = jnp.concatenate([c_ref[n] for n in range(c_ref.shape[0])], 1)
        l2s = l2s_ref[...]
        if elements & (elements - 1) == 0:
            owner = lax.shift_right_logical(l2s, elements.bit_length() - 1)
            slot = l2s & (elements - 1)
        else:
            owner = l2s // elements
            slot = l2s - owner * elements
        ahead = owner - me_ref[0]
        ahead = jnp.where(ahead < 0, ahead + total, ahead)
        group = jnp.where(ahead == 1, 1, jnp.where(ahead == total - 1, 2, jnp.where(ahead == chan, 3, 0)))
        place = lax.broadcasted_iota(jnp.int32, (elements, elements), 0)
        keep = ((place == slot) & (group == 0)).astype(f32).astype(bf16)
        own_ref[...] = lax.dot_general(cond, keep, NT, preferred_element_type=f32).astype(bf16)
        kinds = lax.broadcasted_iota(jnp.int32, (16, elements), 0)
        marks = (kinds == group).astype(f32).astype(bf16)
        before = lax.broadcasted_iota(jnp.int32, (elements, elements), 0) < lax.broadcasted_iota(
            jnp.int32, (elements, elements), 1
        )
        rank = jnp.dot(marks, before.astype(f32).astype(bf16), preferred_element_type=f32).astype(jnp.int32)
        high = lax.shift_right_logical(slot, 5)
        codes = jnp.concatenate(
            [jnp.broadcast_to(high, (8, elements)), jnp.broadcast_to(slot - high * 32, (8, elements))], 0
        )
        tagged = jnp.concatenate([cond, codes.astype(f32).astype(bf16)], 0)
        room = s1_ref.shape[-1]
        position = lax.broadcasted_iota(jnp.int32, (room, elements), 0)
        for g, ref in ((1, s1_ref), (2, s2_ref), (3, s3_ref)):
            take = ((position == rank[g : g + 1]) & (group == g)).astype(f32).astype(bf16)
            ref[...] = lax.dot_general(tagged, take, NT, preferred_element_type=f32).astype(bf16)


def unpack_kernel(
    na, par_ref, own_ref, r1_ref, r2_ref, r3_ref, dc_ref, wt_ref, zb_ref, za_ref, wk_ref, behind_ref, ahead_ref
):
    rows = weight_rows(wt_ref[...] * KRYLOV_SCALE)
    got = jnp.concatenate([r[0:512] for r in (r1_ref, r2_ref, r3_ref)], 1)
    tags = [r[512:528].astype(f32) for r in (r1_ref, r2_ref, r3_ref)]
    slots = [(t[0:1] * 32.0 + t[8:9]).astype(jnp.int32) for t in tags]
    slot = jnp.concatenate(slots, 1)
    for j in range(2 * na):
        place = lax.broadcasted_iota(jnp.int32, (LANES, slot.shape[1]), 0) + j * LANES
        put = (place == slot).astype(f32).astype(bf16)
        cols = slice(j * LANES, (j + 1) * LANES)
        moved = own_ref[:, cols].astype(f32) + lax.dot_general(got, put, NT, preferred_element_type=f32)
        kappa = (moved * dc_ref[0:1, cols]).reshape(8, 8, 8, LANES)
        for r in range(8):
            for s in range(8):
                wk_ref[j, r, s] = rows[r][s] * kappa[r, s]
    behind, ahead = send_rims(lambda j: wk_ref[j].reshape(512, LANES), na)
    for ref, z_rim, rim, inside in ((behind_ref, zb_ref, behind, par_ref[3]), (ahead_ref, za_ref, ahead, par_ref[4])):
        ref[:, 0:640] = jnp.where(inside > 0, z_rim[...], 0.0)
        ref[:, 640:1152] = jnp.where(inside > 0, rim, 0.0)


def lines_t(k_ref, x):
    x = x.reshape(4, 128, LANES)
    out = []
    for p in range(2):
        pair = jnp.concatenate([x[2 * p], x[2 * p + 1]], 1)
        high = pair.astype(bf16)
        low = (pair - high.astype(f32)).astype(bf16)
        y = jnp.dot(k_ref[...], jnp.concatenate([high, low], 0), preferred_element_type=f32)
        y = y[:128] + y[128:]
        out += [y[:, :LANES].reshape(2, 8, 8, LANES), y[:, LANES:].reshape(2, 8, 8, LANES)]
    return out


def squares(v, j, other, iw_ref):
    sums = {}
    for r in range(8):
        for s in range(8):
            key = (0 if r == 0 else 2 if r == 7 else 1, 0 if s == 0 else 2 if s == 7 else 1)
            x = v[j, r, s]
            pair = (x * x,) if other is None else (x * x, x * other[j, r, s])
            old = sums.get((key, r))
            sums[(key, r)] = pair if old is None else tuple(a + b for a, b in zip(old, pair))
    total = None
    for (key, _), pair in sums.items():
        weight = iw_ref[j, key[0] * 3 + key[1]]
        pair = tuple(weight * a for a in pair)
        total = pair if total is None else tuple(a + b for a, b in zip(total, pair))
    return total


def gradient_r(v, j, g):
    for s in range(8):
        for r, value in enumerate(along(DERIV, [v[j, r, s] for r in range(8)])):
            g[r, s] = value


def apply_tile(v, j, wk, c, base, kf_ref, kb_ref, y, g, f):
    for p, part in enumerate(lines_t(kf_ref, v[j])):
        for q in range(2):
            f[2 * p + q] = wk(2 * p + q) * part[q]
    gradient_r(v, j, g)
    for r in range(8):
        line = [v[j, r, s] for s in range(8)]
        second = along(DERIV, line)
        k = wk(r)
        flux = []
        for s in range(8):
            first = g[r, s]
            flux.append(k[s] * (second[s] + c * first))
            g[r, s] = k[s] * (first + c * second[s])
        for s, value in enumerate(along(DERIV.T, flux)):
            y[j, r, s] = value + (base[r] * float(GLL_W[s])) * line[s]
    parts = lines_t(kb_ref, f[...])
    for s in range(8):
        for r, value in enumerate(along(DERIV.T, [g[r, s] for r in range(8)])):
            y[j, r, s] = y[j, r, s] + value
    for p, part in enumerate(parts):
        y[j, 2 * p : 2 * p + 2] = y[j, 2 * p : 2 * p + 2] + part


def mass_rows(wt, base):
    for r in range(8):
        base[r] = wt * float(GLL_W[r] * coolant_throughput * KRYLOV_SCALE)


def step_kernel(na, first, *refs):
    refs = list(refs)
    take = lambda n: [refs.pop(0) for _ in range(n)]
    ghost = 2 * na
    if first:
        par_ref, z_in, wk_ref, from_ahead, from_behind, dc_ref = take(6)
        prev = None
    else:
        par_ref, y_in, a_in, b_in, wk_ref, wkg_ref, cr_ref, prev = take(8)
    wt_ref, iw_ref, kf_ref, kb_ref, v, y, a_out, b_out, dots = take(9)
    if first:
        wkg_ref, cr_ref = take(2)
    g, f, base = refs
    if first:
        v[0:ghost] = z_in[...]
        rims = place_rims(from_ahead[...], from_behind[...])
        v[ghost] = rims[0:512].reshape(8, 8, 8, LANES)
        wkg_ref[...] = rims[640:1152].reshape(8, 8, 8, LANES)
        for j in range(ghost):
            cr_ref[j] = jnp.broadcast_to(dc_ref[1:2, j * LANES : (j + 1) * LANES], (8, LANES))
        cr_ref[ghost] = rims[512:520]
        assemble_axial(na, v)
    else:
        v[...] = y_in[...]
        add_faces(na, par_ref, v, a_in, b_in)
    mass_rows(wt_ref[...], base)
    totals = None
    for j in range(ghost + 1):
        if j < ghost:
            sums = squares(v, j, prev, iw_ref)
            totals = sums if totals is None else [a + b for a, b in zip(totals, sums)]
            wk = lambda r: wk_ref[j, r]
        else:
            wk = lambda r: wkg_ref[r]
        apply_tile(v, j, wk, cr_ref[j], base, kf_ref, kb_ref, y, g.at[j % 2], f.at[j % 2])
    for k, value in enumerate(totals):
        dots[k] = value
    assemble_axial(na, y)
    assemble_lateral(na, par_ref, y, a_out, b_out)


def last_kernel(na, par_ref, y_in, a_in, b_in, wk_ref, cr_ref, prev, wt_ref, iw_ref, kf_ref, d0, d1, d2, d3, v, all_dots, g, base):
    ghost = 2 * na
    v[...] = y_in[...]
    add_faces(na, par_ref, v, a_in, b_in)
    mass_rows(wt_ref[...], base)
    totals = None
    for j in range(ghost):
        gj = g.at[j % 2]
        third = lines_t(kf_ref, v[j])
        sums = list(squares(v, j, prev, iw_ref))
        gradient_r(v, j, gj)
        c = 2.0 * cr_ref[j]
        total = None
        for r in range(8):
            line = [v[j, r, s] for s in range(8)]
            second = along(DERIV, line)
            row = None
            for s in range(8):
                one, two, three = gj[r, s], second[s], third[r // 2][r % 2, s]
                term = (base[r] * float(GLL_W[s])) * (line[s] * line[s])
                term = term + wk_ref[j, r, s] * (one * (one + c * two) + two * two + three * three)
                row = term if row is None else row + term
            total = row if total is None else total + row
        sums.append(total)
        totals = sums if totals is None else [a + b for a, b in zip(totals, sums)]
    lane = lane_index(1)
    rows = [d0[0], d1[1], d1[0], d2[1], d2[0], d3[1], d3[0], totals[1], totals[0], totals[2]]
    out = jnp.zeros((1, LANES), f32)
    for k, row in enumerate(rows):
        out = jnp.where(lane == k, jnp.sum(jnp.sum(row, 0, keepdims=True), 1, keepdims=True), out)
    all_dots[...] = jnp.broadcast_to(out[None], all_dots.shape)


def combine_kernel(na, m_ref, v0, v1, v2, v3, v4, out_ref):
    sums = jnp.sum(m_ref[:, 0, :], 0, keepdims=True)
    lane = lane_index(1)
    m = [jnp.sum(jnp.where(lane == k, sums, 0.0), 1, keepdims=True) for k in range(2 * ITERS)]
    n = ITERS
    low = [[None] * n for _ in range(n)]
    diag = [None] * n
    for j in range(n):
        acc = [m[i + j + 1] for i in range(n)]
        for k in range(j):
            scaled = low[j][k] * diag[k]
            for i in range(j, n):
                acc[i] = acc[i] - low[i][k] * scaled
        diag[j] = acc[j]
        for i in range(j + 1, n):
            low[i][j] = acc[i] / acc[j]
    z = []
    for i in range(n):
        value = m[i]
        for k in range(i):
            value = value - low[i][k] * z[k]
        z.append(value)
    c = [z[i] / diag[i] for i in range(n)]
    for i in reversed(range(n)):
        for k in range(i + 1, n):
            c[i] = c[i] - low[k][i] * c[k]
    c = [jnp.broadcast_to(x * KRYLOV_SCALE, (8, LANES)) for x in c]
    step = 2 * na
    vs = (v0, v1, v2, v3, v4)
    for r in range(8):
        for s in range(8):
            base = (r * 8 + s) * 8 * step
            for l in range(2):
                for at in range(na):
                    x = None
                    for coef, v in zip(c, vs):
                        term = coef * v[l * na + at, r, s]
                        x = term if x is None else x + term
                    out_ref[pl.ds(base + at * 2 + l, 8, stride=step), :] = x


def ring(x, axis, by):
    n = lax.axis_size(axis)
    return lax.ppermute(x, axis, [(i, (i + by) % n) for i in range(n)])


def swap(x, axis, start):
    n = lax.axis_size(axis)
    pairs = [((start + i) % n, (start + i + 1) % n) for i in range(0, n, 2)]
    return lax.ppermute(x, axis, pairs + [(j, i) for i, j in pairs])


def around(x, by):
    n = lax.axis_size("slab") * lax.axis_size("chan")
    return lax.ppermute(x, ("slab", "chan"), [(i, (i + by) % n) for i in range(n)])


def product_weights(count_l, count_a):
    slab, chan = lax.axis_index("slab"), lax.axis_index("chan")
    axial = slab * count_a + jnp.arange(count_a)
    lateral = chan * count_l + jnp.arange(count_l)
    last_a = lax.axis_size("slab") * count_a - 1
    last_l = lax.axis_size("chan") * count_l - 1
    half = lambda cond: jnp.where(cond, 0.5, 1.0).astype(f32)
    along_a = jnp.stack([half(axial > 0), jnp.ones(count_a, f32), half(axial < last_a)])
    along_l = jnp.stack([half(lateral > 0), jnp.ones(count_l, f32), half(lateral < last_l)])
    weights = along_a[:, None, None, :] * along_l[None, :, :, None]
    weights = weights.reshape(9, -1, LANES).transpose(1, 0, 2)
    return jnp.broadcast_to(weights[:, :, None, :], weights.shape[:2] + (8, LANES))


def on_device(
    stream_speed_field,
    liquid_to_solid_element,
    previous_panel_warmth,
    pointwise_energy_source,
    coked_element_flags,
    coking_thickness_plies,
):
    count_l, count_a = coked_element_flags.shape
    assert count_l == 2 and count_a % LANES == 0
    elements = count_l * count_a
    na = count_a // LANES
    tiles = count_l * na
    chan = lax.axis_size("chan")
    total = lax.axis_size("slab") * chan
    slab_at, chan_at = lax.axis_index("slab"), lax.axis_index("chan")
    me = (slab_at * chan + chan_at).astype(jnp.int32).reshape(1)
    position = [
        chan_at % 2,
        chan_at > 0,
        chan_at < chan - 1,
        slab_at > 0,
        slab_at < lax.axis_size("slab") - 1,
    ]
    position = jnp.stack([jnp.asarray(x, jnp.int32) for x in position])

    wt = jnp.asarray(np.broadcast_to(GLL_W[:, None], (8, LANES)), f32)
    kf, kb = (jnp.asarray(k) for k in line_matrices())
    kfluid = jnp.asarray(fluid_matrix())

    layers = coking_thickness_plies.astype(f32)
    flags = coked_element_flags.astype(f32)
    damping = jnp.where(coked_element_flags == 1, 1.0 / (1.0 + layer_damp * layers), jnp.ones_like(layers))
    cross = cross_gain * flags * layers / (layers + 1.0)
    dc = jnp.stack([damping.reshape(elements), cross.reshape(elements)])
    iw = product_weights(count_l, count_a)

    def as_rows(x):
        x = x.reshape(8, 8, 8, count_l, na, LANES).transpose(0, 1, 2, 4, 3, 5)
        return x.reshape(512 * tiles, LANES)

    field = (tiles, 8, 8, 8, LANES)
    whole = (tiles + 1, 8, 8, 8, LANES)
    face = (na + 1, 8, 8, LANES)
    shape = lambda s, d=f32: jax.ShapeDtypeStruct(s, d)
    kept = vmem
    split = elements // LANES
    width = LANES
    room = elements // 4
    out = pl.pallas_call(
        functools.partial(fluid_kernel, chan, total),
        grid=(split,),
        in_specs=[
            pl.BlockSpec(memory_space=pltpu.SMEM),
            pl.BlockSpec((3, 8, 8, 8, width), lambda i: (0, 0, 0, 0, i)),
        ]
        + [pl.BlockSpec(memory_space=pltpu.VMEM)] * 2,
        out_specs=[pl.BlockSpec((3, 8, 8, 8, width), lambda i: (0, 0, 0, 0, i))]
        + [pl.BlockSpec(memory_space=pltpu.VMEM)] * 4,
        out_shape=[shape(stream_speed_field.shape, bf16), shape((512, elements), bf16)]
        + [shape((528, room), bf16)] * 3,
        scratch_shapes=[pltpu.VMEM((split, 512, width), bf16), pltpu.VMEM((3, 8, 8, 8, width), f32)],
        compiler_params=pltpu.CompilerParams(vmem_limit_bytes=48 * 1024 * 1024),
    )(me, stream_speed_field, liquid_to_solid_element.reshape(1, elements), kfluid)
    stepped, own, *outgoing = out
    received = [around(x, by) for x, by in zip(outgoing, (1, -1, chan))]

    warmth, source, own = lax.optimization_barrier((previous_panel_warmth, pointwise_energy_source, own))
    z, a, b = call(
        functools.partial(source_kernel, na),
        [kept(field), shape((na, 8, 8, LANES)), shape((na, 8, 8, LANES))],
        position,
        as_rows(warmth),
        as_rows(source),
        wt,
        smem=1,
    )
    a, b = swap(a, "chan", 0), swap(b, "chan", 1)
    z, z_behind, z_ahead = call(
        functools.partial(rim_kernel, na),
        [kept(field), kept((2 * RIM, 640)), kept((2 * RIM, 640))],
        position,
        z,
        a,
        b,
        dc,
        smem=1,
    )
    wk, behind, ahead = call(
        functools.partial(unpack_kernel, na),
        [kept(field), shape((2 * RIM, 1152)), shape((2 * RIM, 1152))],
        position,
        own,
        *received,
        dc,
        wt,
        z_behind,
        z_ahead,
        smem=1,
    )
    from_ahead = ring(behind, "slab", -1)
    from_behind = ring(ahead, "slab", 1)

    basis, products = [], []
    for number in range(ITERS - 1):
        first = number == 0
        outs = [kept(whole), kept(whole), shape(face), shape(face), kept((2, 8, LANES))]
        if first:
            args = (z, wk, from_ahead, from_behind, dc)
            outs += [kept((8, 8, 8, LANES)), kept((tiles + 1, 8, LANES))]
        else:
            args = (y, a, b, wk, wkg, cr, basis[-1])
        got = call(
            functools.partial(step_kernel, na, first),
            outs,
            position,
            *args,
            wt,
            iw,
            kf,
            kb,
            smem=1,
            scratch=[pltpu.VMEM((2, 8, 8, 8, LANES), f32)] * 2 + [pltpu.VMEM((8, 8, LANES), f32)],
        )
        if first:
            wkg, cr = got[5:]
        v, y, a, b, dots = got[:5]
        basis.append(v)
        products.append(dots)
        a, b = swap(a, "chan", 0), swap(b, "chan", 1)
    v, sums = call(
        functools.partial(last_kernel, na),
        [kept(whole), shape((total, 1, LANES))],
        position,
        y,
        a,
        b,
        wk,
        cr,
        basis[-1],
        wt,
        iw,
        kf,
        *products,
        smem=1,
        scratch=[pltpu.VMEM((2, 8, 8, 8, LANES), f32), pltpu.VMEM((8, 8, LANES), f32)],
    )
    basis.append(v)
    sums = lax.all_to_all(sums, ("slab", "chan"), 0, 0)
    (x,) = call(functools.partial(combine_kernel, na), [shape((512 * tiles, LANES))], sums, *basis)
    x = x.reshape(8, 8, 8, na, count_l, LANES).transpose(0, 1, 2, 4, 3, 5)
    return stepped, x.reshape(8, 8, 8, count_l, count_a)


def solution(mesh):
    in_specs = (
        P(None, None, None, None, ("slab", "chan")),
        P(("slab", "chan")),
        P(None, None, None, "chan", "slab"),
        P(None, None, None, "chan", "slab"),
        P("chan", "slab"),
        P("chan", "slab"),
    )
    out_specs = (P(None, None, None, None, ("slab", "chan")), P(None, None, None, "chan", "slab"))
    return jax.shard_map(
        on_device, mesh=mesh, in_specs=in_specs, out_specs=out_specs, check_vma=False
    )
```

```python
import functools

import jax
import jax.numpy as jnp
import numpy as np
from jax import lax
from jax.experimental import pallas as pl
from jax.experimental.pallas import tpu as pltpu
from jax.sharding import PartitionSpec as P

ITERS = 5
LANES = 128
RIM = 8
KRYLOV_SCALE = 1.0 / 256.0

highest = lax.Precision.HIGHEST
f32 = jnp.float32
bf16 = jnp.bfloat16
coolant_throughput = 0.05
time_step = 0.01
viscosity = 0.02
cross_gain = 0.4
layer_damp = 0.25

NT = (((1,), (1,)), ((), ()))
TN = (((0,), (0,)), ((), ()))


def gll_tables():
    points = np.array(
        [
            -1.0,
            -0.8717401485096066,
            -0.5917001814331423,
            -0.2092992179024789,
            0.2092992179024789,
            0.5917001814331423,
            0.8717401485096066,
            1.0,
        ]
    )
    weights = np.array(
        [
            1.0 / 28.0,
            0.2107042271435061,
            0.3411226924835044,
            0.4124587946587038,
            0.4124587946587038,
            0.3411226924835044,
            0.2107042271435061,
            1.0 / 28.0,
        ]
    )
    lower_poly = np.ones(8)
    upper_poly = points.copy()
    for degree in range(1, 7):
        next_poly = ((2 * degree + 1) * points * upper_poly - degree * lower_poly) / (degree + 1)
        lower_poly = upper_poly
        upper_poly = next_poly
    gaps_matrix = points[:, None] - points[None, :] + np.eye(8)
    derivative = upper_poly[:, None] / (upper_poly[None, :] * gaps_matrix)
    derivative = derivative * (1.0 - np.eye(8))
    derivative[0, 0] = -14.0
    derivative[7, 7] = 14.0
    return derivative, weights


DERIV, GLL_W = gll_tables()
DERIV = DERIV.astype(np.float32).astype(np.float64)
GLL_W = GLL_W.astype(np.float32).astype(np.float64)


def split_hi_lo(matrix):
    high = np.asarray(matrix, np.float32).astype(jnp.bfloat16)
    low = (np.asarray(matrix, np.float64) - high.astype(np.float64)).astype(np.float32)
    return high, low.astype(jnp.bfloat16)


def line_matrices():
    out = []
    for matrix in (DERIV, DERIV.T):
        high, low = split_hi_lo(np.kron(np.eye(16), matrix))
        upper = np.concatenate([high, high], 1)
        out.append(np.concatenate([upper, np.concatenate([low, np.zeros_like(low)], 1)], 0))
    return out


def fluid_matrix():
    eye8 = np.eye(8)
    square = DERIV @ DERIV
    second = np.kron(DERIV, eye8)
    third = np.kron(eye8, DERIV)
    curve = np.kron(square, eye8) + np.kron(eye8, square)
    return np.concatenate([np.concatenate(split_hi_lo(np.kron(np.eye(2), m)), 1) for m in (second, third, curve)], 0)


def halves_of(line):
    return [line[j] + line[7 - j] for j in range(4)], [line[j] - line[7 - j] for j in range(4)]


def combined(matrix, parts, sign):
    even, odd = parts
    result = [None] * 8
    for i in range(4):
        p = sum(float(0.5 * (matrix[i, j] + matrix[i, 7 - j])) * even[j] for j in range(4))
        q = sum(float(0.5 * (matrix[i, j] - matrix[i, 7 - j])) * odd[j] for j in range(4))
        result[i] = p + q
        result[7 - i] = q - p if sign < 0 else p - q
    return result


def along(matrix, line):
    return combined(matrix, halves_of(line), -1)


def lane_index(rows=8):
    return lax.broadcasted_iota(jnp.int32, (rows, LANES), 1)


def vmem(shape, dtype=f32):
    return pltpu.VMEM(shape, dtype)


def call(kernel, out_shape, *args, smem=0, scratch=(), limit=12, **kw):
    specs = [pl.BlockSpec(memory_space=pltpu.SMEM)] * smem
    specs += [pl.BlockSpec(memory_space=pltpu.VMEM)] * (len(args) - smem)
    outs = [pl.BlockSpec(memory_space=pltpu.VMEM) for _ in out_shape]
    return pl.pallas_call(
        kernel,
        in_specs=specs,
        out_specs=outs,
        out_shape=out_shape,
        scratch_shapes=scratch,
        compiler_params=pltpu.CompilerParams(vmem_limit_bytes=limit * 1024 * 1024),
        **kw,
    )(*args)


def weight_rows(wt):
    return [[float(GLL_W[r] * GLL_W[s]) * wt for s in range(8)] for r in range(8)]


def sel_matrix(l, first_lane):
    row = lax.broadcasted_iota(jnp.int32, (2 * RIM, LANES), 0)
    lane = lax.broadcasted_iota(jnp.int32, (2 * RIM, LANES), 1)
    return ((row - l * RIM + first_lane == lane) & (row >= l * RIM) & (row < (l + 1) * RIM)).astype(f32)


def place_matrix(first_lane):
    row = lax.broadcasted_iota(jnp.int32, (2 * RIM, LANES), 0)
    lane = lax.broadcasted_iota(jnp.int32, (2 * RIM, LANES), 1)
    target = jnp.where(row < RIM, row + first_lane, row - RIM + first_lane + LANES // 2)
    return (target == lane).astype(f32)


def send_rims(tile_rows, na):
    behind = sum(
        lax.dot_general(sel_matrix(l, 0), tile_rows(l * na), NT, precision=highest, preferred_element_type=f32)
        for l in range(2)
    )
    ahead = sum(
        lax.dot_general(
            sel_matrix(l, LANES - RIM), tile_rows(l * na + na - 1), NT, precision=highest, preferred_element_type=f32
        )
        for l in range(2)
    )
    return behind, ahead


def place_rims(from_ahead, from_behind):
    a = lax.dot_general(from_ahead, place_matrix(0), TN, precision=highest, preferred_element_type=f32)
    b = lax.dot_general(
        from_behind, place_matrix(LANES // 2 - RIM), TN, precision=highest, preferred_element_type=f32
    )
    return a + b


def source_kernel(na, planes, par_ref, p_ref, q_ref, wr_ref, z_ref, a_ref, b_ref):
    step = 2 * na
    for n in range(planes):
        r = pl.program_id(0) * planes + n
        wr = wr_ref[r]
        ends = {}
        for s in range(8):
            base = (n * 8 + s) * 8 * step
            for l in range(2):
                for at in range(na):
                    pick = pl.ds(base + at * 2 + l, 8, stride=step)
                    value = (wr * float(GLL_W[s])) * (coolant_throughput * p_ref[pick, :] + q_ref[pick, :])
                    if (l, s) in ((0, 0), (0, 7), (1, 0), (1, 7)):
                        ends[l, s, at] = value
                    else:
                        z_ref[l * na + at, r, s] = value
        for at in range(na):
            shared = ends[0, 7, at] + ends[1, 0, at]
            z_ref[at, r, 7] = shared
            z_ref[na + at, r, 0] = shared
            lower, upper = ends[0, 0, at], ends[1, 7, at]
            z_ref[at, r, 0] = lower
            z_ref[na + at, r, 7] = upper
            send_faces(par_ref, (at, r), lower, upper, a_ref, b_ref)


def rim_kernel(na, par_ref, z_in, a_ref, b_ref, dc_ref, z_ref, behind_ref, ahead_ref):
    z_ref[...] = z_in[...]
    for r in range(8):
        for at in range(na):
            lower, upper = got_faces(par_ref, (at, r), a_ref, b_ref)
            z_ref[at, r, 0] = z_ref[at, r, 0] + lower
            z_ref[na + at, r, 7] = z_ref[na + at, r, 7] + upper

    def tile_rows(j):
        cross = jnp.broadcast_to(dc_ref[1:2, j * LANES : (j + 1) * LANES], (LANES, LANES))
        return jnp.concatenate([z_ref[j].reshape(512, LANES), cross], 0)

    behind_ref[...], ahead_ref[...] = send_rims(tile_rows, na)


def send_faces(par_ref, at, lower, upper, a_ref, b_ref):
    even = par_ref[0] == 0
    lower = jnp.where(par_ref[1] > 0, lower, 0.0)
    upper = jnp.where(par_ref[2] > 0, upper, 0.0)
    a_ref[at] = jnp.where(even, upper, lower)
    b_ref[at] = jnp.where(even, lower, upper)


def got_faces(par_ref, at, a_ref, b_ref):
    even = par_ref[0] == 0
    a, b = a_ref[at], b_ref[at]
    return jnp.where(even, b, a), jnp.where(even, a, b)


def assemble_axial(na, y):
    ghost = 2 * na
    lane = lane_index()
    first = lane == 0
    last = lane == LANES - 1
    half = LANES // 2
    roll = pltpu.roll
    for s in range(8):
        far = [y[j, 7, s] for j in range(ghost + 1)]
        near = [y[j, 0, s] for j in range(ghost + 1)]
        right = [roll(f, 1, 1) for f in far]
        left = [roll(f, LANES - 1, 1) for f in near]
        far_half = [roll(far[na * 2 - 1], half + 1, 1), roll(far[ghost], half + 1, 1)]
        near_half = [roll(near[0], half - 1, 1), roll(near[ghost], half - 1, 1)]
        for l in range(2):
            for at in range(na):
                j = l * na + at
                if at > 0:
                    carry = right[j - 1]
                else:
                    carry = far_half[1] if l == 0 else right[ghost]
                y[j, 0, s] = near[j] + jnp.where(first, carry, right[j])
                if at < na - 1:
                    carry = left[j + 1]
                else:
                    carry = left[ghost] if l == 0 else near_half[1]
                y[j, 7, s] = far[j] + jnp.where(last, carry, left[j])
        from_left = jnp.where(first, right[na - 1], jnp.where(lane == half, far_half[0], right[ghost]))
        y[ghost, 0, s] = near[ghost] + from_left
        from_right = jnp.where(last, left[na], jnp.where(lane == half - 1, near_half[0], left[ghost]))
        y[ghost, 7, s] = far[ghost] + from_right


def assemble_lateral(na, par_ref, y, a_ref, b_ref):
    ghost = 2 * na
    half = LANES // 2
    low = lane_index() < half
    for r in range(8):
        for at in range(na):
            shared = y[at, r, 7] + y[na + at, r, 0]
            y[at, r, 7] = shared
            y[na + at, r, 0] = shared
            send_faces(par_ref, (at, r), y[at, r, 0], y[na + at, r, 7], a_ref, b_ref)
        upper = y[ghost, r, 7]
        lower = y[ghost, r, 0]
        new_upper = upper + jnp.where(low, pltpu.roll(lower, half, 1), 0.0)
        new_lower = lower + jnp.where(low, 0.0, pltpu.roll(upper, half, 1))
        y[ghost, r, 7] = new_upper
        y[ghost, r, 0] = new_lower
        to_lower = jnp.where(low, new_lower, 0.0)
        to_upper = jnp.where(low, pltpu.roll(new_upper, half, 1), 0.0)
        send_faces(par_ref, (na, r), to_lower, to_upper, a_ref, b_ref)


def add_faces(na, par_ref, v, a_ref, b_ref):
    ghost = 2 * na
    for r in range(8):
        for at in range(na + 1):
            lower, upper = got_faces(par_ref, (at, r), a_ref, b_ref)
            if at < na:
                v[at, r, 0] = v[at, r, 0] + lower
                v[na + at, r, 7] = v[na + at, r, 7] + upper
            else:
                v[ghost, r, 0] = v[ghost, r, 0] + lower
                v[ghost, r, 7] = v[ghost, r, 7] + pltpu.roll(upper, LANES // 2, 1)


def fluid_kernel(
    chan, total, me_ref, u_ref, l2s_ref, k_ref, out_ref, own_ref, s1_ref, s2_ref, s3_ref, c_ref, t_ref
):
    i = pl.program_id(0)
    k = k_ref[...]
    square = DERIV @ DERIV
    for c in range(3):
        for s in range(8):
            parts = halves_of([u_ref[c, r, s].astype(f32) for r in range(8)])
            slope = combined(DERIV, parts, -1)
            curve = combined(square, parts, 1)
            for r in range(8):
                t_ref[c, r, s] = viscosity * curve[r] - u_ref[0, r, s].astype(f32) * slope[r]
    for p in range(2):
        speed = [None] * 4
        for c in range(3):
            x = u_ref[c, 4 * p : 4 * p + 4].astype(f32).reshape(2, 128, LANES)
            x = jnp.concatenate([x[0], x[1]], 1).astype(bf16)
            y = jnp.dot(k, jnp.concatenate([x, x], 0), preferred_element_type=f32)
            for h in range(2):
                part = y[:, h * LANES : (h + 1) * LANES].reshape(3, 2, 8, 8, LANES)
                for q in range(2):
                    r = 4 * p + 2 * h + q
                    second, third, curve = part[0, q], part[1, q], part[2, q]
                    u2, u3 = u_ref[1, r].astype(f32), u_ref[2, r].astype(f32)
                    rate = t_ref[c, r] + viscosity * curve - u2 * second - u3 * third
                    new = (u_ref[c, r].astype(f32) + time_step * rate).astype(bf16)
                    out_ref[c, r] = new
                    new = new.astype(f32)
                    old = speed[2 * h + q]
                    speed[2 * h + q] = new * new if old is None else old + new * new
        for n, value in enumerate(speed):
            r = 4 * p + n
            c_ref[i, r * 64 : (r + 1) * 64] = (1.0 + 0.5 * value).astype(bf16).reshape(64, LANES)

    @pl.when(i == pl.num_programs(0) - 1)
    def _():
        elements = l2s_ref.shape[-1]
        cond = jnp.concatenate([c_ref[n] for n in range(c_ref.shape[0])], 1)
        l2s = l2s_ref[...]
        if elements & (elements - 1) == 0:
            owner = lax.shift_right_logical(l2s, elements.bit_length() - 1)
            slot = l2s & (elements - 1)
        else:
            owner = l2s // elements
            slot = l2s - owner * elements
        ahead = owner - me_ref[0]
        ahead = jnp.where(ahead < 0, ahead + total, ahead)
        group = jnp.where(ahead == 1, 1, jnp.where(ahead == total - 1, 2, jnp.where(ahead == chan, 3, 0)))
        place = lax.broadcasted_iota(jnp.int32, (elements, elements), 0)
        keep = ((place == slot) & (group == 0)).astype(f32).astype(bf16)
        own_ref[...] = lax.dot_general(cond, keep, NT, preferred_element_type=f32).astype(bf16)
        kinds = lax.broadcasted_iota(jnp.int32, (16, elements), 0)
        marks = (kinds == group).astype(f32).astype(bf16)
        before = lax.broadcasted_iota(jnp.int32, (elements, elements), 0) < lax.broadcasted_iota(
            jnp.int32, (elements, elements), 1
        )
        rank = jnp.dot(marks, before.astype(f32).astype(bf16), preferred_element_type=f32).astype(jnp.int32)
        high = lax.shift_right_logical(slot, 5)
        codes = jnp.concatenate(
            [jnp.broadcast_to(high, (8, elements)), jnp.broadcast_to(slot - high * 32, (8, elements))], 0
        )
        tagged = jnp.concatenate([cond, codes.astype(f32).astype(bf16)], 0)
        room = s1_ref.shape[-1]
        position = lax.broadcasted_iota(jnp.int32, (room, elements), 0)
        for g, ref in ((1, s1_ref), (2, s2_ref), (3, s3_ref)):
            take = ((position == rank[g : g + 1]) & (group == g)).astype(f32).astype(bf16)
            ref[...] = lax.dot_general(tagged, take, NT, preferred_element_type=f32).astype(bf16)


def unpack_kernel(
    na, par_ref, own_ref, r1_ref, r2_ref, r3_ref, dc_ref, wt_ref, zb_ref, za_ref, wk_ref, a_ref, b_ref
):
    rows = weight_rows(wt_ref[...] * KRYLOV_SCALE)
    got = jnp.concatenate([r[0:512] for r in (r1_ref, r2_ref, r3_ref)], 1)
    tags = [r[512:528].astype(f32) for r in (r1_ref, r2_ref, r3_ref)]
    slots = [(t[0:1] * 32.0 + t[8:9]).astype(jnp.int32) for t in tags]
    slot = jnp.concatenate(slots, 1)
    for j in range(2 * na):
        place = lax.broadcasted_iota(jnp.int32, (LANES, slot.shape[1]), 0) + j * LANES
        put = (place == slot).astype(f32).astype(bf16)
        cols = slice(j * LANES, (j + 1) * LANES)
        moved = own_ref[:, cols].astype(f32) + lax.dot_general(got, put, NT, preferred_element_type=f32)
        kappa = (moved * dc_ref[0:1, cols]).reshape(8, 8, 8, LANES)
        for r in range(8):
            for s in range(8):
                wk_ref[j, r, s] = rows[r][s] * kappa[r, s]
    behind, ahead = send_rims(lambda j: wk_ref[j].reshape(512, LANES), na)
    behind = jnp.where(par_ref[3] > 0, jnp.concatenate([zb_ref[...], behind], 1), 0.0)
    ahead = jnp.where(par_ref[4] > 0, jnp.concatenate([za_ref[...], ahead], 1), 0.0)
    even = par_ref[5] == 0
    a_ref[...] = jnp.where(even, ahead, behind)
    b_ref[...] = jnp.where(even, behind, ahead)


def lines_t(k_ref, x):
    x = x.reshape(4, 128, LANES)
    out = []
    for p in range(2):
        pair = jnp.concatenate([x[2 * p], x[2 * p + 1]], 1)
        high = pair.astype(bf16)
        low = (pair - high.astype(f32)).astype(bf16)
        y = jnp.dot(k_ref[...], jnp.concatenate([high, low], 0), preferred_element_type=f32)
        y = y[:128] + y[128:]
        out += [y[:, :LANES].reshape(2, 8, 8, LANES), y[:, LANES:].reshape(2, 8, 8, LANES)]
    return out


def squares(v, j, other, iw_ref):
    sums = {}
    for r in range(8):
        for s in range(8):
            key = (0 if r == 0 else 2 if r == 7 else 1, 0 if s == 0 else 2 if s == 7 else 1)
            x = v[j, r, s]
            pair = (x * x,) if other is None else (x * x, x * other[j, r, s])
            old = sums.get((key, r))
            sums[(key, r)] = pair if old is None else tuple(a + b for a, b in zip(old, pair))
    total = None
    for (key, _), pair in sums.items():
        weight = iw_ref[j, key[0] * 3 + key[1]]
        pair = tuple(weight * a for a in pair)
        total = pair if total is None else tuple(a + b for a, b in zip(total, pair))
    return total


def gradient_r(v, j, g):
    for s in range(8):
        for r, value in enumerate(along(DERIV, [v[j, r, s] for r in range(8)])):
            g[r, s] = value


def apply_tile(v, j, wk, c, base, kf_ref, kb_ref, y, g, f):
    for p, part in enumerate(lines_t(kf_ref, v[j])):
        for q in range(2):
            f[2 * p + q] = wk(2 * p + q) * part[q]
    gradient_r(v, j, g)
    for r in range(8):
        line = [v[j, r, s] for s in range(8)]
        second = along(DERIV, line)
        k = wk(r)
        flux = []
        for s in range(8):
            first = g[r, s]
            flux.append(k[s] * (second[s] + c * first))
            g[r, s] = k[s] * (first + c * second[s])
        for s, value in enumerate(along(DERIV.T, flux)):
            y[j, r, s] = value + (base[r] * float(GLL_W[s])) * line[s]
    parts = lines_t(kb_ref, f[...])
    for s in range(8):
        for r, value in enumerate(along(DERIV.T, [g[r, s] for r in range(8)])):
            y[j, r, s] = y[j, r, s] + value
    for p, part in enumerate(parts):
        y[j, 2 * p : 2 * p + 2] = y[j, 2 * p : 2 * p + 2] + part


def mass_rows(wt, base):
    for r in range(8):
        base[r] = wt * float(GLL_W[r] * coolant_throughput * KRYLOV_SCALE)


def step_kernel(na, first, *refs):
    refs = list(refs)
    take = lambda n: [refs.pop(0) for _ in range(n)]
    ghost = 2 * na
    if first:
        par_ref, z_in, wk_ref, a_in, b_in, dc_ref = take(6)
        prev = None
    else:
        par_ref, y_in, a_in, b_in, wk_ref, wkg_ref, cr_ref, prev = take(8)
    wt_ref, iw_ref, kf_ref, kb_ref, v, y, a_out, b_out, dots = take(9)
    if first:
        wkg_ref, cr_ref = take(2)
    g, f, base = refs
    if first:
        v[0:ghost] = z_in[...]
        even = par_ref[5] == 0
        a, b = a_in[...], b_in[...]
        rims = place_rims(jnp.where(even, a, b), jnp.where(even, b, a))
        v[ghost] = rims[0:512].reshape(8, 8, 8, LANES)
        wkg_ref[...] = rims[640:1152].reshape(8, 8, 8, LANES)
        for j in range(ghost):
            cr_ref[j] = jnp.broadcast_to(dc_ref[1:2, j * LANES : (j + 1) * LANES], (8, LANES))
        cr_ref[ghost] = rims[512:520]
        assemble_axial(na, v)
    else:
        v[...] = y_in[...]
        add_faces(na, par_ref, v, a_in, b_in)
    mass_rows(wt_ref[...], base)
    totals = None
    for j in range(ghost + 1):
        if j < ghost:
            sums = squares(v, j, prev, iw_ref)
            totals = sums if totals is None else [a + b for a, b in zip(totals, sums)]
            wk = lambda r: wk_ref[j, r]
        else:
            wk = lambda r: wkg_ref[r]
        apply_tile(v, j, wk, cr_ref[j], base, kf_ref, kb_ref, y, g.at[j % 2], f.at[j % 2])
    for k, value in enumerate(totals):
        dots[k] = value
    assemble_axial(na, y)
    assemble_lateral(na, par_ref, y, a_out, b_out)


def last_kernel(na, par_ref, y_in, a_in, b_in, wk_ref, cr_ref, prev, wt_ref, iw_ref, kf_ref, d0, d1, d2, d3, v, all_dots, g, base):
    ghost = 2 * na
    v[...] = y_in[...]
    add_faces(na, par_ref, v, a_in, b_in)
    mass_rows(wt_ref[...], base)
    totals = None
    for j in range(ghost):
        gj = g.at[j % 2]
        third = lines_t(kf_ref, v[j])
        sums = list(squares(v, j, prev, iw_ref))
        gradient_r(v, j, gj)
        c = 2.0 * cr_ref[j]
        total = None
        for r in range(8):
            line = [v[j, r, s] for s in range(8)]
            second = along(DERIV, line)
            row = None
            for s in range(8):
                one, two, three = gj[r, s], second[s], third[r // 2][r % 2, s]
                term = (base[r] * float(GLL_W[s])) * (line[s] * line[s])
                term = term + wk_ref[j, r, s] * (one * (one + c * two) + two * two + three * three)
                row = term if row is None else row + term
            total = row if total is None else total + row
        sums.append(total)
        totals = sums if totals is None else [a + b for a, b in zip(totals, sums)]
    lane = lane_index(1)
    rows = [d0[0], d1[1], d1[0], d2[1], d2[0], d3[1], d3[0], totals[1], totals[0], totals[2]]
    out = jnp.zeros((1, LANES), f32)
    for k, row in enumerate(rows):
        out = jnp.where(lane == k, jnp.sum(jnp.sum(row, 0, keepdims=True), 1, keepdims=True), out)
    all_dots[...] = jnp.broadcast_to(out[None], all_dots.shape)


def solve_moments(m_ref, coef_ref):
    sums = jnp.sum(m_ref[:, 0, :], 0, keepdims=True)
    lane = lane_index(1)
    m = [jnp.sum(jnp.where(lane == k, sums, 0.0), 1, keepdims=True) for k in range(2 * ITERS)]
    n = ITERS
    low = [[None] * n for _ in range(n)]
    diag = [None] * n
    for j in range(n):
        acc = [m[i + j + 1] for i in range(n)]
        for k in range(j):
            scaled = low[j][k] * diag[k]
            for i in range(j, n):
                acc[i] = acc[i] - low[i][k] * scaled
        diag[j] = acc[j]
        for i in range(j + 1, n):
            low[i][j] = acc[i] / acc[j]
    z = []
    for i in range(n):
        value = m[i]
        for k in range(i):
            value = value - low[i][k] * z[k]
        z.append(value)
    c = [z[i] / diag[i] for i in range(n)]
    for i in reversed(range(n)):
        for k in range(i + 1, n):
            c[i] = c[i] - low[k][i] * c[k]
    for k, x in enumerate(c):
        coef_ref[k] = jnp.broadcast_to(x * KRYLOV_SCALE, (8, LANES))


def combine_kernel(na, planes, m_ref, v0, v1, v2, v3, v4, out_ref, coef_ref):
    i = pl.program_id(0)

    @pl.when(i == 0)
    def _():
        solve_moments(m_ref, coef_ref)

    c = [coef_ref[k] for k in range(ITERS)]
    step = 2 * na
    for n in range(planes):
        r = i * planes + n
        for s in range(8):
            base = (n * 8 + s) * 8 * step
            for l in range(2):
                for at in range(na):
                    x = None
                    for coef, v in zip(c, (v0, v1, v2, v3, v4)):
                        term = coef * v[l * na + at, r, s]
                        x = term if x is None else x + term
                    out_ref[pl.ds(base + at * 2 + l, 8, stride=step), :] = x


def slab_swap(x, start):
    n, m = lax.axis_size("slab"), lax.axis_size("chan")
    pairs = [(i * m + c, (i + 1) * m + c) for i in range(start, n - 1, 2) for c in range(m)]
    busy = {i for pair in pairs for i in pair}
    pairs += [(i, i + 1) for i in range(0, n * m, 2) if i not in busy]
    return lax.ppermute(x, ("slab", "chan"), pairs + [(j, i) for i, j in pairs])


def swap(x, axis, start):
    n = lax.axis_size(axis)
    pairs = [((start + i) % n, (start + i + 1) % n) for i in range(0, n, 2)]
    return lax.ppermute(x, axis, pairs + [(j, i) for i, j in pairs])


def around(x, by):
    n = lax.axis_size("slab") * lax.axis_size("chan")
    return lax.ppermute(x, ("slab", "chan"), [(i, (i + by) % n) for i in range(n)])


def product_weights(count_l, count_a):
    slab, chan = lax.axis_index("slab"), lax.axis_index("chan")
    axial = slab * count_a + jnp.arange(count_a)
    lateral = chan * count_l + jnp.arange(count_l)
    last_a = lax.axis_size("slab") * count_a - 1
    last_l = lax.axis_size("chan") * count_l - 1
    half = lambda cond: jnp.where(cond, 0.5, 1.0).astype(f32)
    along_a = jnp.stack([half(axial > 0), jnp.ones(count_a, f32), half(axial < last_a)])
    along_l = jnp.stack([half(lateral > 0), jnp.ones(count_l, f32), half(lateral < last_l)])
    weights = along_a[:, None, None, :] * along_l[None, :, :, None]
    weights = weights.reshape(9, -1, LANES).transpose(1, 0, 2)
    return jnp.broadcast_to(weights[:, :, None, :], weights.shape[:2] + (8, LANES))


def on_device(
    stream_speed_field,
    liquid_to_solid_element,
    previous_panel_warmth,
    pointwise_energy_source,
    coked_element_flags,
    coking_thickness_plies,
):
    count_l, count_a = coked_element_flags.shape
    assert count_l == 2 and count_a % LANES == 0
    elements = count_l * count_a
    na = count_a // LANES
    tiles = count_l * na
    chan = lax.axis_size("chan")
    total = lax.axis_size("slab") * chan
    slab_at, chan_at = lax.axis_index("slab"), lax.axis_index("chan")
    me = (slab_at * chan + chan_at).astype(jnp.int32).reshape(1)
    position = [
        chan_at % 2,
        chan_at > 0,
        chan_at < chan - 1,
        slab_at > 0,
        slab_at < lax.axis_size("slab") - 1,
        slab_at % 2,
    ]
    position = jnp.stack([jnp.asarray(x, jnp.int32) for x in position])

    wt = jnp.asarray(np.broadcast_to(GLL_W[:, None], (8, LANES)), f32)
    wr = jnp.asarray(np.broadcast_to((GLL_W[:, None] * GLL_W)[:, :, None], (8, 8, LANES)), f32)
    kf, kb = (jnp.asarray(k) for k in line_matrices())
    kfluid = jnp.asarray(fluid_matrix())

    layers = coking_thickness_plies.astype(f32)
    flags = coked_element_flags.astype(f32)
    damping = jnp.where(coked_element_flags == 1, 1.0 / (1.0 + layer_damp * layers), jnp.ones_like(layers))
    cross = cross_gain * flags * layers / (layers + 1.0)
    dc = jnp.stack([damping.reshape(elements), cross.reshape(elements)])
    iw = product_weights(count_l, count_a)

    def as_rows(x):
        x = x.reshape(8, 8, 8, count_l, na, LANES).transpose(0, 1, 2, 4, 3, 5)
        return x.reshape(512 * tiles, LANES)

    field = (tiles, 8, 8, 8, LANES)
    whole = (tiles + 1, 8, 8, 8, LANES)
    face = (na + 1, 8, 8, LANES)
    shape = lambda s, d=f32: jax.ShapeDtypeStruct(s, d)
    kept = vmem
    split = elements // LANES
    width = LANES
    room = elements // 4
    in_hbm = lambda x: pltpu.with_memory_space_constraint(x, pltpu.HBM)
    here = lambda: pl.BlockSpec(memory_space=pltpu.VMEM)
    scalars = pl.BlockSpec(memory_space=pltpu.SMEM)
    steps = 4
    rows = 512 * tiles // steps
    z, a, b = pl.pallas_call(
        functools.partial(source_kernel, na, 8 // steps),
        grid=(steps,),
        in_specs=[scalars]
        + [pl.BlockSpec((rows, LANES), lambda i: (i, 0))] * 2
        + [pl.BlockSpec((8, 8, LANES), lambda i: (0, 0, 0))],
        out_specs=[here()] * 3,
        out_shape=[kept(field), kept((na, 8, 8, LANES)), kept((na, 8, 8, LANES))],
        compiler_params=pltpu.CompilerParams(vmem_limit_bytes=12 * 1024 * 1024),
    )(position, in_hbm(as_rows(previous_panel_warmth)), in_hbm(as_rows(pointwise_energy_source)), in_hbm(wr))
    a, b = swap(a, "chan", 0), swap(b, "chan", 1)

    velocity, z = lax.optimization_barrier((stream_speed_field, z))
    out = pl.pallas_call(
        functools.partial(fluid_kernel, chan, total),
        grid=(split,),
        in_specs=[
            scalars,
            pl.BlockSpec((3, 8, 8, 8, width), lambda i: (0, 0, 0, 0, i)),
            pl.BlockSpec((1, elements), lambda i: (0, 0)),
            pl.BlockSpec(kfluid.shape, lambda i: (0, 0)),
        ],
        out_specs=[pl.BlockSpec((3, 8, 8, 8, width), lambda i: (0, 0, 0, 0, i))] + [here()] * 4,
        out_shape=[shape(stream_speed_field.shape, bf16), kept((512, elements), bf16)]
        + [kept((528, room), bf16)] * 3,
        scratch_shapes=[pltpu.VMEM((split, 512, width), bf16), pltpu.VMEM((3, 8, 8, 8, width), f32)],
        compiler_params=pltpu.CompilerParams(vmem_limit_bytes=24 * 1024 * 1024),
    )(me, in_hbm(velocity), in_hbm(liquid_to_solid_element.reshape(1, elements)), in_hbm(kfluid))
    stepped, own, *outgoing = out
    received = [around(x, by) for x, by in zip(outgoing, (1, -1, chan))]
    z, z_behind, z_ahead = call(
        functools.partial(rim_kernel, na),
        [kept(field), kept((2 * RIM, 640)), kept((2 * RIM, 640))],
        position,
        z,
        a,
        b,
        dc,
        smem=1,
    )
    wk, a, b = call(
        functools.partial(unpack_kernel, na),
        [kept(field), kept((2 * RIM, 1152)), kept((2 * RIM, 1152))],
        position,
        own,
        *received,
        dc,
        wt,
        z_behind,
        z_ahead,
        smem=1,
    )
    a, b = slab_swap(a, 0), slab_swap(b, 1)

    basis, products = [], []
    for number in range(ITERS - 1):
        first = number == 0
        outs = [kept(whole), kept(whole), kept(face), kept(face), kept((2, 8, LANES))]
        if first:
            args = (z, wk, a, b, dc)
            outs += [kept((8, 8, 8, LANES)), kept((tiles + 1, 8, LANES))]
        else:
            args = (y, a, b, wk, wkg, cr, basis[-1])
        got = call(
            functools.partial(step_kernel, na, first),
            outs,
            position,
            *args,
            wt,
            iw,
            kf,
            kb,
            smem=1,
            scratch=[pltpu.VMEM((2, 8, 8, 8, LANES), f32)] * 2 + [pltpu.VMEM((8, 8, LANES), f32)],
        )
        if first:
            wkg, cr = got[5:]
        v, y, a, b, dots = got[:5]
        basis.append(v)
        products.append(dots)
        a, b = swap(a, "chan", 0), swap(b, "chan", 1)
    v, sums = call(
        functools.partial(last_kernel, na),
        [kept(whole), kept((total, 1, LANES))],
        position,
        y,
        a,
        b,
        wk,
        cr,
        basis[-1],
        wt,
        iw,
        kf,
        *products,
        smem=1,
        scratch=[pltpu.VMEM((2, 8, 8, 8, LANES), f32), pltpu.VMEM((8, 8, LANES), f32)],
    )
    basis.append(v)
    sums = lax.all_to_all(sums, ("slab", "chan"), 0, 0)
    x = pl.pallas_call(
        functools.partial(combine_kernel, na, 8 // steps),
        grid=(steps,),
        in_specs=[here()] * 6,
        out_specs=pl.BlockSpec((rows, LANES), lambda i: (i, 0)),
        out_shape=shape((512 * tiles, LANES)),
        scratch_shapes=[pltpu.VMEM((ITERS, 8, LANES), f32)],
        compiler_params=pltpu.CompilerParams(vmem_limit_bytes=12 * 1024 * 1024),
    )(sums, *basis)
    x = x.reshape(8, 8, 8, na, count_l, LANES).transpose(0, 1, 2, 4, 3, 5)
    return stepped, x.reshape(8, 8, 8, count_l, count_a)


def solution(mesh):
    in_specs = (
        P(None, None, None, None, ("slab", "chan")),
        P(("slab", "chan")),
        P(None, None, None, "chan", "slab"),
        P(None, None, None, "chan", "slab"),
        P("chan", "slab"),
        P("chan", "slab"),
    )
    out_specs = (P(None, None, None, None, ("slab", "chan")), P(None, None, None, "chan", "slab"))
    return jax.shard_map(
        on_device, mesh=mesh, in_specs=in_specs, out_specs=out_specs, check_vma=False
    )
```

```python
import functools

import jax
import jax.numpy as jnp
import numpy as np
from jax import lax
from jax.experimental import pallas as pl
from jax.experimental.pallas import tpu as pltpu
from jax.sharding import PartitionSpec as P

ITERS = 5
LANES = 128
RIM = 8
KRYLOV_SCALE = 1.0 / 256.0

highest = lax.Precision.HIGHEST
f32 = jnp.float32
bf16 = jnp.bfloat16
coolant_throughput = 0.05
time_step = 0.01
viscosity = 0.02
cross_gain = 0.4
layer_damp = 0.25

NT = (((1,), (1,)), ((), ()))
TN = (((0,), (0,)), ((), ()))


def gll_tables():
    points = np.array(
        [
            -1.0,
            -0.8717401485096066,
            -0.5917001814331423,
            -0.2092992179024789,
            0.2092992179024789,
            0.5917001814331423,
            0.8717401485096066,
            1.0,
        ]
    )
    weights = np.array(
        [
            1.0 / 28.0,
            0.2107042271435061,
            0.3411226924835044,
            0.4124587946587038,
            0.4124587946587038,
            0.3411226924835044,
            0.2107042271435061,
            1.0 / 28.0,
        ]
    )
    lower_poly = np.ones(8)
    upper_poly = points.copy()
    for degree in range(1, 7):
        next_poly = ((2 * degree + 1) * points * upper_poly - degree * lower_poly) / (degree + 1)
        lower_poly = upper_poly
        upper_poly = next_poly
    gaps_matrix = points[:, None] - points[None, :] + np.eye(8)
    derivative = upper_poly[:, None] / (upper_poly[None, :] * gaps_matrix)
    derivative = derivative * (1.0 - np.eye(8))
    derivative[0, 0] = -14.0
    derivative[7, 7] = 14.0
    return derivative, weights


DERIV, GLL_W = gll_tables()
DERIV = DERIV.astype(np.float32).astype(np.float64)
GLL_W = GLL_W.astype(np.float32).astype(np.float64)


def split_hi_lo(matrix):
    high = np.asarray(matrix, np.float32).astype(jnp.bfloat16)
    low = (np.asarray(matrix, np.float64) - high.astype(np.float64)).astype(np.float32)
    return high, low.astype(jnp.bfloat16)


def line_matrices():
    out = []
    for matrix in (DERIV, DERIV.T):
        high, low = split_hi_lo(np.kron(np.eye(16), matrix))
        upper = np.concatenate([high, high], 1)
        out.append(np.concatenate([upper, np.concatenate([low, np.zeros_like(low)], 1)], 0))
    return out


def fluid_matrix():
    eye8 = np.eye(8)
    square = DERIV @ DERIV
    second = np.kron(DERIV, eye8)
    third = np.kron(eye8, DERIV)
    curve = np.kron(square, eye8) + np.kron(eye8, square)
    return np.concatenate([np.concatenate(split_hi_lo(np.kron(np.eye(2), m)), 1) for m in (second, third, curve)], 0)


def halves_of(line):
    return [line[j] + line[7 - j] for j in range(4)], [line[j] - line[7 - j] for j in range(4)]


def combined(matrix, parts, sign):
    even, odd = parts
    result = [None] * 8
    for i in range(4):
        p = sum(float(0.5 * (matrix[i, j] + matrix[i, 7 - j])) * even[j] for j in range(4))
        q = sum(float(0.5 * (matrix[i, j] - matrix[i, 7 - j])) * odd[j] for j in range(4))
        result[i] = p + q
        result[7 - i] = q - p if sign < 0 else p - q
    return result


def along(matrix, line):
    return combined(matrix, halves_of(line), -1)


def lane_index(rows=8):
    return lax.broadcasted_iota(jnp.int32, (rows, LANES), 1)


def vmem(shape, dtype=f32):
    return pltpu.VMEM(shape, dtype)


def call(kernel, out_shape, *args, smem=0, scratch=(), limit=12, **kw):
    specs = [pl.BlockSpec(memory_space=pltpu.SMEM)] * smem
    specs += [pl.BlockSpec(memory_space=pltpu.VMEM)] * (len(args) - smem)
    outs = [pl.BlockSpec(memory_space=pltpu.VMEM) for _ in out_shape]
    return pl.pallas_call(
        kernel,
        in_specs=specs,
        out_specs=outs,
        out_shape=out_shape,
        scratch_shapes=scratch,
        compiler_params=pltpu.CompilerParams(vmem_limit_bytes=limit * 1024 * 1024),
        **kw,
    )(*args)


def weight_rows(wt):
    return [[float(GLL_W[r] * GLL_W[s]) * wt for s in range(8)] for r in range(8)]


def sel_matrix(l, first_lane):
    row = lax.broadcasted_iota(jnp.int32, (2 * RIM, LANES), 0)
    lane = lax.broadcasted_iota(jnp.int32, (2 * RIM, LANES), 1)
    return ((row - l * RIM + first_lane == lane) & (row >= l * RIM) & (row < (l + 1) * RIM)).astype(f32)


def place_matrix(first_lane):
    row = lax.broadcasted_iota(jnp.int32, (2 * RIM, LANES), 0)
    lane = lax.broadcasted_iota(jnp.int32, (2 * RIM, LANES), 1)
    target = jnp.where(row < RIM, row + first_lane, row - RIM + first_lane + LANES // 2)
    return (target == lane).astype(f32)


def send_rims(tile_rows, na):
    behind = sum(
        lax.dot_general(sel_matrix(l, 0), tile_rows(l * na), NT, precision=highest, preferred_element_type=f32)
        for l in range(2)
    )
    ahead = sum(
        lax.dot_general(
            sel_matrix(l, LANES - RIM), tile_rows(l * na + na - 1), NT, precision=highest, preferred_element_type=f32
        )
        for l in range(2)
    )
    return behind, ahead


def place_rims(from_ahead, from_behind):
    a = lax.dot_general(from_ahead, place_matrix(0), TN, precision=highest, preferred_element_type=f32)
    b = lax.dot_general(
        from_behind, place_matrix(LANES // 2 - RIM), TN, precision=highest, preferred_element_type=f32
    )
    return a + b


def source_kernel(na, planes, par_ref, p_ref, q_ref, wr_ref, z_ref, a_ref, b_ref):
    step = 2 * na
    for n in range(planes):
        r = pl.program_id(0) * planes + n
        wr = wr_ref[r]
        ends = {}
        for s in range(8):
            base = (n * 8 + s) * 8 * step
            for l in range(2):
                for at in range(na):
                    pick = pl.ds(base + at * 2 + l, 8, stride=step)
                    value = (wr * float(GLL_W[s])) * (coolant_throughput * p_ref[pick, :] + q_ref[pick, :])
                    if (l, s) in ((0, 0), (0, 7), (1, 0), (1, 7)):
                        ends[l, s, at] = value
                    else:
                        z_ref[l * na + at, r, s] = value
        for at in range(na):
            shared = ends[0, 7, at] + ends[1, 0, at]
            z_ref[at, r, 7] = shared
            z_ref[na + at, r, 0] = shared
            lower, upper = ends[0, 0, at], ends[1, 7, at]
            z_ref[at, r, 0] = lower
            z_ref[na + at, r, 7] = upper
            send_faces(par_ref, (at, r), lower, upper, a_ref, b_ref)


def rim_kernel(na, par_ref, z_in, a_ref, b_ref, dc_ref, z_ref, behind_ref, ahead_ref):
    z_ref[...] = z_in[...]
    for r in range(8):
        for at in range(na):
            lower, upper = got_faces(par_ref, (at, r), a_ref, b_ref)
            z_ref[at, r, 0] = z_ref[at, r, 0] + lower
            z_ref[na + at, r, 7] = z_ref[na + at, r, 7] + upper

    def tile_rows(j):
        cross = jnp.broadcast_to(dc_ref[1:2, j * LANES : (j + 1) * LANES], (LANES, LANES))
        return jnp.concatenate([z_ref[j].reshape(512, LANES), cross], 0)

    behind_ref[...], ahead_ref[...] = send_rims(tile_rows, na)


def send_faces(par_ref, at, lower, upper, a_ref, b_ref):
    even = par_ref[0] == 0
    lower = jnp.where(par_ref[1] > 0, lower, 0.0)
    upper = jnp.where(par_ref[2] > 0, upper, 0.0)
    a_ref[at] = jnp.where(even, upper, lower)
    b_ref[at] = jnp.where(even, lower, upper)


def got_faces(par_ref, at, a_ref, b_ref):
    even = par_ref[0] == 0
    a, b = a_ref[at], b_ref[at]
    return jnp.where(even, b, a), jnp.where(even, a, b)


def axial_row(l, far, near):
    ghost = len(far) - 1
    lane = lane_index()
    half = LANES // 2
    roll = pltpu.roll
    right = [roll(x, 1, 1) for x in far]
    left = [roll(x, LANES - 1, 1) for x in near]
    new_far, new_near = [], []
    for at in range(ghost):
        if at > 0:
            carry = right[at - 1]
        else:
            carry = roll(far[ghost], half + 1, 1) if l == 0 else right[ghost]
        new_near.append(near[at] + jnp.where(lane == 0, carry, right[at]))
        if at < ghost - 1:
            carry = left[at + 1]
        else:
            carry = left[ghost] if l == 0 else roll(near[ghost], half - 1, 1)
        new_far.append(far[at] + jnp.where(lane == LANES - 1, carry, left[at]))
    carry = right[ghost - 1] if l == 0 else roll(far[ghost - 1], half + 1, 1)
    new_near.append(near[ghost] + jnp.where(lane == half * l, carry, right[ghost]))
    carry = roll(near[0], half - 1, 1) if l == 0 else left[0]
    new_far.append(far[ghost] + jnp.where(lane == half * (l + 1) - 1, carry, left[ghost]))
    return new_far, new_near


def assemble_axial(na, y):
    ghost = 2 * na
    low = lane_index() < LANES // 2
    for s in range(8):
        rims = []
        for l in range(2):
            tiles = list(range(l * na, l * na + na)) + [ghost]
            far, near = axial_row(l, [y[j, 7, s] for j in tiles], [y[j, 0, s] for j in tiles])
            for n, j in enumerate(tiles[:-1]):
                y[j, 7, s] = far[n]
                y[j, 0, s] = near[n]
            rims.append((far[-1], near[-1]))
        y[ghost, 7, s] = jnp.where(low, rims[0][0], rims[1][0])
        y[ghost, 0, s] = jnp.where(low, rims[0][1], rims[1][1])


def assemble_lateral(na, y):
    ghost = 2 * na
    half = LANES // 2
    low = lane_index() < half
    for r in range(8):
        for at in range(na):
            shared = y[at, r, 7] + y[na + at, r, 0]
            y[at, r, 7] = shared
            y[na + at, r, 0] = shared
        upper = y[ghost, r, 7]
        lower = y[ghost, r, 0]
        y[ghost, r, 7] = upper + jnp.where(low, pltpu.roll(lower, half, 1), 0.0)
        y[ghost, r, 0] = lower + jnp.where(low, 0.0, pltpu.roll(upper, half, 1))


def turn(x, by):
    return x if by % LANES == 0 else pltpu.roll(x, by % LANES, 1)


def pack_rim(planes, l):
    lane = lane_index()
    half = LANES // 2
    out = None
    for r, x in enumerate(planes):
        at = 2 * RIM * r
        near = turn(x, at - half * l)
        far = turn(x, at + RIM - (half * (l + 1) - RIM))
        near = jnp.where((lane >= at) & (lane < at + RIM), near, 0.0)
        both = jnp.where((lane >= at + RIM) & (lane < at + 2 * RIM), far, near)
        out = both if out is None else out + both
    return out


def unpack_rim(x, r, l):
    lane = lane_index()
    half = LANES // 2
    at = 2 * RIM * r
    near = turn(x, half * l - at)
    far = turn(x, half * (l + 1) - RIM - (at + RIM))
    near = jnp.where((lane >= half * l) & (lane < half * l + RIM), near, 0.0)
    return jnp.where((lane >= half * (l + 1) - RIM) & (lane < half * (l + 1)), far, near)


def add_faces(na, par_ref, v, a_ref, b_ref):
    ghost = 2 * na
    for at in range(na):
        for r in range(8):
            lower, upper = got_faces(par_ref, at * 8 + r, a_ref, b_ref)
            v[at, r, 0] = v[at, r, 0] + lower
            v[na + at, r, 7] = v[na + at, r, 7] + upper
    lower, upper = got_faces(par_ref, na * 8, a_ref, b_ref)
    for r in range(8):
        v[ghost, r, 0] = v[ghost, r, 0] + unpack_rim(lower, r, 0)
        v[ghost, r, 7] = v[ghost, r, 7] + unpack_rim(upper, r, 1)


def fluid_kernel(
    chan, total, me_ref, u_ref, l2s_ref, k_ref, out_ref, own_ref, s1_ref, s2_ref, s3_ref, c_ref, t_ref
):
    i = pl.program_id(0)
    k = k_ref[...]
    square = DERIV @ DERIV
    for c in range(3):
        for s in range(8):
            parts = halves_of([u_ref[c, r, s].astype(f32) for r in range(8)])
            slope = combined(DERIV, parts, -1)
            curve = combined(square, parts, 1)
            for r in range(8):
                t_ref[c, r, s] = viscosity * curve[r] - u_ref[0, r, s].astype(f32) * slope[r]
    for p in range(2):
        speed = [None] * 4
        for c in range(3):
            x = u_ref[c, 4 * p : 4 * p + 4].astype(f32).reshape(2, 128, LANES)
            x = jnp.concatenate([x[0], x[1]], 1).astype(bf16)
            y = jnp.dot(k, jnp.concatenate([x, x], 0), preferred_element_type=f32)
            for h in range(2):
                part = y[:, h * LANES : (h + 1) * LANES].reshape(3, 2, 8, 8, LANES)
                for q in range(2):
                    r = 4 * p + 2 * h + q
                    second, third, curve = part[0, q], part[1, q], part[2, q]
                    u2, u3 = u_ref[1, r].astype(f32), u_ref[2, r].astype(f32)
                    rate = t_ref[c, r] + viscosity * curve - u2 * second - u3 * third
                    new = (u_ref[c, r].astype(f32) + time_step * rate).astype(bf16)
                    out_ref[c, r] = new
                    new = new.astype(f32)
                    old = speed[2 * h + q]
                    speed[2 * h + q] = new * new if old is None else old + new * new
        for n, value in enumerate(speed):
            r = 4 * p + n
            c_ref[i, r * 64 : (r + 1) * 64] = (1.0 + 0.5 * value).astype(bf16).reshape(64, LANES)

    @pl.when(i == pl.num_programs(0) - 1)
    def _():
        elements = l2s_ref.shape[-1]
        cond = jnp.concatenate([c_ref[n] for n in range(c_ref.shape[0])], 1)
        l2s = l2s_ref[...]
        if elements & (elements - 1) == 0:
            owner = lax.shift_right_logical(l2s, elements.bit_length() - 1)
            slot = l2s & (elements - 1)
        else:
            owner = l2s // elements
            slot = l2s - owner * elements
        ahead = owner - me_ref[0]
        ahead = jnp.where(ahead < 0, ahead + total, ahead)
        group = jnp.where(ahead == 1, 1, jnp.where(ahead == total - 1, 2, jnp.where(ahead == chan, 3, 0)))
        place = lax.broadcasted_iota(jnp.int32, (elements, elements), 0)
        keep = ((place == slot) & (group == 0)).astype(f32).astype(bf16)
        own_ref[...] = lax.dot_general(cond, keep, NT, preferred_element_type=f32).astype(bf16)
        kinds = lax.broadcasted_iota(jnp.int32, (16, elements), 0)
        marks = (kinds == group).astype(f32).astype(bf16)
        before = lax.broadcasted_iota(jnp.int32, (elements, elements), 0) < lax.broadcasted_iota(
            jnp.int32, (elements, elements), 1
        )
        rank = jnp.dot(marks, before.astype(f32).astype(bf16), preferred_element_type=f32).astype(jnp.int32)
        high = lax.shift_right_logical(slot, 5)
        codes = jnp.concatenate(
            [jnp.broadcast_to(high, (8, elements)), jnp.broadcast_to(slot - high * 32, (8, elements))], 0
        )
        tagged = jnp.concatenate([cond, codes.astype(f32).astype(bf16)], 0)
        room = s1_ref.shape[-1]
        position = lax.broadcasted_iota(jnp.int32, (room, elements), 0)
        even = me_ref[0] % 2 == 0
        one, two = rank[1:2], rank[2:3]
        sends = (
            (jnp.where(even, 1, 2), jnp.where(even, one, two), s1_ref),
            (jnp.where(even, 2, 1), jnp.where(even, two, one), s2_ref),
            (3, rank[3:4], s3_ref),
        )
        for g, order, ref in sends:
            take = ((position == order) & (group == g)).astype(f32).astype(bf16)
            ref[...] = lax.dot_general(tagged, take, NT, preferred_element_type=f32).astype(bf16)


def unpack_kernel(
    na, par_ref, own_ref, r1_ref, r2_ref, r3_ref, dc_ref, wt_ref, zb_ref, za_ref, wk_ref, a_ref, b_ref
):
    rows = weight_rows(wt_ref[...] * KRYLOV_SCALE)
    got = jnp.concatenate([r[0:512] for r in (r1_ref, r2_ref, r3_ref)], 1)
    tags = [r[512:528].astype(f32) for r in (r1_ref, r2_ref, r3_ref)]
    slots = [(t[0:1] * 32.0 + t[8:9]).astype(jnp.int32) for t in tags]
    slot = jnp.concatenate(slots, 1)
    for j in range(2 * na):
        place = lax.broadcasted_iota(jnp.int32, (LANES, slot.shape[1]), 0) + j * LANES
        put = (place == slot).astype(f32).astype(bf16)
        cols = slice(j * LANES, (j + 1) * LANES)
        moved = own_ref[:, cols].astype(f32) + lax.dot_general(got, put, NT, preferred_element_type=f32)
        kappa = (moved * dc_ref[0:1, cols]).reshape(8, 8, 8, LANES)
        for r in range(8):
            for s in range(8):
                wk_ref[j, r, s] = rows[r][s] * kappa[r, s]
    behind, ahead = send_rims(lambda j: wk_ref[j].reshape(512, LANES), na)
    behind = jnp.where(par_ref[3] > 0, jnp.concatenate([zb_ref[...], behind], 1), 0.0)
    ahead = jnp.where(par_ref[4] > 0, jnp.concatenate([za_ref[...], ahead], 1), 0.0)
    even = par_ref[5] == 0
    a_ref[...] = jnp.where(even, ahead, behind)
    b_ref[...] = jnp.where(even, behind, ahead)


def lines_t(k_ref, blocks):
    out = []
    for p in range(0, len(blocks), 2):
        pair = jnp.concatenate(blocks[p : p + 2], 1)
        high = pair.astype(bf16)
        low = (pair - high.astype(f32)).astype(bf16)
        y = jnp.dot(k_ref[...], jnp.concatenate([high, low], 0), preferred_element_type=f32)
        y = y[:128] + y[128:]
        out += [y[:, n * LANES : (n + 1) * LANES].reshape(2, 8, 8, LANES) for n in range(len(blocks[p : p + 2]))]
    return out


def blocks_of(x):
    x = x.reshape(4, 128, LANES)
    return [x[n] for n in range(4)]


def squares(v, j, other, iw_ref):
    sums = {}
    for r in range(8):
        for s in range(8):
            key = (0 if r == 0 else 2 if r == 7 else 1, 0 if s == 0 else 2 if s == 7 else 1)
            x = v[j, r, s]
            pair = (x * x,) if other is None else (x * x, x * other[j, r, s])
            old = sums.get((key, r))
            sums[(key, r)] = pair if old is None else tuple(a + b for a, b in zip(old, pair))
    total = None
    for (key, _), pair in sums.items():
        weight = iw_ref[j, key[0] * 3 + key[1]]
        pair = tuple(weight * a for a in pair)
        total = pair if total is None else tuple(a + b for a, b in zip(total, pair))
    return total


def gradient_r(v, j, g):
    for s in range(8):
        for r, value in enumerate(along(DERIV, [v[j, r, s] for r in range(8)])):
            g[r, s] = value


def fluxes(v, j, wk, c, kf_ref, g, f1, f2, f3):
    for p, part in enumerate(lines_t(kf_ref, blocks_of(v[j]))):
        for q in range(2):
            f3[j, 2 * p + q] = wk(2 * p + q) * part[q]
    gradient_r(v, j, g)
    for r in range(8):
        second = along(DERIV, [v[j, r, s] for s in range(8)])
        k = wk(r)
        for s in range(8):
            first = g[r, s]
            f2[j, r, s] = k[s] * (second[s] + c * first)
            f1[j, r, s] = k[s] * (first + c * second[s])


def lateral_faces(na, par_ref, v, f1, f2, f3, base, kb_ref, a_ref, b_ref):
    rows = [[(l * na + at, 7 * l) for at in range(na)] + [(2 * na, 7 * l)] for l in range(2)]
    flat = rows[0] + rows[1]
    blocks = []
    for n in range(0, len(flat), 2):
        pair = [f3[j, :, s].reshape(64, LANES) for j, s in flat[n : n + 2]]
        blocks.append(jnp.concatenate(pair, 0))
    thirds = []
    for part in lines_t(kb_ref, blocks):
        part = part.reshape(2, 8, 8, LANES)
        thirds += [part[0], part[1]]
    faces = []
    for (j, s), third in zip(flat, thirds):
        first = along(DERIV.T, [f1[j, r, s] for r in range(8)])
        face = []
        for r in range(8):
            second = sum(float(DERIV[i, s]) * f2[j, r, i] for i in range(8) if DERIV[i, s] != 0.0)
            face.append(second + (base[r] * float(GLL_W[s])) * v[j, r, s] + first[r] + third[r])
        faces.append(face)
    for l in range(2):
        row = faces[l * (na + 1) : (l + 1) * (na + 1)]
        far, near = axial_row(l, [x[7] for x in row], [x[0] for x in row])
        for x, last, start in zip(row, far, near):
            x[7], x[0] = last, start
    for at in range(na):
        for r in range(8):
            send_faces(par_ref, at * 8 + r, faces[at][r], faces[na + 1 + at][r], a_ref, b_ref)
    send_faces(par_ref, na * 8, pack_rim(faces[na], 0), pack_rim(faces[2 * na + 1], 1), a_ref, b_ref)


def mass_rows(wt, base):
    for r in range(8):
        base[r] = wt * float(GLL_W[r] * coolant_throughput * KRYLOV_SCALE)


def flux_kernel(na, first, *refs):
    refs = list(refs)
    take = lambda n: [refs.pop(0) for _ in range(n)]
    ghost = 2 * na
    if first:
        par_ref, z_in, wk_ref, a_in, b_in, dc_ref = take(6)
    else:
        par_ref, _, a_in, b_in, wk_ref, wkg_ref, cr_ref = take(7)
    wt_ref, kf_ref, kb_ref, v, f1, f2, f3, a_out, b_out = take(9)
    if first:
        wkg_ref, cr_ref = take(2)
    g, base = refs
    if first:
        v[0:ghost] = z_in[...]
        even = par_ref[5] == 0
        a, b = a_in[...], b_in[...]
        rims = place_rims(jnp.where(even, a, b), jnp.where(even, b, a))
        v[ghost] = rims[0:512].reshape(8, 8, 8, LANES)
        wkg_ref[...] = rims[640:1152].reshape(8, 8, 8, LANES)
        for j in range(ghost):
            cr_ref[j] = jnp.broadcast_to(dc_ref[1:2, j * LANES : (j + 1) * LANES], (8, LANES))
        cr_ref[ghost] = rims[512:520]
        assemble_axial(na, v)
    else:
        add_faces(na, par_ref, v, a_in, b_in)
    mass_rows(wt_ref[...], base)
    for j in range(ghost + 1):
        if j < ghost:
            wk = lambda r: wk_ref[j, r]
        else:
            wk = lambda r: wkg_ref[r]
        fluxes(v, j, wk, cr_ref[j], kf_ref, g.at[j % 2], f1, f2, f3)
    lateral_faces(na, par_ref, v, f1, f2, f3, base, kb_ref, a_out, b_out)


def rest_kernel(na, first, *refs):
    refs = list(refs)
    prev = None if first else refs.pop(0)
    v, f1, f2, f3, wt_ref, iw_ref, kb_ref, y, dots, base = refs
    ghost = 2 * na
    mass_rows(wt_ref[...], base)
    totals = None
    for j in range(ghost + 1):
        if j < ghost:
            sums = squares(v, j, prev, iw_ref)
            totals = sums if totals is None else [a + b for a, b in zip(totals, sums)]
        parts = lines_t(kb_ref, blocks_of(f3[j]))
        for r in range(8):
            for s, value in enumerate(along(DERIV.T, [f2[j, r, s] for s in range(8)])):
                y[j, r, s] = value + (base[r] * float(GLL_W[s])) * v[j, r, s]
        for s in range(8):
            for r, value in enumerate(along(DERIV.T, [f1[j, r, s] for r in range(8)])):
                y[j, r, s] = y[j, r, s] + value + parts[r // 2][r % 2, s]
    for k, value in enumerate(totals):
        dots[k] = value
    assemble_axial(na, y)
    assemble_lateral(na, y)


def last_kernel(na, par_ref, _, a_in, b_in, wk_ref, cr_ref, prev, wt_ref, iw_ref, kf_ref, d0, d1, d2, d3, v, all_dots, g, base):
    ghost = 2 * na
    add_faces(na, par_ref, v, a_in, b_in)
    mass_rows(wt_ref[...], base)
    totals = None
    for j in range(ghost):
        gj = g.at[j % 2]
        third = lines_t(kf_ref, blocks_of(v[j]))
        sums = list(squares(v, j, prev, iw_ref))
        gradient_r(v, j, gj)
        c = 2.0 * cr_ref[j]
        total = None
        for r in range(8):
            line = [v[j, r, s] for s in range(8)]
            second = along(DERIV, line)
            row = None
            for s in range(8):
                one, two, three = gj[r, s], second[s], third[r // 2][r % 2, s]
                term = (base[r] * float(GLL_W[s])) * (line[s] * line[s])
                term = term + wk_ref[j, r, s] * (one * (one + c * two) + two * two + three * three)
                row = term if row is None else row + term
            total = row if total is None else total + row
        sums.append(total)
        totals = sums if totals is None else [a + b for a, b in zip(totals, sums)]
    lane = lane_index(1)
    rows = [d0[0], d1[1], d1[0], d2[1], d2[0], d3[1], d3[0], totals[1], totals[0], totals[2]]
    out = jnp.zeros((1, LANES), f32)
    for k, row in enumerate(rows):
        out = jnp.where(lane == k, jnp.sum(jnp.sum(row, 0, keepdims=True), 1, keepdims=True), out)
    all_dots[...] = jnp.broadcast_to(out[None], all_dots.shape)


def solve_moments(m_ref, coef_ref):
    sums = jnp.sum(m_ref[:, 0, :], 0, keepdims=True)
    lane = lane_index(1)
    m = [jnp.sum(jnp.where(lane == k, sums, 0.0), 1, keepdims=True) for k in range(2 * ITERS)]
    n = ITERS
    low = [[None] * n for _ in range(n)]
    diag = [None] * n
    for j in range(n):
        acc = [m[i + j + 1] for i in range(n)]
        for k in range(j):
            scaled = low[j][k] * diag[k]
            for i in range(j, n):
                acc[i] = acc[i] - low[i][k] * scaled
        diag[j] = acc[j]
        for i in range(j + 1, n):
            low[i][j] = acc[i] / acc[j]
    z = []
    for i in range(n):
        value = m[i]
        for k in range(i):
            value = value - low[i][k] * z[k]
        z.append(value)
    c = [z[i] / diag[i] for i in range(n)]
    for i in reversed(range(n)):
        for k in range(i + 1, n):
            c[i] = c[i] - low[k][i] * c[k]
    for k, x in enumerate(c):
        coef_ref[k] = jnp.broadcast_to(x * KRYLOV_SCALE, (8, LANES))


def combine_kernel(na, planes, m_ref, v0, v1, v2, v3, v4, out_ref, coef_ref):
    i = pl.program_id(0)

    @pl.when(i == 0)
    def _():
        solve_moments(m_ref, coef_ref)

    c = [coef_ref[k] for k in range(ITERS)]
    step = 2 * na
    for n in range(planes):
        r = i * planes + n
        for s in range(8):
            base = (n * 8 + s) * 8 * step
            for l in range(2):
                for at in range(na):
                    x = None
                    for coef, v in zip(c, (v0, v1, v2, v3, v4)):
                        term = coef * v[l * na + at, r, s]
                        x = term if x is None else x + term
                    out_ref[pl.ds(base + at * 2 + l, 8, stride=step), :] = x


def slab_swap(x, start):
    n, m = lax.axis_size("slab"), lax.axis_size("chan")
    pairs = [(i * m + c, (i + 1) * m + c) for i in range(start, n - 1, 2) for c in range(m)]
    busy = {i for pair in pairs for i in pair}
    pairs += [(i, i + 1) for i in range(0, n * m, 2) if i not in busy]
    return lax.ppermute(x, ("slab", "chan"), pairs + [(j, i) for i, j in pairs])


def swap(x, axis, start):
    n = lax.axis_size(axis)
    pairs = [((start + i) % n, (start + i + 1) % n) for i in range(0, n, 2)]
    return lax.ppermute(x, axis, pairs + [(j, i) for i, j in pairs])


def around(x, by):
    n = lax.axis_size("slab") * lax.axis_size("chan")
    return lax.ppermute(x, ("slab", "chan"), [(i, (i + by) % n) for i in range(n)])


def swap_around(x, start):
    n = lax.axis_size("slab") * lax.axis_size("chan")
    pairs = [((start + i) % n, (start + i + 1) % n) for i in range(0, n, 2)]
    return lax.ppermute(x, ("slab", "chan"), pairs + [(j, i) for i, j in pairs])


def product_weights(count_l, count_a):
    slab, chan = lax.axis_index("slab"), lax.axis_index("chan")
    axial = slab * count_a + jnp.arange(count_a)
    lateral = chan * count_l + jnp.arange(count_l)
    last_a = lax.axis_size("slab") * count_a - 1
    last_l = lax.axis_size("chan") * count_l - 1
    half = lambda cond: jnp.where(cond, 0.5, 1.0).astype(f32)
    along_a = jnp.stack([half(axial > 0), jnp.ones(count_a, f32), half(axial < last_a)])
    along_l = jnp.stack([half(lateral > 0), jnp.ones(count_l, f32), half(lateral < last_l)])
    weights = along_a[:, None, None, :] * along_l[None, :, :, None]
    weights = weights.reshape(9, -1, LANES).transpose(1, 0, 2)
    return jnp.broadcast_to(weights[:, :, None, :], weights.shape[:2] + (8, LANES))


def on_device(
    stream_speed_field,
    liquid_to_solid_element,
    previous_panel_warmth,
    pointwise_energy_source,
    coked_element_flags,
    coking_thickness_plies,
):
    count_l, count_a = coked_element_flags.shape
    assert count_l == 2 and count_a % LANES == 0
    elements = count_l * count_a
    na = count_a // LANES
    tiles = count_l * na
    chan = lax.axis_size("chan")
    total = lax.axis_size("slab") * chan
    slab_at, chan_at = lax.axis_index("slab"), lax.axis_index("chan")
    me = (slab_at * chan + chan_at).astype(jnp.int32).reshape(1)
    position = [
        chan_at % 2,
        chan_at > 0,
        chan_at < chan - 1,
        slab_at > 0,
        slab_at < lax.axis_size("slab") - 1,
        slab_at % 2,
    ]
    position = jnp.stack([jnp.asarray(x, jnp.int32) for x in position])

    wt = jnp.asarray(np.broadcast_to(GLL_W[:, None], (8, LANES)), f32)
    wr = jnp.asarray(np.broadcast_to((GLL_W[:, None] * GLL_W)[:, :, None], (8, 8, LANES)), f32)
    kf, kb = (jnp.asarray(k) for k in line_matrices())
    kfluid = jnp.asarray(fluid_matrix())

    layers = coking_thickness_plies.astype(f32)
    flags = coked_element_flags.astype(f32)
    damping = jnp.where(coked_element_flags == 1, 1.0 / (1.0 + layer_damp * layers), jnp.ones_like(layers))
    cross = cross_gain * flags * layers / (layers + 1.0)
    dc = jnp.stack([damping.reshape(elements), cross.reshape(elements)])
    iw = product_weights(count_l, count_a)

    def as_rows(x):
        x = x.reshape(8, 8, 8, count_l, na, LANES).transpose(0, 1, 2, 4, 3, 5)
        return x.reshape(512 * tiles, LANES)

    field = (tiles, 8, 8, 8, LANES)
    whole = (tiles + 1, 8, 8, 8, LANES)
    shape = lambda s, d=f32: jax.ShapeDtypeStruct(s, d)
    kept = vmem
    split = elements // LANES
    width = LANES
    room = elements // 4
    in_hbm = lambda x: pltpu.with_memory_space_constraint(x, pltpu.HBM)
    here = lambda: pl.BlockSpec(memory_space=pltpu.VMEM)
    scalars = pl.BlockSpec(memory_space=pltpu.SMEM)
    steps = 4
    rows = 512 * tiles // steps
    z, a, b = pl.pallas_call(
        functools.partial(source_kernel, na, 8 // steps),
        grid=(steps,),
        in_specs=[scalars]
        + [pl.BlockSpec((rows, LANES), lambda i: (i, 0))] * 2
        + [pl.BlockSpec((8, 8, LANES), lambda i: (0, 0, 0))],
        out_specs=[here()] * 3,
        out_shape=[kept(field), kept((na, 8, 8, LANES)), kept((na, 8, 8, LANES))],
        compiler_params=pltpu.CompilerParams(vmem_limit_bytes=12 * 1024 * 1024),
    )(position, in_hbm(as_rows(previous_panel_warmth)), in_hbm(as_rows(pointwise_energy_source)), in_hbm(wr))
    a, b = swap(a, "chan", 0), swap(b, "chan", 1)

    velocity, z = lax.optimization_barrier((stream_speed_field, z))
    out = pl.pallas_call(
        functools.partial(fluid_kernel, chan, total),
        grid=(split,),
        in_specs=[
            scalars,
            pl.BlockSpec((3, 8, 8, 8, width), lambda i: (0, 0, 0, 0, i)),
            pl.BlockSpec((1, elements), lambda i: (0, 0)),
            pl.BlockSpec(kfluid.shape, lambda i: (0, 0)),
        ],
        out_specs=[pl.BlockSpec((3, 8, 8, 8, width), lambda i: (0, 0, 0, 0, i))] + [here()] * 4,
        out_shape=[shape(stream_speed_field.shape, bf16), kept((512, elements), bf16)]
        + [kept((528, room), bf16)] * 3,
        scratch_shapes=[pltpu.VMEM((split, 512, width), bf16), pltpu.VMEM((3, 8, 8, 8, width), f32)],
        compiler_params=pltpu.CompilerParams(vmem_limit_bytes=24 * 1024 * 1024),
    )(me, in_hbm(velocity), in_hbm(liquid_to_solid_element.reshape(1, elements)), in_hbm(kfluid))
    stepped, own, *outgoing = out
    received = [swap_around(outgoing[0], 0), swap_around(outgoing[1], 1), around(outgoing[2], chan)]
    z, z_behind, z_ahead = call(
        functools.partial(rim_kernel, na),
        [kept(field), kept((2 * RIM, 640)), kept((2 * RIM, 640))],
        position,
        z,
        a,
        b,
        dc,
        smem=1,
    )
    wk, a, b = call(
        functools.partial(unpack_kernel, na),
        [kept(field), kept((2 * RIM, 1152)), kept((2 * RIM, 1152))],
        position,
        own,
        *received,
        dc,
        wt,
        z_behind,
        z_ahead,
        smem=1,
    )
    a, b = slab_swap(a, 0), slab_swap(b, 1)

    basis, products = [], []
    face = (8 * na + 1, 8, LANES)
    for number in range(ITERS - 1):
        first = number == 0
        outs = [kept(whole)] * 4 + [kept(face)] * 2
        if first:
            args = (z, wk, a, b, dc)
            outs += [kept((8, 8, 8, LANES)), kept((tiles + 1, 8, LANES))]
        else:
            args = (y, a, b, wk, wkg, cr)
        got = call(
            functools.partial(flux_kernel, na, first),
            outs,
            position,
            *args,
            wt,
            kf,
            kb,
            smem=1,
            scratch=[pltpu.VMEM((2, 8, 8, 8, LANES), f32), pltpu.VMEM((8, 8, LANES), f32)],
            input_output_aliases={} if first else {1: 0},
        )
        if first:
            wkg, cr = got[6:]
        v, f1, f2, f3, a, b = got[:6]
        a, b = swap(a, "chan", 0), swap(b, "chan", 1)
        y, dots = call(
            functools.partial(rest_kernel, na, first),
            [kept(whole), kept((2, 8, LANES))],
            *basis[-1:],
            v,
            f1,
            f2,
            f3,
            wt,
            iw,
            kb,
            scratch=[pltpu.VMEM((8, 8, LANES), f32)],
        )
        basis.append(v)
        products.append(dots)
    v, sums = call(
        functools.partial(last_kernel, na),
        [kept(whole), kept((total, 1, LANES))],
        position,
        y,
        a,
        b,
        wk,
        cr,
        basis[-1],
        wt,
        iw,
        kf,
        *products,
        smem=1,
        input_output_aliases={1: 0},
        scratch=[pltpu.VMEM((2, 8, 8, 8, LANES), f32), pltpu.VMEM((8, 8, LANES), f32)],
    )
    basis.append(v)
    sums = lax.all_to_all(sums, ("slab", "chan"), 0, 0)
    x = pl.pallas_call(
        functools.partial(combine_kernel, na, 8 // steps),
        grid=(steps,),
        in_specs=[here()] * 6,
        out_specs=pl.BlockSpec((rows, LANES), lambda i: (i, 0)),
        out_shape=shape((512 * tiles, LANES)),
        scratch_shapes=[pltpu.VMEM((ITERS, 8, LANES), f32)],
        compiler_params=pltpu.CompilerParams(vmem_limit_bytes=12 * 1024 * 1024),
    )(sums, *basis)
    x = x.reshape(8, 8, 8, na, count_l, LANES).transpose(0, 1, 2, 4, 3, 5)
    return stepped, x.reshape(8, 8, 8, count_l, count_a)


def solution(mesh):
    in_specs = (
        P(None, None, None, None, ("slab", "chan")),
        P(("slab", "chan")),
        P(None, None, None, "chan", "slab"),
        P(None, None, None, "chan", "slab"),
        P("chan", "slab"),
        P("chan", "slab"),
    )
    out_specs = (P(None, None, None, None, ("slab", "chan")), P(None, None, None, "chan", "slab"))
    return jax.shard_map(
        on_device, mesh=mesh, in_specs=in_specs, out_specs=out_specs, check_vma=False
    )
```

```python
import functools

import jax
import jax.numpy as jnp
import numpy as np
from jax import lax
from jax.experimental import pallas as pl
from jax.experimental.pallas import tpu as pltpu
from jax.sharding import PartitionSpec as P

ITERS = 5
LANES = 128
RIM = 8
KRYLOV_SCALE = 1.0 / 256.0

highest = lax.Precision.HIGHEST
f32 = jnp.float32
bf16 = jnp.bfloat16
coolant_throughput = 0.05
time_step = 0.01
viscosity = 0.02
cross_gain = 0.4
layer_damp = 0.25

NT = (((1,), (1,)), ((), ()))
TN = (((0,), (0,)), ((), ()))


def gll_tables():
    points = np.array(
        [
            -1.0,
            -0.8717401485096066,
            -0.5917001814331423,
            -0.2092992179024789,
            0.2092992179024789,
            0.5917001814331423,
            0.8717401485096066,
            1.0,
        ]
    )
    weights = np.array(
        [
            1.0 / 28.0,
            0.2107042271435061,
            0.3411226924835044,
            0.4124587946587038,
            0.4124587946587038,
            0.3411226924835044,
            0.2107042271435061,
            1.0 / 28.0,
        ]
    )
    lower_poly = np.ones(8)
    upper_poly = points.copy()
    for degree in range(1, 7):
        next_poly = ((2 * degree + 1) * points * upper_poly - degree * lower_poly) / (degree + 1)
        lower_poly = upper_poly
        upper_poly = next_poly
    gaps_matrix = points[:, None] - points[None, :] + np.eye(8)
    derivative = upper_poly[:, None] / (upper_poly[None, :] * gaps_matrix)
    derivative = derivative * (1.0 - np.eye(8))
    derivative[0, 0] = -14.0
    derivative[7, 7] = 14.0
    return derivative, weights


DERIV, GLL_W = gll_tables()
DERIV = DERIV.astype(np.float32).astype(np.float64)
GLL_W = GLL_W.astype(np.float32).astype(np.float64)


def split_hi_lo(matrix):
    high = np.asarray(matrix, np.float32).astype(jnp.bfloat16)
    low = (np.asarray(matrix, np.float64) - high.astype(np.float64)).astype(np.float32)
    return high, low.astype(jnp.bfloat16)


def line_matrices():
    out = []
    for matrix in (DERIV, DERIV.T):
        high, low = split_hi_lo(np.kron(np.eye(16), matrix))
        upper = np.concatenate([high, high], 1)
        out.append(np.concatenate([upper, np.concatenate([low, np.zeros_like(low)], 1)], 0))
    return out


def fluid_matrix():
    eye8 = np.eye(8)
    square = DERIV @ DERIV
    second = time_step * np.kron(DERIV, eye8)
    third = time_step * np.kron(eye8, DERIV)
    curve = np.eye(64) + time_step * viscosity * (np.kron(square, eye8) + np.kron(eye8, square))
    return np.concatenate([np.concatenate(split_hi_lo(np.kron(np.eye(2), m)), 1) for m in (second, third, curve)], 0)


def halves_of(line):
    return [line[j] + line[7 - j] for j in range(4)], [line[j] - line[7 - j] for j in range(4)]


def combined(matrix, parts, sign):
    even, odd = parts
    result = [None] * 8
    for i in range(4):
        p = sum(float(0.5 * (matrix[i, j] + matrix[i, 7 - j])) * even[j] for j in range(4))
        q = sum(float(0.5 * (matrix[i, j] - matrix[i, 7 - j])) * odd[j] for j in range(4))
        result[i] = p + q
        result[7 - i] = q - p if sign < 0 else p - q
    return result


def along(matrix, line):
    return combined(matrix, halves_of(line), -1)


def lane_index(rows=8):
    return lax.broadcasted_iota(jnp.int32, (rows, LANES), 1)


def vmem(shape, dtype=f32):
    return pltpu.VMEM(shape, dtype)


def call(kernel, out_shape, *args, smem=0, scratch=(), limit=12, **kw):
    specs = [pl.BlockSpec(memory_space=pltpu.SMEM)] * smem
    specs += [pl.BlockSpec(memory_space=pltpu.VMEM)] * (len(args) - smem)
    outs = [pl.BlockSpec(memory_space=pltpu.VMEM) for _ in out_shape]
    return pl.pallas_call(
        kernel,
        in_specs=specs,
        out_specs=outs,
        out_shape=out_shape,
        scratch_shapes=scratch,
        compiler_params=pltpu.CompilerParams(vmem_limit_bytes=limit * 1024 * 1024),
        **kw,
    )(*args)


def weight_rows(wt):
    return [[float(GLL_W[r] * GLL_W[s]) * wt for s in range(8)] for r in range(8)]


def in_three(x):
    high = x.astype(bf16)
    rest = x - high.astype(f32)
    middle = rest.astype(bf16)
    return [high, middle, (rest - middle.astype(f32)).astype(bf16)]


def sel_matrix(l, first_lane):
    row = lax.broadcasted_iota(jnp.int32, (2 * RIM, LANES), 0)
    lane = lax.broadcasted_iota(jnp.int32, (2 * RIM, LANES), 1)
    inside = (row >= l * RIM) & (row < (l + 1) * RIM)
    return ((row - l * RIM + first_lane == lane) & inside).astype(f32).astype(bf16)


def place_matrix(first_lane):
    row = lax.broadcasted_iota(jnp.int32, (2 * RIM, LANES), 0)
    lane = lax.broadcasted_iota(jnp.int32, (2 * RIM, LANES), 1)
    target = jnp.where(row < RIM, row + first_lane, row - RIM + first_lane + LANES // 2)
    return (target == lane).astype(f32).astype(bf16)


def send_rims(tile_rows, na):
    def pick(tiles, first_lane):
        out = None
        for l, j in enumerate(tiles):
            terms = jnp.concatenate(in_three(tile_rows(j)), 1)
            sel = jnp.concatenate([sel_matrix(l, first_lane)] * 3, 1)
            part = lax.dot_general(sel, terms, NT, preferred_element_type=f32)
            out = part if out is None else out + part
        return out

    return pick((0, na), 0), pick((na - 1, 2 * na - 1), LANES - RIM)


def place_rims(from_ahead, from_behind):
    terms = jnp.concatenate(in_three(from_ahead) + in_three(from_behind), 0)
    places = jnp.concatenate([place_matrix(0)] * 3 + [place_matrix(LANES // 2 - RIM)] * 3, 0)
    return lax.dot_general(terms, places, TN, preferred_element_type=f32)


def source_planes(na, planes, par_ref, p_ref, q_ref, wr_ref, z_ref, a_ref, b_ref):
    step = 2 * na
    for n in range(planes):
        r = pl.program_id(0) * planes + n
        wr = wr_ref[r]
        ends = {}
        for s in range(8):
            base = (n * 8 + s) * 8 * step
            for l in range(2):
                for at in range(na):
                    pick = pl.ds(base + at * 2 + l, 8, stride=step)
                    value = (wr * float(GLL_W[s])) * (coolant_throughput * p_ref[pick, :] + q_ref[pick, :])
                    if (l, s) in ((0, 0), (0, 7), (1, 0), (1, 7)):
                        ends[l, s, at] = value
                    else:
                        z_ref[l * na + at, r, s] = value
        for at in range(na):
            shared = ends[0, 7, at] + ends[1, 0, at]
            z_ref[at, r, 7] = shared
            z_ref[na + at, r, 0] = shared
            lower, upper = ends[0, 0, at], ends[1, 7, at]
            z_ref[at, r, 0] = lower
            z_ref[na + at, r, 7] = upper
            send_faces(par_ref, (at, r), lower, upper, a_ref, b_ref)


def rim_kernel(na, par_ref, z_in, b_ref, a_ref, dc_ref, z_ref, behind_ref, ahead_ref):
    z_ref[...] = z_in[...]
    for r in range(8):
        for at in range(na):
            lower, upper = got_faces(par_ref, (at, r), a_ref, b_ref)
            z_ref[at, r, 0] = z_ref[at, r, 0] + lower
            z_ref[na + at, r, 7] = z_ref[na + at, r, 7] + upper

    def tile_rows(j):
        cross = jnp.broadcast_to(dc_ref[1:2, j * LANES : (j + 1) * LANES], (LANES, LANES))
        return jnp.concatenate([z_ref[j].reshape(512, LANES), cross], 0)

    behind_ref[...], ahead_ref[...] = send_rims(tile_rows, na)


def send_faces(par_ref, at, lower, upper, a_ref, b_ref):
    even = par_ref[0] == 0
    lower = jnp.where(par_ref[1] > 0, lower, 0.0)
    upper = jnp.where(par_ref[2] > 0, upper, 0.0)
    a_ref[at] = jnp.where(even, upper, lower)
    b_ref[at] = jnp.where(even, lower, upper)


def got_faces(par_ref, at, a_ref, b_ref):
    even = par_ref[0] == 0
    a, b = a_ref[at], b_ref[at]
    return jnp.where(even, b, a), jnp.where(even, a, b)


def axial_row(l, far, near):
    ghost = len(far) - 1
    lane = lane_index()
    half = LANES // 2
    roll = pltpu.roll
    right = [roll(x, 1, 1) for x in far]
    left = [roll(x, LANES - 1, 1) for x in near]
    new_far, new_near = [], []
    for at in range(ghost):
        if at > 0:
            carry = right[at - 1]
        else:
            carry = roll(far[ghost], half + 1, 1) if l == 0 else right[ghost]
        new_near.append(near[at] + jnp.where(lane == 0, carry, right[at]))
        if at < ghost - 1:
            carry = left[at + 1]
        else:
            carry = left[ghost] if l == 0 else roll(near[ghost], half - 1, 1)
        new_far.append(far[at] + jnp.where(lane == LANES - 1, carry, left[at]))
    carry = right[ghost - 1] if l == 0 else roll(far[ghost - 1], half + 1, 1)
    new_near.append(near[ghost] + jnp.where(lane == half * l, carry, right[ghost]))
    carry = roll(near[0], half - 1, 1) if l == 0 else left[0]
    new_far.append(far[ghost] + jnp.where(lane == half * (l + 1) - 1, carry, left[ghost]))
    return new_far, new_near


def assemble_axial(na, y):
    ghost = 2 * na
    low = lane_index() < LANES // 2
    for s in range(8):
        rims = []
        for l in range(2):
            tiles = list(range(l * na, l * na + na)) + [ghost]
            far, near = axial_row(l, [y[j, 7, s] for j in tiles], [y[j, 0, s] for j in tiles])
            for n, j in enumerate(tiles[:-1]):
                y[j, 7, s] = far[n]
                y[j, 0, s] = near[n]
            rims.append((far[-1], near[-1]))
        y[ghost, 7, s] = jnp.where(low, rims[0][0], rims[1][0])
        y[ghost, 0, s] = jnp.where(low, rims[0][1], rims[1][1])


def assemble_lateral(na, y):
    ghost = 2 * na
    half = LANES // 2
    low = lane_index() < half
    for r in range(8):
        for at in range(na):
            shared = y[at, r, 7] + y[na + at, r, 0]
            y[at, r, 7] = shared
            y[na + at, r, 0] = shared
        upper = y[ghost, r, 7]
        lower = y[ghost, r, 0]
        y[ghost, r, 7] = upper + jnp.where(low, pltpu.roll(lower, half, 1), 0.0)
        y[ghost, r, 0] = lower + jnp.where(low, 0.0, pltpu.roll(upper, half, 1))


def turn(x, by):
    return x if by % LANES == 0 else pltpu.roll(x, by % LANES, 1)


def pack_rim(planes, l):
    lane = lane_index()
    half = LANES // 2
    out = None
    for r, x in enumerate(planes):
        at = 2 * RIM * r
        near = turn(x, at - half * l)
        far = turn(x, at + RIM - (half * (l + 1) - RIM))
        near = jnp.where((lane >= at) & (lane < at + RIM), near, 0.0)
        both = jnp.where((lane >= at + RIM) & (lane < at + 2 * RIM), far, near)
        out = both if out is None else out + both
    return out


def unpack_rim(x, r, l):
    lane = lane_index()
    half = LANES // 2
    at = 2 * RIM * r
    near = turn(x, half * l - at)
    far = turn(x, half * (l + 1) - RIM - (at + RIM))
    near = jnp.where((lane >= half * l) & (lane < half * l + RIM), near, 0.0)
    return jnp.where((lane >= half * (l + 1) - RIM) & (lane < half * (l + 1)), far, near)


def add_faces(na, par_ref, v, a_ref, b_ref):
    ghost = 2 * na
    for at in range(na):
        for r in range(8):
            lower, upper = got_faces(par_ref, at * 8 + r, a_ref, b_ref)
            v[at, r, 0] = v[at, r, 0] + lower
            v[na + at, r, 7] = v[na + at, r, 7] + upper
    lower, upper = got_faces(par_ref, na * 8, a_ref, b_ref)
    for r in range(8):
        v[ghost, r, 0] = v[ghost, r, 0] + unpack_rim(lower, r, 0)
        v[ghost, r, 7] = v[ghost, r, 7] + unpack_rim(upper, r, 1)


def owners(l2s, me, total, chan):
    elements = l2s.shape[1]
    if elements & (elements - 1) == 0:
        owner = lax.shift_right_logical(l2s, elements.bit_length() - 1)
        slot = l2s & (elements - 1)
    else:
        owner = l2s // elements
        slot = l2s - owner * elements
    ahead = owner - me
    ahead = jnp.where(ahead < 0, ahead + total, ahead)
    group = jnp.where(ahead == 1, 1, jnp.where(ahead == total - 1, 2, jnp.where(ahead == chan, 3, 0)))
    return slot, group


def fluid_kernel(
    na, planes, chan, total, me_ref, par_ref, u_ref, l2s_ref, k_ref, p_ref, q_ref, wr_ref,
    out_ref, cond_ref, s1_ref, s2_ref, s3_ref, z_ref, fa_ref, fb_ref, t_ref, uf_ref
):
    i = pl.program_id(0)
    k = k_ref[...]
    curve_matrix = time_step * viscosity * (DERIV @ DERIV)
    slope_matrix = time_step * DERIV
    for c in range(3):
        for s in range(8):
            line = [u_ref[c, r, s].astype(f32) for r in range(8)]
            for r in range(8):
                uf_ref[c, r, s] = line[r]
            parts = halves_of(line)
            slope = combined(slope_matrix, parts, -1)
            curve = combined(curve_matrix, parts, 1)
            for r in range(8):
                t_ref[c, r, s] = curve[r] - uf_ref[0, r, s] * slope[r]
    for p in range(2):
        speed = [None] * 32
        for c in range(3):
            x = uf_ref[c, 4 * p : 4 * p + 4].reshape(2, 128, LANES)
            x = jnp.concatenate([x[0], x[1]], 1).astype(bf16)
            y = jnp.dot(k, jnp.concatenate([x, x], 0), preferred_element_type=f32)
            for h in range(2):
                part = y[:, h * LANES : (h + 1) * LANES].reshape(3, 2, 8, 8, LANES)
                for q in range(2):
                    r = 4 * p + 2 * h + q
                    for s in range(8):
                        change = t_ref[c, r, s] - uf_ref[1, r, s] * part[0, q, s] - uf_ref[2, r, s] * part[1, q, s]
                        new = (part[2, q, s] + change).astype(bf16)
                        out_ref[c, r, s] = new
                        new = new.astype(f32)
                        n = (2 * h + q) * 8 + s
                        speed[n] = new * new if speed[n] is None else speed[n] + new * new
        for n, value in enumerate(speed):
            t_ref[0, 4 * p + n // 8, n % 8] = 1.0 + 0.5 * value
    cond_ref[i] = t_ref[0].reshape(512, LANES).astype(bf16)
    source_planes(na, planes, par_ref, p_ref, q_ref, wr_ref, z_ref, fa_ref, fb_ref)

    @pl.when(i == pl.num_programs(0) - 1)
    def _():
        elements = l2s_ref.shape[-1]
        cond = jnp.concatenate([cond_ref[n] for n in range(cond_ref.shape[0])], 1)
        slot, group = owners(l2s_ref[...], me_ref[0], total, chan)
        kinds = lax.broadcasted_iota(jnp.int32, (16, elements), 0)
        marks = (kinds == group).astype(f32).astype(bf16)
        before = lax.broadcasted_iota(jnp.int32, (elements, elements), 0) < lax.broadcasted_iota(
            jnp.int32, (elements, elements), 1
        )
        rank = jnp.dot(marks, before.astype(f32).astype(bf16), preferred_element_type=f32).astype(jnp.int32)
        high = lax.shift_right_logical(slot, 5)
        codes = jnp.concatenate(
            [jnp.broadcast_to(high, (8, elements)), jnp.broadcast_to(slot - high * 32, (8, elements))], 0
        )
        tagged = jnp.concatenate([cond, codes.astype(f32).astype(bf16)], 0)
        room = s1_ref.shape[-1]
        position = lax.broadcasted_iota(jnp.int32, (room, elements), 0)
        even = me_ref[0] % 2 == 0
        one, two = rank[1:2], rank[2:3]
        sends = (
            (jnp.where(even, 1, 2), jnp.where(even, one, two), s1_ref),
            (jnp.where(even, 2, 1), jnp.where(even, two, one), s2_ref),
            (3, rank[3:4], s3_ref),
        )
        for g, order, ref in sends:
            take = ((position == order) & (group == g)).astype(f32).astype(bf16)
            ref[...] = lax.dot_general(tagged, take, NT, preferred_element_type=f32).astype(bf16)


def keep_kernel(chan, total, me_ref, cond_ref, l2s_ref, own_ref):
    elements = l2s_ref.shape[-1]
    cond = jnp.concatenate([cond_ref[n] for n in range(cond_ref.shape[0])], 1)
    slot, group = owners(l2s_ref[...], me_ref[0], total, chan)
    place = lax.broadcasted_iota(jnp.int32, (elements, elements), 0)
    keep = ((place == slot) & (group == 0)).astype(f32).astype(bf16)
    own_ref[...] = lax.dot_general(cond, keep, NT, preferred_element_type=f32).astype(bf16)


def unpack_kernel(
    na, par_ref, own_ref, r1_ref, r2_ref, r3_ref, dc_ref, wt_ref, zb_ref, za_ref, wk_ref, a_ref, b_ref
):
    rows = weight_rows(wt_ref[...] * KRYLOV_SCALE)
    got = jnp.concatenate([r[0:512] for r in (r1_ref, r2_ref, r3_ref)], 1)
    tags = [r[512:528].astype(f32) for r in (r1_ref, r2_ref, r3_ref)]
    slots = [(t[0:1] * 32.0 + t[8:9]).astype(jnp.int32) for t in tags]
    slot = jnp.concatenate(slots, 1)
    for j in range(2 * na):
        place = lax.broadcasted_iota(jnp.int32, (LANES, slot.shape[1]), 0) + j * LANES
        put = (place == slot).astype(f32).astype(bf16)
        cols = slice(j * LANES, (j + 1) * LANES)
        moved = own_ref[:, cols].astype(f32) + lax.dot_general(got, put, NT, preferred_element_type=f32)
        kappa = (moved * dc_ref[0:1, cols]).reshape(8, 8, 8, LANES)
        for r in range(8):
            for s in range(8):
                wk_ref[j, r, s] = rows[r][s] * kappa[r, s]
    behind, ahead = send_rims(lambda j: wk_ref[j].reshape(512, LANES), na)
    behind = jnp.where(par_ref[3] > 0, jnp.concatenate([zb_ref[...], behind], 1), 0.0)
    ahead = jnp.where(par_ref[4] > 0, jnp.concatenate([za_ref[...], ahead], 1), 0.0)
    even = par_ref[5] == 0
    a_ref[...] = jnp.where(even, ahead, behind)
    b_ref[...] = jnp.where(even, behind, ahead)


def lines_t(k_ref, blocks):
    out = []
    for p in range(0, len(blocks), 2):
        pair = jnp.concatenate(blocks[p : p + 2], 1)
        high = pair.astype(bf16)
        low = (pair - high.astype(f32)).astype(bf16)
        y = jnp.dot(k_ref[...], jnp.concatenate([high, low], 0), preferred_element_type=f32)
        y = y[:128] + y[128:]
        out += [y[:, n * LANES : (n + 1) * LANES].reshape(2, 8, 8, LANES) for n in range(len(blocks[p : p + 2]))]
    return out


def blocks_of(x):
    x = x.reshape(4, 128, LANES)
    return [x[n] for n in range(4)]


def squares(v, j, other, iw_ref):
    sums = {}
    for r in range(8):
        for s in range(8):
            key = (0 if r == 0 else 2 if r == 7 else 1, 0 if s == 0 else 2 if s == 7 else 1)
            x = v[j, r, s]
            pair = (x * x,) if other is None else (x * x, x * other[j, r, s])
            old = sums.get((key, r))
            sums[(key, r)] = pair if old is None else tuple(a + b for a, b in zip(old, pair))
    total = None
    for (key, _), pair in sums.items():
        weight = iw_ref[j, key[0] * 3 + key[1]]
        pair = tuple(weight * a for a in pair)
        total = pair if total is None else tuple(a + b for a, b in zip(total, pair))
    return total


def gradient_r(v, j, g):
    for s in range(8):
        for r, value in enumerate(along(DERIV, [v[j, r, s] for r in range(8)])):
            g[r, s] = value


def fluxes(v, j, wk, c, kf_ref, g, f1, f2, f3):
    for p, part in enumerate(lines_t(kf_ref, blocks_of(v[j]))):
        for q in range(2):
            f3[j, 2 * p + q] = wk(2 * p + q) * part[q]
    gradient_r(v, j, g)
    for r in range(8):
        second = along(DERIV, [v[j, r, s] for s in range(8)])
        k = wk(r)
        for s in range(8):
            first = g[r, s]
            f2[j, r, s] = k[s] * (second[s] + c * first)
            f1[j, r, s] = k[s] * (first + c * second[s])


def lateral_faces(na, par_ref, v, f1, f2, f3, base, kb_ref, a_ref, b_ref):
    rows = [[(l * na + at, 7 * l) for at in range(na)] + [(2 * na, 7 * l)] for l in range(2)]
    flat = rows[0] + rows[1]
    blocks = []
    for n in range(0, len(flat), 2):
        pair = [f3[j, :, s].reshape(64, LANES) for j, s in flat[n : n + 2]]
        blocks.append(jnp.concatenate(pair, 0))
    thirds = []
    for part in lines_t(kb_ref, blocks):
        part = part.reshape(2, 8, 8, LANES)
        thirds += [part[0], part[1]]
    faces = []
    for (j, s), third in zip(flat, thirds):
        first = along(DERIV.T, [f1[j, r, s] for r in range(8)])
        face = []
        for r in range(8):
            second = sum(float(DERIV[i, s]) * f2[j, r, i] for i in range(8) if DERIV[i, s] != 0.0)
            face.append(second + (base[r] * float(GLL_W[s])) * v[j, r, s] + first[r] + third[r])
        faces.append(face)
    for l in range(2):
        row = faces[l * (na + 1) : (l + 1) * (na + 1)]
        far, near = axial_row(l, [x[7] for x in row], [x[0] for x in row])
        for x, last, start in zip(row, far, near):
            x[7], x[0] = last, start
    for at in range(na):
        for r in range(8):
            send_faces(par_ref, at * 8 + r, faces[at][r], faces[na + 1 + at][r], a_ref, b_ref)
    send_faces(par_ref, na * 8, pack_rim(faces[na], 0), pack_rim(faces[2 * na + 1], 1), a_ref, b_ref)


def mass_rows(wt, base):
    for r in range(8):
        base[r] = wt * float(GLL_W[r] * coolant_throughput * KRYLOV_SCALE)


def flux_kernel(na, first, *refs):
    refs = list(refs)
    take = lambda n: [refs.pop(0) for _ in range(n)]
    ghost = 2 * na
    if first:
        par_ref, z_in, wk_ref, b_in, a_in, dc_ref = take(6)
    else:
        par_ref, _, b_in, a_in, wk_ref, wkg_ref, cr_ref = take(7)
    wt_ref, kf_ref, kb_ref, v, f1, f2, f3, a_out, b_out = take(9)
    if first:
        wkg_ref, cr_ref = take(2)
    g, base = refs
    if first:
        v[0:ghost] = z_in[...]
        even = par_ref[5] == 0
        a, b = a_in[...], b_in[...]
        rims = place_rims(jnp.where(even, a, b), jnp.where(even, b, a))
        v[ghost] = rims[0:512].reshape(8, 8, 8, LANES)
        wkg_ref[...] = rims[640:1152].reshape(8, 8, 8, LANES)
        for j in range(ghost):
            cr_ref[j] = jnp.broadcast_to(dc_ref[1:2, j * LANES : (j + 1) * LANES], (8, LANES))
        cr_ref[ghost] = rims[512:520]
        assemble_axial(na, v)
    else:
        add_faces(na, par_ref, v, a_in, b_in)
    mass_rows(wt_ref[...], base)
    for j in range(ghost + 1):
        if j < ghost:
            wk = lambda r: wk_ref[j, r]
        else:
            wk = lambda r: wkg_ref[r]
        fluxes(v, j, wk, cr_ref[j], kf_ref, g.at[j % 2], f1, f2, f3)
    lateral_faces(na, par_ref, v, f1, f2, f3, base, kb_ref, a_out, b_out)


def rest_kernel(na, first, *refs):
    refs = list(refs)
    prev = None if first else refs.pop(0)
    v, f1, f2, f3, wt_ref, iw_ref, kb_ref, y, dots, base = refs
    ghost = 2 * na
    mass_rows(wt_ref[...], base)
    totals = None
    for j in range(ghost + 1):
        if j < ghost:
            sums = squares(v, j, prev, iw_ref)
            totals = sums if totals is None else [a + b for a, b in zip(totals, sums)]
        parts = lines_t(kb_ref, blocks_of(f3[j]))
        for r in range(8):
            for s, value in enumerate(along(DERIV.T, [f2[j, r, s] for s in range(8)])):
                y[j, r, s] = value + (base[r] * float(GLL_W[s])) * v[j, r, s]
        for s in range(8):
            for r, value in enumerate(along(DERIV.T, [f1[j, r, s] for r in range(8)])):
                y[j, r, s] = y[j, r, s] + value + parts[r // 2][r % 2, s]
    for k, value in enumerate(totals):
        dots[k] = value
    assemble_axial(na, y)
    assemble_lateral(na, y)


def last_kernel(na, par_ref, _, b_in, a_in, wk_ref, cr_ref, prev, wt_ref, iw_ref, kf_ref, d0, d1, d2, d3, v, all_dots, g, base):
    ghost = 2 * na
    add_faces(na, par_ref, v, a_in, b_in)
    mass_rows(wt_ref[...], base)
    totals = None
    for j in range(ghost):
        gj = g.at[j % 2]
        third = lines_t(kf_ref, blocks_of(v[j]))
        sums = list(squares(v, j, prev, iw_ref))
        gradient_r(v, j, gj)
        c = 2.0 * cr_ref[j]
        total = None
        for r in range(8):
            line = [v[j, r, s] for s in range(8)]
            second = along(DERIV, line)
            row = None
            for s in range(8):
                one, two, three = gj[r, s], second[s], third[r // 2][r % 2, s]
                term = (base[r] * float(GLL_W[s])) * (line[s] * line[s])
                term = term + wk_ref[j, r, s] * (one * (one + c * two) + two * two + three * three)
                row = term if row is None else row + term
            total = row if total is None else total + row
        sums.append(total)
        totals = sums if totals is None else [a + b for a, b in zip(totals, sums)]
    lane = lane_index(1)
    rows = [d0[0], d1[1], d1[0], d2[1], d2[0], d3[1], d3[0], totals[1], totals[0], totals[2]]
    out = jnp.zeros((1, LANES), f32)
    for k, row in enumerate(rows):
        out = jnp.where(lane == k, jnp.sum(jnp.sum(row, 0, keepdims=True), 1, keepdims=True), out)
    all_dots[...] = jnp.broadcast_to(out[None], all_dots.shape)


def solve_moments(m_ref, coef_ref):
    sums = jnp.sum(m_ref[:, 0, :], 0, keepdims=True)
    lane = lane_index(1)
    m = [jnp.sum(jnp.where(lane == k, sums, 0.0), 1, keepdims=True) for k in range(2 * ITERS)]
    n = ITERS
    low = [[None] * n for _ in range(n)]
    diag = [None] * n
    for j in range(n):
        acc = [m[i + j + 1] for i in range(n)]
        for k in range(j):
            scaled = low[j][k] * diag[k]
            for i in range(j, n):
                acc[i] = acc[i] - low[i][k] * scaled
        diag[j] = acc[j]
        for i in range(j + 1, n):
            low[i][j] = acc[i] / acc[j]
    z = []
    for i in range(n):
        value = m[i]
        for k in range(i):
            value = value - low[i][k] * z[k]
        z.append(value)
    c = [z[i] / diag[i] for i in range(n)]
    for i in reversed(range(n)):
        for k in range(i + 1, n):
            c[i] = c[i] - low[k][i] * c[k]
    for k, x in enumerate(c):
        coef_ref[k] = jnp.broadcast_to(x * KRYLOV_SCALE, (8, LANES))


def combine_kernel(na, planes, m_ref, v0, v1, v2, v3, v4, out_ref, coef_ref):
    i = pl.program_id(0)

    @pl.when(i == 0)
    def _():
        solve_moments(m_ref, coef_ref)

    c = [coef_ref[k] for k in range(ITERS)]
    step = 2 * na
    for n in range(planes):
        r = i * planes + n
        for s in range(8):
            base = (n * 8 + s) * 8 * step
            for l in range(2):
                for at in range(na):
                    x = None
                    for coef, v in zip(c, (v0, v1, v2, v3, v4)):
                        term = coef * v[l * na + at, r, s]
                        x = term if x is None else x + term
                    out_ref[pl.ds(base + at * 2 + l, 8, stride=step), :] = x


def slab_swap(x, start):
    n, m = lax.axis_size("slab"), lax.axis_size("chan")
    pairs = [(i * m + c, (i + 1) * m + c) for i in range(start, n - 1, 2) for c in range(m)]
    busy = {i for pair in pairs for i in pair}
    pairs += [(i, i + 1) for i in range(0, n * m, 2) if i not in busy]
    return lax.ppermute(x, ("slab", "chan"), pairs + [(j, i) for i, j in pairs])


def swap(x, axis, start):
    n = lax.axis_size(axis)
    pairs = [((start + i) % n, (start + i + 1) % n) for i in range(0, n, 2)]
    return lax.ppermute(x, axis, pairs + [(j, i) for i, j in pairs])


def around(x, by):
    n = lax.axis_size("slab") * lax.axis_size("chan")
    return lax.ppermute(x, ("slab", "chan"), [(i, (i + by) % n) for i in range(n)])


def swap_around(x, start):
    n = lax.axis_size("slab") * lax.axis_size("chan")
    pairs = [((start + i) % n, (start + i + 1) % n) for i in range(0, n, 2)]
    return lax.ppermute(x, ("slab", "chan"), pairs + [(j, i) for i, j in pairs])


def product_weights(count_l, count_a):
    slab, chan = lax.axis_index("slab"), lax.axis_index("chan")
    axial = slab * count_a + jnp.arange(count_a)
    lateral = chan * count_l + jnp.arange(count_l)
    last_a = lax.axis_size("slab") * count_a - 1
    last_l = lax.axis_size("chan") * count_l - 1
    half = lambda cond: jnp.where(cond, 0.5, 1.0).astype(f32)
    along_a = jnp.stack([half(axial > 0), jnp.ones(count_a, f32), half(axial < last_a)])
    along_l = jnp.stack([half(lateral > 0), jnp.ones(count_l, f32), half(lateral < last_l)])
    weights = along_a[:, None, None, :] * along_l[None, :, :, None]
    weights = weights.reshape(9, -1, LANES).transpose(1, 0, 2)
    return jnp.broadcast_to(weights[:, :, None, :], weights.shape[:2] + (8, LANES))


def on_device(
    stream_speed_field,
    liquid_to_solid_element,
    previous_panel_warmth,
    pointwise_energy_source,
    coked_element_flags,
    coking_thickness_plies,
):
    count_l, count_a = coked_element_flags.shape
    assert count_l == 2 and count_a % LANES == 0
    elements = count_l * count_a
    na = count_a // LANES
    tiles = count_l * na
    chan = lax.axis_size("chan")
    total = lax.axis_size("slab") * chan
    slab_at, chan_at = lax.axis_index("slab"), lax.axis_index("chan")
    me = (slab_at * chan + chan_at).astype(jnp.int32).reshape(1)
    position = [
        chan_at % 2,
        chan_at > 0,
        chan_at < chan - 1,
        slab_at > 0,
        slab_at < lax.axis_size("slab") - 1,
        slab_at % 2,
    ]
    position = jnp.stack([jnp.asarray(x, jnp.int32) for x in position])

    wt = jnp.asarray(np.broadcast_to(GLL_W[:, None], (8, LANES)), f32)
    wr = jnp.asarray(np.broadcast_to((GLL_W[:, None] * GLL_W)[:, :, None], (8, 8, LANES)), f32)
    kf, kb = (jnp.asarray(k) for k in line_matrices())
    kfluid = jnp.asarray(fluid_matrix())

    layers = coking_thickness_plies.astype(f32)
    flags = coked_element_flags.astype(f32)
    damping = jnp.where(coked_element_flags == 1, 1.0 / (1.0 + layer_damp * layers), jnp.ones_like(layers))
    cross = cross_gain * flags * layers / (layers + 1.0)
    dc = jnp.stack([damping.reshape(elements), cross.reshape(elements)])
    iw = product_weights(count_l, count_a)

    def as_rows(x):
        x = x.reshape(8, 8, 8, count_l, na, LANES).transpose(0, 1, 2, 4, 3, 5)
        return x.reshape(512 * tiles, LANES)

    field = (tiles, 8, 8, 8, LANES)
    whole = (tiles + 1, 8, 8, 8, LANES)
    shape = lambda s, d=f32: jax.ShapeDtypeStruct(s, d)
    kept = vmem
    split = elements // LANES
    width = LANES
    room = elements // 4
    in_hbm = lambda x: pltpu.with_memory_space_constraint(x, pltpu.HBM)
    here = lambda: pl.BlockSpec(memory_space=pltpu.VMEM)
    scalars = pl.BlockSpec(memory_space=pltpu.SMEM)
    steps = 4
    rows = 512 * tiles // steps
    l2s = liquid_to_solid_element.reshape(1, elements)
    out = pl.pallas_call(
        functools.partial(fluid_kernel, na, 8 // split, chan, total),
        grid=(split,),
        in_specs=[
            scalars,
            scalars,
            pl.BlockSpec((3, 8, 8, 8, width), lambda i: (0, 0, 0, 0, i)),
            pl.BlockSpec((1, elements), lambda i: (0, 0)),
            pl.BlockSpec(kfluid.shape, lambda i: (0, 0)),
        ]
        + [pl.BlockSpec((512 * tiles // split, LANES), lambda i: (i, 0))] * 2
        + [pl.BlockSpec((8, 8, LANES), lambda i: (0, 0, 0))],
        out_specs=[pl.BlockSpec((3, 8, 8, 8, width), lambda i: (0, 0, 0, 0, i))] + [here()] * 7,
        out_shape=[shape(stream_speed_field.shape, bf16), kept((split, 512, width), bf16)]
        + [kept((528, room), bf16)] * 3
        + [kept(field), kept((na, 8, 8, LANES)), kept((na, 8, 8, LANES))],
        scratch_shapes=[pltpu.VMEM((3, 8, 8, 8, width), f32)] * 2,
        compiler_params=pltpu.CompilerParams(vmem_limit_bytes=24 * 1024 * 1024),
    )(
        me,
        position,
        in_hbm(stream_speed_field),
        in_hbm(l2s),
        in_hbm(kfluid),
        in_hbm(as_rows(previous_panel_warmth)),
        in_hbm(as_rows(pointwise_energy_source)),
        in_hbm(wr),
    )
    stepped, cond, out_even, out_odd, out_far, z, a, b = out
    received = [around(out_far, chan), swap_around(out_odd, 1), swap_around(out_even, 0)]
    (own,) = call(
        functools.partial(keep_kernel, chan, total), [kept((512, elements), bf16)], me, cond, l2s, smem=1
    )
    a, b, own = lax.optimization_barrier((a, b, own))
    b, a = swap(b, "chan", 1), swap(a, "chan", 0)
    z, z_behind, z_ahead = call(
        functools.partial(rim_kernel, na),
        [kept(field), kept((2 * RIM, 640)), kept((2 * RIM, 640))],
        position,
        z,
        b,
        a,
        dc,
        smem=1,
    )
    wk, a, b = call(
        functools.partial(unpack_kernel, na),
        [kept(field), kept((2 * RIM, 1152)), kept((2 * RIM, 1152))],
        position,
        own,
        *received,
        dc,
        wt,
        z_behind,
        z_ahead,
        smem=1,
    )
    b, a = slab_swap(b, 1), slab_swap(a, 0)

    basis, products = [], []
    face = (8 * na + 1, 8, LANES)
    for number in range(ITERS - 1):
        first = number == 0
        outs = [kept(whole)] * 4 + [kept(face)] * 2
        if first:
            args = (z, wk, b, a, dc)
            outs += [kept((8, 8, 8, LANES)), kept((tiles + 1, 8, LANES))]
        else:
            args = (y, b, a, wk, wkg, cr)
        got = call(
            functools.partial(flux_kernel, na, first),
            outs,
            position,
            *args,
            wt,
            kf,
            kb,
            smem=1,
            scratch=[pltpu.VMEM((2, 8, 8, 8, LANES), f32), pltpu.VMEM((8, 8, LANES), f32)],
            input_output_aliases={} if first else {1: 0},
        )
        if first:
            wkg, cr = got[6:]
        v, f1, f2, f3, a, b = got[:6]
        b, a = swap(b, "chan", 1), swap(a, "chan", 0)
        y, dots = call(
            functools.partial(rest_kernel, na, first),
            [kept(whole), kept((2, 8, LANES))],
            *basis[-1:],
            v,
            f1,
            f2,
            f3,
            wt,
            iw,
            kb,
            scratch=[pltpu.VMEM((8, 8, LANES), f32)],
        )
        basis.append(v)
        products.append(dots)
    v, sums = call(
        functools.partial(last_kernel, na),
        [kept(whole), kept((total, 1, LANES))],
        position,
        y,
        b,
        a,
        wk,
        cr,
        basis[-1],
        wt,
        iw,
        kf,
        *products,
        smem=1,
        input_output_aliases={1: 0},
        scratch=[pltpu.VMEM((2, 8, 8, 8, LANES), f32), pltpu.VMEM((8, 8, LANES), f32)],
    )
    basis.append(v)
    sums = lax.all_to_all(sums, ("slab", "chan"), 0, 0)
    x = pl.pallas_call(
        functools.partial(combine_kernel, na, 8 // steps),
        grid=(steps,),
        in_specs=[here()] * 6,
        out_specs=pl.BlockSpec((rows, LANES), lambda i: (i, 0)),
        out_shape=shape((512 * tiles, LANES)),
        scratch_shapes=[pltpu.VMEM((ITERS, 8, LANES), f32)],
        compiler_params=pltpu.CompilerParams(vmem_limit_bytes=12 * 1024 * 1024),
    )(sums, *basis)
    x = x.reshape(8, 8, 8, na, count_l, LANES).transpose(0, 1, 2, 4, 3, 5)
    return stepped, x.reshape(8, 8, 8, count_l, count_a)


def solution(mesh):
    in_specs = (
        P(None, None, None, None, ("slab", "chan")),
        P(("slab", "chan")),
        P(None, None, None, "chan", "slab"),
        P(None, None, None, "chan", "slab"),
        P("chan", "slab"),
        P("chan", "slab"),
    )
    out_specs = (P(None, None, None, None, ("slab", "chan")), P(None, None, None, "chan", "slab"))
    return jax.shard_map(
        on_device, mesh=mesh, in_specs=in_specs, out_specs=out_specs, check_vma=False
    )
```

```python
import functools

import jax
import jax.numpy as jnp
import numpy as np
from jax import lax
from jax.experimental import pallas as pl
from jax.experimental.pallas import tpu as pltpu
from jax.sharding import PartitionSpec as P

ITERS = 5
LANES = 128
RIM = 8
KRYLOV_SCALE = 1.0 / 256.0

highest = lax.Precision.HIGHEST
f32 = jnp.float32
bf16 = jnp.bfloat16
coolant_throughput = 0.05
time_step = 0.01
viscosity = 0.02
cross_gain = 0.4
layer_damp = 0.25

NT = (((1,), (1,)), ((), ()))
TN = (((0,), (0,)), ((), ()))


def gll_tables():
    points = np.array(
        [
            -1.0,
            -0.8717401485096066,
            -0.5917001814331423,
            -0.2092992179024789,
            0.2092992179024789,
            0.5917001814331423,
            0.8717401485096066,
            1.0,
        ]
    )
    weights = np.array(
        [
            1.0 / 28.0,
            0.2107042271435061,
            0.3411226924835044,
            0.4124587946587038,
            0.4124587946587038,
            0.3411226924835044,
            0.2107042271435061,
            1.0 / 28.0,
        ]
    )
    lower_poly = np.ones(8)
    upper_poly = points.copy()
    for degree in range(1, 7):
        next_poly = ((2 * degree + 1) * points * upper_poly - degree * lower_poly) / (degree + 1)
        lower_poly = upper_poly
        upper_poly = next_poly
    gaps_matrix = points[:, None] - points[None, :] + np.eye(8)
    derivative = upper_poly[:, None] / (upper_poly[None, :] * gaps_matrix)
    derivative = derivative * (1.0 - np.eye(8))
    derivative[0, 0] = -14.0
    derivative[7, 7] = 14.0
    return derivative, weights


DERIV, GLL_W = gll_tables()
DERIV = DERIV.astype(np.float32).astype(np.float64)
GLL_W = GLL_W.astype(np.float32).astype(np.float64)


def split_hi_lo(matrix):
    high = np.asarray(matrix, np.float32).astype(jnp.bfloat16)
    low = (np.asarray(matrix, np.float64) - high.astype(np.float64)).astype(np.float32)
    return high, low.astype(jnp.bfloat16)


def line_matrices():
    out = []
    for matrix in (DERIV, DERIV.T):
        high, low = split_hi_lo(np.kron(np.eye(16), matrix))
        upper = np.concatenate([high, high], 1)
        out.append(np.concatenate([upper, np.concatenate([low, np.zeros_like(low)], 1)], 0))
    return out


def fluid_matrix():
    eye8 = np.eye(8)
    square = DERIV @ DERIV
    second = time_step * np.kron(DERIV, eye8)
    third = time_step * np.kron(eye8, DERIV)
    curve = np.eye(64) + time_step * viscosity * (np.kron(square, eye8) + np.kron(eye8, square))
    return np.concatenate([np.concatenate(split_hi_lo(np.kron(np.eye(2), m)), 1) for m in (second, third, curve)], 0)


def halves_of(line):
    return [line[j] + line[7 - j] for j in range(4)], [line[j] - line[7 - j] for j in range(4)]


def combined(matrix, parts, sign):
    even, odd = parts
    result = [None] * 8
    for i in range(4):
        p = sum(float(0.5 * (matrix[i, j] + matrix[i, 7 - j])) * even[j] for j in range(4))
        q = sum(float(0.5 * (matrix[i, j] - matrix[i, 7 - j])) * odd[j] for j in range(4))
        result[i] = p + q
        result[7 - i] = q - p if sign < 0 else p - q
    return result


def along(matrix, line):
    return combined(matrix, halves_of(line), -1)


def lane_index(rows=8):
    return lax.broadcasted_iota(jnp.int32, (rows, LANES), 1)


def vmem(shape, dtype=f32):
    return pltpu.VMEM(shape, dtype)


def call(kernel, out_shape, *args, smem=0, scratch=(), limit=12, **kw):
    specs = [pl.BlockSpec(memory_space=pltpu.SMEM)] * smem
    specs += [pl.BlockSpec(memory_space=pltpu.VMEM)] * (len(args) - smem)
    outs = [pl.BlockSpec(memory_space=pltpu.VMEM) for _ in out_shape]
    return pl.pallas_call(
        kernel,
        in_specs=specs,
        out_specs=outs,
        out_shape=out_shape,
        scratch_shapes=scratch,
        compiler_params=pltpu.CompilerParams(vmem_limit_bytes=limit * 1024 * 1024),
        **kw,
    )(*args)


def weight_rows(wt):
    return [[float(GLL_W[r] * GLL_W[s]) * wt for s in range(8)] for r in range(8)]


def in_three(x):
    high = x.astype(bf16)
    rest = x - high.astype(f32)
    middle = rest.astype(bf16)
    return [high, middle, (rest - middle.astype(f32)).astype(bf16)]


def sel_matrix(l, first_lane):
    row = lax.broadcasted_iota(jnp.int32, (2 * RIM, LANES), 0)
    lane = lax.broadcasted_iota(jnp.int32, (2 * RIM, LANES), 1)
    inside = (row >= l * RIM) & (row < (l + 1) * RIM)
    return ((row - l * RIM + first_lane == lane) & inside).astype(f32).astype(bf16)


def place_matrix(first_lane):
    row = lax.broadcasted_iota(jnp.int32, (2 * RIM, LANES), 0)
    lane = lax.broadcasted_iota(jnp.int32, (2 * RIM, LANES), 1)
    target = jnp.where(row < RIM, row + first_lane, row - RIM + first_lane + LANES // 2)
    return (target == lane).astype(f32).astype(bf16)


def send_rims(tile_rows, na):
    def pick(tiles, first_lane):
        out = None
        for l, j in enumerate(tiles):
            terms = jnp.concatenate(in_three(tile_rows(j)), 1)
            sel = jnp.concatenate([sel_matrix(l, first_lane)] * 3, 1)
            part = lax.dot_general(sel, terms, NT, preferred_element_type=f32)
            out = part if out is None else out + part
        return out

    return pick((0, na), 0), pick((na - 1, 2 * na - 1), LANES - RIM)


def place_rims(from_ahead, from_behind):
    terms = jnp.concatenate(in_three(from_ahead) + in_three(from_behind), 0)
    places = jnp.concatenate([place_matrix(0)] * 3 + [place_matrix(LANES // 2 - RIM)] * 3, 0)
    return lax.dot_general(terms, places, TN, preferred_element_type=f32)


def source_planes(na, planes, par_ref, p_ref, q_ref, wr_ref, z_ref, a_ref, b_ref):
    step = 2 * na
    for n in range(planes):
        r = pl.program_id(0) * planes + n
        wr = wr_ref[r]
        ends = {}
        for s in range(8):
            base = (n * 8 + s) * 8 * step
            for l in range(2):
                for at in range(na):
                    pick = pl.ds(base + at * 2 + l, 8, stride=step)
                    value = (wr * float(GLL_W[s])) * (coolant_throughput * p_ref[pick, :] + q_ref[pick, :])
                    if (l, s) in ((0, 0), (0, 7), (1, 0), (1, 7)):
                        ends[l, s, at] = value
                    else:
                        z_ref[l * na + at, r, s] = value
        for at in range(na):
            shared = ends[0, 7, at] + ends[1, 0, at]
            z_ref[at, r, 7] = shared
            z_ref[na + at, r, 0] = shared
            lower, upper = ends[0, 0, at], ends[1, 7, at]
            z_ref[at, r, 0] = lower
            z_ref[na + at, r, 7] = upper
            send_faces(par_ref, (at, r), lower, upper, a_ref, b_ref)


def rim_kernel(na, par_ref, z_in, b_ref, a_ref, dc_ref, wkb_ref, wka_ref, z_ref, a_out, b_out):
    z_ref[...] = z_in[...]
    for r in range(8):
        for at in range(na):
            lower, upper = got_faces(par_ref, (at, r), a_ref, b_ref)
            z_ref[at, r, 0] = z_ref[at, r, 0] + lower
            z_ref[na + at, r, 7] = z_ref[na + at, r, 7] + upper

    def tile_rows(j):
        cross = jnp.broadcast_to(dc_ref[1:2, j * LANES : (j + 1) * LANES], (LANES, LANES))
        return jnp.concatenate([z_ref[j].reshape(512, LANES), cross], 0)

    behind, ahead = send_rims(tile_rows, na)
    behind = jnp.where(par_ref[3] > 0, jnp.concatenate([behind, wkb_ref[...]], 1), 0.0)
    ahead = jnp.where(par_ref[4] > 0, jnp.concatenate([ahead, wka_ref[...]], 1), 0.0)
    even = par_ref[5] == 0
    a_out[...] = jnp.where(even, ahead, behind)
    b_out[...] = jnp.where(even, behind, ahead)


def send_faces(par_ref, at, lower, upper, a_ref, b_ref):
    even = par_ref[0] == 0
    lower = jnp.where(par_ref[1] > 0, lower, 0.0)
    upper = jnp.where(par_ref[2] > 0, upper, 0.0)
    a_ref[at] = jnp.where(even, upper, lower)
    b_ref[at] = jnp.where(even, lower, upper)


def got_faces(par_ref, at, a_ref, b_ref):
    even = par_ref[0] == 0
    a, b = a_ref[at], b_ref[at]
    return jnp.where(even, b, a), jnp.where(even, a, b)


def axial_row(l, far, near):
    ghost = len(far) - 1
    lane = lane_index()
    half = LANES // 2
    roll = pltpu.roll
    right = [roll(x, 1, 1) for x in far]
    left = [roll(x, LANES - 1, 1) for x in near]
    new_far, new_near = [], []
    for at in range(ghost):
        if at > 0:
            carry = right[at - 1]
        else:
            carry = roll(far[ghost], half + 1, 1) if l == 0 else right[ghost]
        new_near.append(near[at] + jnp.where(lane == 0, carry, right[at]))
        if at < ghost - 1:
            carry = left[at + 1]
        else:
            carry = left[ghost] if l == 0 else roll(near[ghost], half - 1, 1)
        new_far.append(far[at] + jnp.where(lane == LANES - 1, carry, left[at]))
    carry = right[ghost - 1] if l == 0 else roll(far[ghost - 1], half + 1, 1)
    new_near.append(near[ghost] + jnp.where(lane == half * l, carry, right[ghost]))
    carry = roll(near[0], half - 1, 1) if l == 0 else left[0]
    new_far.append(far[ghost] + jnp.where(lane == half * (l + 1) - 1, carry, left[ghost]))
    return new_far, new_near


def assemble_axial(na, y):
    ghost = 2 * na
    low = lane_index() < LANES // 2
    for s in range(8):
        rims = []
        for l in range(2):
            tiles = list(range(l * na, l * na + na)) + [ghost]
            far, near = axial_row(l, [y[j, 7, s] for j in tiles], [y[j, 0, s] for j in tiles])
            for n, j in enumerate(tiles[:-1]):
                y[j, 7, s] = far[n]
                y[j, 0, s] = near[n]
            rims.append((far[-1], near[-1]))
        y[ghost, 7, s] = jnp.where(low, rims[0][0], rims[1][0])
        y[ghost, 0, s] = jnp.where(low, rims[0][1], rims[1][1])


def assemble_lateral(na, y):
    ghost = 2 * na
    half = LANES // 2
    low = lane_index() < half
    for r in range(8):
        for at in range(na):
            shared = y[at, r, 7] + y[na + at, r, 0]
            y[at, r, 7] = shared
            y[na + at, r, 0] = shared
        upper = y[ghost, r, 7]
        lower = y[ghost, r, 0]
        y[ghost, r, 7] = upper + jnp.where(low, pltpu.roll(lower, half, 1), 0.0)
        y[ghost, r, 0] = lower + jnp.where(low, 0.0, pltpu.roll(upper, half, 1))


def turn(x, by):
    return x if by % LANES == 0 else pltpu.roll(x, by % LANES, 1)


def pack_rim(planes, l):
    lane = lane_index()
    half = LANES // 2
    out = None
    for r, x in enumerate(planes):
        at = 2 * RIM * r
        near = turn(x, at - half * l)
        far = turn(x, at + RIM - (half * (l + 1) - RIM))
        near = jnp.where((lane >= at) & (lane < at + RIM), near, 0.0)
        both = jnp.where((lane >= at + RIM) & (lane < at + 2 * RIM), far, near)
        out = both if out is None else out + both
    return out


def unpack_rim(x, r, l):
    lane = lane_index()
    half = LANES // 2
    at = 2 * RIM * r
    near = turn(x, half * l - at)
    far = turn(x, half * (l + 1) - RIM - (at + RIM))
    near = jnp.where((lane >= half * l) & (lane < half * l + RIM), near, 0.0)
    return jnp.where((lane >= half * (l + 1) - RIM) & (lane < half * (l + 1)), far, near)


def add_faces(na, par_ref, v, a_ref, b_ref):
    ghost = 2 * na
    for at in range(na):
        for r in range(8):
            lower, upper = got_faces(par_ref, at * 8 + r, a_ref, b_ref)
            v[at, r, 0] = v[at, r, 0] + lower
            v[na + at, r, 7] = v[na + at, r, 7] + upper
    lower, upper = got_faces(par_ref, na * 8, a_ref, b_ref)
    for r in range(8):
        v[ghost, r, 0] = v[ghost, r, 0] + unpack_rim(lower, r, 0)
        v[ghost, r, 7] = v[ghost, r, 7] + unpack_rim(upper, r, 1)


def owners(l2s, me, total, chan):
    elements = l2s.shape[1]
    if elements & (elements - 1) == 0:
        owner = lax.shift_right_logical(l2s, elements.bit_length() - 1)
        slot = l2s & (elements - 1)
    else:
        owner = l2s // elements
        slot = l2s - owner * elements
    ahead = owner - me
    ahead = jnp.where(ahead < 0, ahead + total, ahead)
    group = jnp.where(ahead == 1, 1, jnp.where(ahead == total - 1, 2, jnp.where(ahead == chan, 3, 0)))
    return slot, group


def fluid_kernel(
    na, planes, chan, total, me_ref, par_ref, u_ref, l2s_ref, k_ref, p_ref, q_ref, wr_ref,
    out_ref, cond_ref, s1_ref, s2_ref, s3_ref, z_ref, fa_ref, fb_ref, t_ref, uf_ref
):
    i = pl.program_id(0)
    k = k_ref[...]
    curve_matrix = time_step * viscosity * (DERIV @ DERIV)
    slope_matrix = time_step * DERIV
    for c in range(3):
        for s in range(8):
            line = [u_ref[c, r, s].astype(f32) for r in range(8)]
            for r in range(8):
                uf_ref[c, r, s] = line[r]
            parts = halves_of(line)
            slope = combined(slope_matrix, parts, -1)
            curve = combined(curve_matrix, parts, 1)
            for r in range(8):
                t_ref[c, r, s] = curve[r] - uf_ref[0, r, s] * slope[r]
    for p in range(2):
        speed = [None] * 32
        for c in range(3):
            x = uf_ref[c, 4 * p : 4 * p + 4].reshape(2, 128, LANES)
            x = jnp.concatenate([x[0], x[1]], 1).astype(bf16)
            y = jnp.dot(k, jnp.concatenate([x, x], 0), preferred_element_type=f32)
            for h in range(2):
                part = y[:, h * LANES : (h + 1) * LANES].reshape(3, 2, 8, 8, LANES)
                for q in range(2):
                    r = 4 * p + 2 * h + q
                    for s in range(8):
                        change = t_ref[c, r, s] - uf_ref[1, r, s] * part[0, q, s] - uf_ref[2, r, s] * part[1, q, s]
                        new = (part[2, q, s] + change).astype(bf16)
                        out_ref[c, r, s] = new
                        new = new.astype(f32)
                        n = (2 * h + q) * 8 + s
                        speed[n] = new * new if speed[n] is None else speed[n] + new * new
        for n, value in enumerate(speed):
            t_ref[0, 4 * p + n // 8, n % 8] = 1.0 + 0.5 * value
    cond_ref[i] = t_ref[0].reshape(512, LANES).astype(bf16)
    source_planes(na, planes, par_ref, p_ref, q_ref, wr_ref, z_ref, fa_ref, fb_ref)

    @pl.when(i == pl.num_programs(0) - 1)
    def _():
        elements = l2s_ref.shape[-1]
        cond = jnp.concatenate([cond_ref[n] for n in range(cond_ref.shape[0])], 1)
        slot, group = owners(l2s_ref[...], me_ref[0], total, chan)
        kinds = lax.broadcasted_iota(jnp.int32, (16, elements), 0)
        marks = (kinds == group).astype(f32).astype(bf16)
        before = lax.broadcasted_iota(jnp.int32, (elements, elements), 0) < lax.broadcasted_iota(
            jnp.int32, (elements, elements), 1
        )
        rank = jnp.dot(marks, before.astype(f32).astype(bf16), preferred_element_type=f32).astype(jnp.int32)
        high = lax.shift_right_logical(slot, 5)
        codes = jnp.concatenate(
            [jnp.broadcast_to(high, (8, elements)), jnp.broadcast_to(slot - high * 32, (8, elements))], 0
        )
        tagged = jnp.concatenate([cond, codes.astype(f32).astype(bf16)], 0)
        room = s1_ref.shape[-1]
        position = lax.broadcasted_iota(jnp.int32, (room, elements), 0)
        even = me_ref[0] % 2 == 0
        one, two = rank[1:2], rank[2:3]
        sends = (
            (jnp.where(even, 1, 2), jnp.where(even, one, two), s1_ref),
            (jnp.where(even, 2, 1), jnp.where(even, two, one), s2_ref),
            (3, rank[3:4], s3_ref),
        )
        for g, order, ref in sends:
            take = ((position == order) & (group == g)).astype(f32).astype(bf16)
            ref[...] = lax.dot_general(tagged, take, NT, preferred_element_type=f32).astype(bf16)


def keep_kernel(chan, total, me_ref, cond_ref, l2s_ref, own_ref):
    elements = l2s_ref.shape[-1]
    cond = jnp.concatenate([cond_ref[n] for n in range(cond_ref.shape[0])], 1)
    slot, group = owners(l2s_ref[...], me_ref[0], total, chan)
    place = lax.broadcasted_iota(jnp.int32, (elements, elements), 0)
    keep = ((place == slot) & (group == 0)).astype(f32).astype(bf16)
    own_ref[...] = lax.dot_general(cond, keep, NT, preferred_element_type=f32).astype(bf16)


def unpack_kernel(na, own_ref, r1_ref, r2_ref, r3_ref, dc_ref, wt_ref, wk_ref, behind_ref, ahead_ref):
    rows = weight_rows(wt_ref[...] * KRYLOV_SCALE)
    got = jnp.concatenate([r[0:512] for r in (r1_ref, r2_ref, r3_ref)], 1)
    tags = [r[512:528].astype(f32) for r in (r1_ref, r2_ref, r3_ref)]
    slots = [(t[0:1] * 32.0 + t[8:9]).astype(jnp.int32) for t in tags]
    slot = jnp.concatenate(slots, 1)
    for j in range(2 * na):
        place = lax.broadcasted_iota(jnp.int32, (LANES, slot.shape[1]), 0) + j * LANES
        put = (place == slot).astype(f32).astype(bf16)
        cols = slice(j * LANES, (j + 1) * LANES)
        moved = own_ref[:, cols].astype(f32) + lax.dot_general(got, put, NT, preferred_element_type=f32)
        kappa = (moved * dc_ref[0:1, cols]).reshape(8, 8, 8, LANES)
        for r in range(8):
            for s in range(8):
                wk_ref[j, r, s] = rows[r][s] * kappa[r, s]
    behind_ref[...], ahead_ref[...] = send_rims(lambda j: wk_ref[j].reshape(512, LANES), na)


def lines_t(k_ref, blocks):
    out = []
    for p in range(0, len(blocks), 2):
        pair = jnp.concatenate(blocks[p : p + 2], 1)
        high = pair.astype(bf16)
        low = (pair - high.astype(f32)).astype(bf16)
        y = jnp.dot(k_ref[...], jnp.concatenate([high, low], 0), preferred_element_type=f32)
        y = y[:128] + y[128:]
        out += [y[:, n * LANES : (n + 1) * LANES].reshape(2, 8, 8, LANES) for n in range(len(blocks[p : p + 2]))]
    return out


def blocks_of(x):
    x = x.reshape(4, 128, LANES)
    return [x[n] for n in range(4)]


def squares(v, j, other, iw_ref):
    sums = {}
    for r in range(8):
        for s in range(8):
            key = (0 if r == 0 else 2 if r == 7 else 1, 0 if s == 0 else 2 if s == 7 else 1)
            x = v[j, r, s]
            pair = (x * x,) if other is None else (x * x, x * other[j, r, s])
            old = sums.get((key, r))
            sums[(key, r)] = pair if old is None else tuple(a + b for a, b in zip(old, pair))
    total = None
    for (key, _), pair in sums.items():
        weight = iw_ref[j, key[0] * 3 + key[1]]
        pair = tuple(weight * a for a in pair)
        total = pair if total is None else tuple(a + b for a, b in zip(total, pair))
    return total


def gradient_r(v, j, g):
    for s in range(8):
        for r, value in enumerate(along(DERIV, [v[j, r, s] for r in range(8)])):
            g[r, s] = value


def fluxes(v, j, wk, c, g, f1, f2):
    gradient_r(v, j, g)
    for r in range(8):
        second = along(DERIV, [v[j, r, s] for s in range(8)])
        k = wk(r)
        for s in range(8):
            first = g[r, s]
            f2[j, r, s] = k[s] * (second[s] + c * first)
            f1[j, r, s] = k[s] * (first + c * second[s])


def lateral_faces(na, par_ref, v, wk, f1, f2, base, kf_ref, kb_ref, a_ref, b_ref):
    rows = [[(l * na + at, 7 * l) for at in range(na)] + [(2 * na, 7 * l)] for l in range(2)]
    flat = rows[0] + rows[1]

    def lines(k_ref, xs):
        blocks = []
        for n in range(0, len(xs), 2):
            blocks.append(jnp.concatenate([x.reshape(64, LANES) for x in xs[n : n + 2]], 0))
        out = []
        for part in lines_t(k_ref, blocks):
            part = part.reshape(2, 8, 8, LANES)
            out += [part[0], part[1]]
        return out

    thirds = lines(kf_ref, [v[j, :, s] for j, s in flat])
    scaled = []
    for (j, s), third in zip(flat, thirds):
        scaled.append(jnp.stack([wk(j, r, s) * third[r] for r in range(8)]))
    thirds = lines(kb_ref, scaled)
    faces = []
    for (j, s), third in zip(flat, thirds):
        first = along(DERIV.T, [f1[j, r, s] for r in range(8)])
        face = []
        for r in range(8):
            second = sum(float(DERIV[i, s]) * f2[j, r, i] for i in range(8) if DERIV[i, s] != 0.0)
            face.append(second + (base[r] * float(GLL_W[s])) * v[j, r, s] + first[r] + third[r])
        faces.append(face)
    for l in range(2):
        row = faces[l * (na + 1) : (l + 1) * (na + 1)]
        far, near = axial_row(l, [x[7] for x in row], [x[0] for x in row])
        for x, last, start in zip(row, far, near):
            x[7], x[0] = last, start
    for at in range(na):
        for r in range(8):
            send_faces(par_ref, at * 8 + r, faces[at][r], faces[na + 1 + at][r], a_ref, b_ref)
    send_faces(par_ref, na * 8, pack_rim(faces[na], 0), pack_rim(faces[2 * na + 1], 1), a_ref, b_ref)


def mass_rows(wt, base):
    for r in range(8):
        base[r] = wt * float(GLL_W[r] * coolant_throughput * KRYLOV_SCALE)


def flux_kernel(na, first, *refs):
    refs = list(refs)
    take = lambda n: [refs.pop(0) for _ in range(n)]
    ghost = 2 * na
    if first:
        par_ref, z_in, wk_ref, b_in, a_in, dc_ref = take(6)
    else:
        par_ref, _, b_in, a_in, wk_ref, wkg_ref, cr_ref = take(7)
    wt_ref, kf_ref, kb_ref, v, f1, f2, a_out, b_out = take(8)
    if first:
        wkg_ref, cr_ref = take(2)
    g, base = refs
    if first:
        v[0:ghost] = z_in[...]
        even = par_ref[5] == 0
        a, b = a_in[...], b_in[...]
        rims = place_rims(jnp.where(even, a, b), jnp.where(even, b, a))
        v[ghost] = rims[0:512].reshape(8, 8, 8, LANES)
        wkg_ref[...] = rims[640:1152].reshape(8, 8, 8, LANES)
        for j in range(ghost):
            cr_ref[j] = jnp.broadcast_to(dc_ref[1:2, j * LANES : (j + 1) * LANES], (8, LANES))
        cr_ref[ghost] = rims[512:520]
        assemble_axial(na, v)
    else:
        add_faces(na, par_ref, v, a_in, b_in)
    mass_rows(wt_ref[...], base)
    for j in range(ghost + 1):
        if j < ghost:
            wk = lambda r: wk_ref[j, r]
        else:
            wk = lambda r: wkg_ref[r]
        fluxes(v, j, wk, cr_ref[j], g.at[j % 2], f1, f2)
    face_wk = lambda j, r, s: wk_ref[j, r, s] if j < ghost else wkg_ref[r, s]
    lateral_faces(na, par_ref, v, face_wk, f1, f2, base, kf_ref, kb_ref, a_out, b_out)


def rest_kernel(na, first, *refs):
    refs = list(refs)
    prev = None if first else refs.pop(0)
    v, f1, f2, wk_ref, wkg_ref, wt_ref, iw_ref, kf_ref, kb_ref, y, dots, base, f3 = refs
    ghost = 2 * na
    mass_rows(wt_ref[...], base)
    totals = None
    for j in range(ghost + 1):
        if j < ghost:
            sums = squares(v, j, prev, iw_ref)
            totals = sums if totals is None else [a + b for a, b in zip(totals, sums)]
        for p, part in enumerate(lines_t(kf_ref, blocks_of(v[j]))):
            for q in range(2):
                r = 2 * p + q
                f3[j % 2, r] = (wk_ref[j, r] if j < ghost else wkg_ref[r]) * part[q]
        parts = lines_t(kb_ref, blocks_of(f3[j % 2]))
        for r in range(8):
            for s, value in enumerate(along(DERIV.T, [f2[j, r, s] for s in range(8)])):
                y[j, r, s] = value + (base[r] * float(GLL_W[s])) * v[j, r, s]
        for s in range(8):
            for r, value in enumerate(along(DERIV.T, [f1[j, r, s] for r in range(8)])):
                y[j, r, s] = y[j, r, s] + value + parts[r // 2][r % 2, s]
    for k, value in enumerate(totals):
        dots[k] = jnp.broadcast_to(jnp.sum(jnp.sum(value, 0, keepdims=True), 1, keepdims=True), (8, LANES))
    assemble_axial(na, y)
    assemble_lateral(na, y)


def last_kernel(na, par_ref, _, b_in, a_in, wk_ref, cr_ref, prev, wt_ref, iw_ref, kf_ref, d0, d1, d2, d3, v, all_dots, g, base):
    ghost = 2 * na
    add_faces(na, par_ref, v, a_in, b_in)
    mass_rows(wt_ref[...], base)
    totals = None
    for j in range(ghost):
        gj = g.at[j % 2]
        third = lines_t(kf_ref, blocks_of(v[j]))
        sums = list(squares(v, j, prev, iw_ref))
        gradient_r(v, j, gj)
        c = 2.0 * cr_ref[j]
        total = None
        for r in range(8):
            line = [v[j, r, s] for s in range(8)]
            second = along(DERIV, line)
            row = None
            for s in range(8):
                one, two, three = gj[r, s], second[s], third[r // 2][r % 2, s]
                term = (base[r] * float(GLL_W[s])) * (line[s] * line[s])
                term = term + wk_ref[j, r, s] * (one * (one + c * two) + two * two + three * three)
                row = term if row is None else row + term
            total = row if total is None else total + row
        sums.append(total)
        totals = sums if totals is None else [a + b for a, b in zip(totals, sums)]
    lane = lane_index(1)
    rows = [d0[0], d1[1], d1[0], d2[1], d2[0], d3[1], d3[0], totals[1], totals[0], totals[2]]
    out = jnp.zeros((1, LANES), f32)
    for k, row in enumerate(rows):
        if k < 2 * ITERS - 3:
            row = row[0:1]
        else:
            row = jnp.sum(jnp.sum(row, 0, keepdims=True), 1, keepdims=True)
        out = jnp.where(lane == k, row, out)
    all_dots[...] = jnp.broadcast_to(out[None], all_dots.shape)


def solve_moments(m_ref, coef_ref):
    sums = jnp.sum(m_ref[:, 0, :], 0, keepdims=True)
    lane = lane_index(1)
    m = [jnp.sum(jnp.where(lane == k, sums, 0.0), 1, keepdims=True) for k in range(2 * ITERS)]
    n = ITERS
    low = [[None] * n for _ in range(n)]
    diag = [None] * n
    for j in range(n):
        acc = [m[i + j + 1] for i in range(n)]
        for k in range(j):
            scaled = low[j][k] * diag[k]
            for i in range(j, n):
                acc[i] = acc[i] - low[i][k] * scaled
        diag[j] = acc[j]
        for i in range(j + 1, n):
            low[i][j] = acc[i] / acc[j]
    z = []
    for i in range(n):
        value = m[i]
        for k in range(i):
            value = value - low[i][k] * z[k]
        z.append(value)
    c = [z[i] / diag[i] for i in range(n)]
    for i in reversed(range(n)):
        for k in range(i + 1, n):
            c[i] = c[i] - low[k][i] * c[k]
    for k, x in enumerate(c):
        coef_ref[k] = jnp.broadcast_to(x * KRYLOV_SCALE, (8, LANES))


def combine_kernel(na, planes, m_ref, v0, v1, v2, v3, v4, out_ref, coef_ref):
    i = pl.program_id(0)

    @pl.when(i == 0)
    def _():
        solve_moments(m_ref, coef_ref)

    c = [coef_ref[k] for k in range(ITERS)]
    step = 2 * na
    for n in range(planes):
        r = i * planes + n
        for s in range(8):
            base = (n * 8 + s) * 8 * step
            for l in range(2):
                for at in range(na):
                    x = None
                    for coef, v in zip(c, (v0, v1, v2, v3, v4)):
                        term = coef * v[l * na + at, r, s]
                        x = term if x is None else x + term
                    out_ref[pl.ds(base + at * 2 + l, 8, stride=step), :] = x


def slab_swap(x, start):
    n, m = lax.axis_size("slab"), lax.axis_size("chan")
    pairs = [(i * m + c, (i + 1) * m + c) for i in range(start, n - 1, 2) for c in range(m)]
    busy = {i for pair in pairs for i in pair}
    pairs += [(i, i + 1) for i in range(0, n * m, 2) if i not in busy]
    return lax.ppermute(x, ("slab", "chan"), pairs + [(j, i) for i, j in pairs])


def swap(x, axis, start):
    n = lax.axis_size(axis)
    pairs = [((start + i) % n, (start + i + 1) % n) for i in range(0, n, 2)]
    return lax.ppermute(x, axis, pairs + [(j, i) for i, j in pairs])


def around(x, by):
    n = lax.axis_size("slab") * lax.axis_size("chan")
    return lax.ppermute(x, ("slab", "chan"), [(i, (i + by) % n) for i in range(n)])


def swap_around(x, start):
    n = lax.axis_size("slab") * lax.axis_size("chan")
    pairs = [((start + i) % n, (start + i + 1) % n) for i in range(0, n, 2)]
    return lax.ppermute(x, ("slab", "chan"), pairs + [(j, i) for i, j in pairs])


def product_weights(count_l, count_a):
    slab, chan = lax.axis_index("slab"), lax.axis_index("chan")
    axial = slab * count_a + jnp.arange(count_a)
    lateral = chan * count_l + jnp.arange(count_l)
    last_a = lax.axis_size("slab") * count_a - 1
    last_l = lax.axis_size("chan") * count_l - 1
    half = lambda cond: jnp.where(cond, 0.5, 1.0).astype(f32)
    along_a = jnp.stack([half(axial > 0), jnp.ones(count_a, f32), half(axial < last_a)])
    along_l = jnp.stack([half(lateral > 0), jnp.ones(count_l, f32), half(lateral < last_l)])
    weights = along_a[:, None, None, :] * along_l[None, :, :, None]
    weights = weights.reshape(9, -1, LANES).transpose(1, 0, 2)
    return jnp.broadcast_to(weights[:, :, None, :], weights.shape[:2] + (8, LANES))


def on_device(
    stream_speed_field,
    liquid_to_solid_element,
    previous_panel_warmth,
    pointwise_energy_source,
    coked_element_flags,
    coking_thickness_plies,
):
    count_l, count_a = coked_element_flags.shape
    assert count_l == 2 and count_a % LANES == 0
    elements = count_l * count_a
    na = count_a // LANES
    tiles = count_l * na
    chan = lax.axis_size("chan")
    total = lax.axis_size("slab") * chan
    slab_at, chan_at = lax.axis_index("slab"), lax.axis_index("chan")
    me = (slab_at * chan + chan_at).astype(jnp.int32).reshape(1)
    position = [
        chan_at % 2,
        chan_at > 0,
        chan_at < chan - 1,
        slab_at > 0,
        slab_at < lax.axis_size("slab") - 1,
        slab_at % 2,
    ]
    position = jnp.stack([jnp.asarray(x, jnp.int32) for x in position])

    wt = jnp.asarray(np.broadcast_to(GLL_W[:, None], (8, LANES)), f32)
    wr = jnp.asarray(np.broadcast_to((GLL_W[:, None] * GLL_W)[:, :, None], (8, 8, LANES)), f32)
    kf, kb = (jnp.asarray(k) for k in line_matrices())
    kfluid = jnp.asarray(fluid_matrix())

    layers = coking_thickness_plies.astype(f32)
    flags = coked_element_flags.astype(f32)
    damping = jnp.where(coked_element_flags == 1, 1.0 / (1.0 + layer_damp * layers), jnp.ones_like(layers))
    cross = cross_gain * flags * layers / (layers + 1.0)
    dc = jnp.stack([damping.reshape(elements), cross.reshape(elements)])
    iw = product_weights(count_l, count_a)

    def as_rows(x):
        x = x.reshape(8, 8, 8, count_l, na, LANES).transpose(0, 1, 2, 4, 3, 5)
        return x.reshape(512 * tiles, LANES)

    field = (tiles, 8, 8, 8, LANES)
    whole = (tiles + 1, 8, 8, 8, LANES)
    shape = lambda s, d=f32: jax.ShapeDtypeStruct(s, d)
    kept = vmem
    split = elements // LANES
    width = LANES
    room = elements // 4
    in_hbm = lambda x: pltpu.with_memory_space_constraint(x, pltpu.HBM)
    here = lambda: pl.BlockSpec(memory_space=pltpu.VMEM)
    scalars = pl.BlockSpec(memory_space=pltpu.SMEM)
    steps = 4
    rows = 512 * tiles // steps
    l2s = liquid_to_solid_element.reshape(1, elements)
    out = pl.pallas_call(
        functools.partial(fluid_kernel, na, 8 // split, chan, total),
        grid=(split,),
        in_specs=[
            scalars,
            scalars,
            pl.BlockSpec((3, 8, 8, 8, width), lambda i: (0, 0, 0, 0, i)),
            pl.BlockSpec((1, elements), lambda i: (0, 0)),
            pl.BlockSpec(kfluid.shape, lambda i: (0, 0)),
        ]
        + [pl.BlockSpec((512 * tiles // split, LANES), lambda i: (i, 0))] * 2
        + [pl.BlockSpec((8, 8, LANES), lambda i: (0, 0, 0))],
        out_specs=[pl.BlockSpec((3, 8, 8, 8, width), lambda i: (0, 0, 0, 0, i))] + [here()] * 7,
        out_shape=[shape(stream_speed_field.shape, bf16), kept((split, 512, width), bf16)]
        + [kept((528, room), bf16)] * 3
        + [kept(field), kept((na, 8, 8, LANES)), kept((na, 8, 8, LANES))],
        scratch_shapes=[pltpu.VMEM((3, 8, 8, 8, width), f32)] * 2,
        compiler_params=pltpu.CompilerParams(vmem_limit_bytes=24 * 1024 * 1024),
    )(
        me,
        position,
        in_hbm(stream_speed_field),
        in_hbm(l2s),
        in_hbm(kfluid),
        in_hbm(as_rows(previous_panel_warmth)),
        in_hbm(as_rows(pointwise_energy_source)),
        in_hbm(wr),
    )
    stepped, cond, out_even, out_odd, out_far, z, a, b = out
    received = [around(out_far, chan), swap_around(out_odd, 1), swap_around(out_even, 0)]
    (own,) = call(
        functools.partial(keep_kernel, chan, total), [kept((512, elements), bf16)], me, cond, l2s, smem=1
    )
    a, b, own = lax.optimization_barrier((a, b, own))
    b, a = swap(b, "chan", 1), swap(a, "chan", 0)
    wk, wk_behind, wk_ahead = call(
        functools.partial(unpack_kernel, na),
        [kept(field), kept((2 * RIM, 512)), kept((2 * RIM, 512))],
        own,
        *received,
        dc,
        wt,
    )
    z, a, b = call(
        functools.partial(rim_kernel, na),
        [kept(field), kept((2 * RIM, 1152)), kept((2 * RIM, 1152))],
        position,
        z,
        b,
        a,
        dc,
        wk_behind,
        wk_ahead,
        smem=1,
    )
    b, a = slab_swap(b, 1), slab_swap(a, 0)

    basis, products = [], []
    face = (8 * na + 1, 8, LANES)
    for number in range(ITERS - 1):
        first = number == 0
        outs = [kept(whole)] * 3 + [kept(face)] * 2
        if first:
            args = (z, wk, b, a, dc)
            outs += [kept((8, 8, 8, LANES)), kept((tiles + 1, 8, LANES))]
        else:
            args = (y, b, a, wk, wkg, cr)
        got = call(
            functools.partial(flux_kernel, na, first),
            outs,
            position,
            *args,
            wt,
            kf,
            kb,
            smem=1,
            scratch=[pltpu.VMEM((2, 8, 8, 8, LANES), f32), pltpu.VMEM((8, 8, LANES), f32)],
            input_output_aliases={} if first else {1: 0},
        )
        if first:
            wkg, cr = got[5:]
        v, f1, f2, a, b = got[:5]
        b, a = swap(b, "chan", 1), swap(a, "chan", 0)
        y, dots = call(
            functools.partial(rest_kernel, na, first),
            [kept(whole), kept((2, 8, LANES))],
            *basis[-1:],
            v,
            f1,
            f2,
            wk,
            wkg,
            wt,
            iw,
            kf,
            kb,
            scratch=[pltpu.VMEM((8, 8, LANES), f32), pltpu.VMEM((2, 8, 8, 8, LANES), f32)],
        )
        basis.append(v)
        products.append(dots)
    v, sums = call(
        functools.partial(last_kernel, na),
        [kept(whole), kept((total, 1, LANES))],
        position,
        y,
        b,
        a,
        wk,
        cr,
        basis[-1],
        wt,
        iw,
        kf,
        *products,
        smem=1,
        input_output_aliases={1: 0},
        scratch=[pltpu.VMEM((2, 8, 8, 8, LANES), f32), pltpu.VMEM((8, 8, LANES), f32)],
    )
    basis.append(v)
    sums = lax.all_to_all(sums, ("slab", "chan"), 0, 0)
    x = pl.pallas_call(
        functools.partial(combine_kernel, na, 8 // steps),
        grid=(steps,),
        in_specs=[here()] * 6,
        out_specs=pl.BlockSpec((rows, LANES), lambda i: (i, 0)),
        out_shape=shape((512 * tiles, LANES)),
        scratch_shapes=[pltpu.VMEM((ITERS, 8, LANES), f32)],
        compiler_params=pltpu.CompilerParams(vmem_limit_bytes=12 * 1024 * 1024),
    )(sums, *basis)
    x = x.reshape(8, 8, 8, na, count_l, LANES).transpose(0, 1, 2, 4, 3, 5)
    return stepped, x.reshape(8, 8, 8, count_l, count_a)


def solution(mesh):
    in_specs = (
        P(None, None, None, None, ("slab", "chan")),
        P(("slab", "chan")),
        P(None, None, None, "chan", "slab"),
        P(None, None, None, "chan", "slab"),
        P("chan", "slab"),
        P("chan", "slab"),
    )
    out_specs = (P(None, None, None, None, ("slab", "chan")), P(None, None, None, "chan", "slab"))
    return jax.shard_map(
        on_device, mesh=mesh, in_specs=in_specs, out_specs=out_specs, check_vma=False
    )
```

```python
import functools

import jax
import jax.numpy as jnp
import numpy as np
from jax import lax
from jax.experimental import pallas as pl
from jax.experimental.pallas import tpu as pltpu
from jax.sharding import PartitionSpec as P

ITERS = 5
LANES = 128
RIM = 4
KRYLOV_SCALE = 1.0 / 256.0

highest = lax.Precision.HIGHEST
f32 = jnp.float32
bf16 = jnp.bfloat16
coolant_throughput = 0.05
time_step = 0.01
viscosity = 0.02
cross_gain = 0.4
layer_damp = 0.25

NT = (((1,), (1,)), ((), ()))
TN = (((0,), (0,)), ((), ()))


def gll_tables():
    points = np.array(
        [
            -1.0,
            -0.8717401485096066,
            -0.5917001814331423,
            -0.2092992179024789,
            0.2092992179024789,
            0.5917001814331423,
            0.8717401485096066,
            1.0,
        ]
    )
    weights = np.array(
        [
            1.0 / 28.0,
            0.2107042271435061,
            0.3411226924835044,
            0.4124587946587038,
            0.4124587946587038,
            0.3411226924835044,
            0.2107042271435061,
            1.0 / 28.0,
        ]
    )
    lower_poly = np.ones(8)
    upper_poly = points.copy()
    for degree in range(1, 7):
        next_poly = ((2 * degree + 1) * points * upper_poly - degree * lower_poly) / (degree + 1)
        lower_poly = upper_poly
        upper_poly = next_poly
    gaps_matrix = points[:, None] - points[None, :] + np.eye(8)
    derivative = upper_poly[:, None] / (upper_poly[None, :] * gaps_matrix)
    derivative = derivative * (1.0 - np.eye(8))
    derivative[0, 0] = -14.0
    derivative[7, 7] = 14.0
    return derivative, weights


DERIV, GLL_W = gll_tables()
DERIV = DERIV.astype(np.float32).astype(np.float64)
GLL_W = GLL_W.astype(np.float32).astype(np.float64)


def split_hi_lo(matrix):
    high = np.asarray(matrix, np.float32).astype(jnp.bfloat16)
    low = (np.asarray(matrix, np.float64) - high.astype(np.float64)).astype(np.float32)
    return high, low.astype(jnp.bfloat16)


def line_matrices():
    out = []
    for matrix in (DERIV, DERIV.T):
        high, low = split_hi_lo(np.kron(np.eye(16), matrix))
        upper = np.concatenate([high, high], 1)
        out.append(np.concatenate([upper, np.concatenate([low, np.zeros_like(low)], 1)], 0))
    return out


def fluid_matrix():
    eye8 = np.eye(8)
    square = DERIV @ DERIV
    second = time_step * np.kron(DERIV, eye8)
    third = time_step * np.kron(eye8, DERIV)
    curve = np.eye(64) + time_step * viscosity * (np.kron(square, eye8) + np.kron(eye8, square))
    return np.concatenate([np.concatenate(split_hi_lo(np.kron(np.eye(2), m)), 1) for m in (second, third, curve)], 0)


def halves_of(line):
    return [line[j] + line[7 - j] for j in range(4)], [line[j] - line[7 - j] for j in range(4)]


def combined(matrix, parts, sign):
    even, odd = parts
    result = [None] * 8
    for i in range(4):
        p = sum(float(0.5 * (matrix[i, j] + matrix[i, 7 - j])) * even[j] for j in range(4))
        q = sum(float(0.5 * (matrix[i, j] - matrix[i, 7 - j])) * odd[j] for j in range(4))
        result[i] = p + q
        result[7 - i] = q - p if sign < 0 else p - q
    return result


def along(matrix, line):
    return combined(matrix, halves_of(line), -1)


def lane_index(rows=8):
    return lax.broadcasted_iota(jnp.int32, (rows, LANES), 1)


def vmem(shape, dtype=f32):
    return pltpu.VMEM(shape, dtype)


def call(kernel, out_shape, *args, smem=0, scratch=(), limit=12, **kw):
    specs = [pl.BlockSpec(memory_space=pltpu.SMEM)] * smem
    specs += [pl.BlockSpec(memory_space=pltpu.VMEM)] * (len(args) - smem)
    outs = [pl.BlockSpec(memory_space=pltpu.VMEM) for _ in out_shape]
    return pl.pallas_call(
        kernel,
        in_specs=specs,
        out_specs=outs,
        out_shape=out_shape,
        scratch_shapes=scratch,
        compiler_params=pltpu.CompilerParams(vmem_limit_bytes=limit * 1024 * 1024),
        **kw,
    )(*args)


def weight_rows(wt):
    return [[float(GLL_W[r] * GLL_W[s]) * wt for s in range(8)] for r in range(8)]


def in_three(x):
    high = x.astype(bf16)
    rest = x - high.astype(f32)
    middle = rest.astype(bf16)
    return [high, middle, (rest - middle.astype(f32)).astype(bf16)]


def sel_matrix(l, first_lane):
    row = lax.broadcasted_iota(jnp.int32, (2 * RIM, LANES), 0)
    lane = lax.broadcasted_iota(jnp.int32, (2 * RIM, LANES), 1)
    inside = (row >= l * RIM) & (row < (l + 1) * RIM)
    return ((row - l * RIM + first_lane == lane) & inside).astype(f32)


def place_matrix(first_lane):
    row = lax.broadcasted_iota(jnp.int32, (2 * RIM, LANES), 0)
    lane = lax.broadcasted_iota(jnp.int32, (2 * RIM, LANES), 1)
    target = jnp.where(row < RIM, row + first_lane, row - RIM + first_lane + LANES // 2)
    return (target == lane).astype(f32)


def send_rims(near_rows, far_rows, na):
    def pick(tile_rows, tiles, first_lane):
        out = None
        for l, j in enumerate(tiles):
            terms = jnp.concatenate(in_three(tile_rows(j)), 1)
            sel = jnp.concatenate([sel_matrix(l, first_lane)] * 3, 1).astype(bf16)
            part = lax.dot_general(sel, terms, NT, preferred_element_type=f32)
            out = part if out is None else out + part
        return out

    return pick(near_rows, (0, na), 0), pick(far_rows, (na - 1, 2 * na - 1), LANES - RIM)


def place_rims(from_ahead, from_behind):
    terms = [x.astype(f32) for x in in_three(from_ahead) + in_three(from_behind)]
    places = [place_matrix(0)] * 3 + [place_matrix(LANES // 2 - RIM)] * 3
    terms = jnp.concatenate(terms, 0).astype(bf16)
    places = jnp.concatenate(places, 0).astype(bf16)
    return lax.dot_general(terms, places, TN, preferred_element_type=f32)


def source_planes(na, planes, par_ref, p_ref, q_ref, wr_ref, z_ref, a_ref, b_ref):
    step = 2 * na
    for n in range(planes):
        r = pl.program_id(0) * planes + n
        wr = wr_ref[r]
        ends = {}
        for s in range(8):
            base = (n * 8 + s) * 8 * step
            for l in range(2):
                for at in range(na):
                    pick = pl.ds(base + at * 2 + l, 8, stride=step)
                    value = (wr * float(GLL_W[s])) * (coolant_throughput * p_ref[pick, :] + q_ref[pick, :])
                    if (l, s) in ((0, 0), (0, 7), (1, 0), (1, 7)):
                        ends[l, s, at] = value
                    else:
                        z_ref[l * na + at, r, s] = value
        for at in range(na):
            shared = ends[0, 7, at] + ends[1, 0, at]
            z_ref[at, r, 7] = shared
            z_ref[na + at, r, 0] = shared
            lower, upper = ends[0, 0, at], ends[1, 7, at]
            z_ref[at, r, 0] = lower
            z_ref[na + at, r, 7] = upper
            send_faces(par_ref, (at, r), lower, upper, a_ref, b_ref)


def rim_kernel(na, par_ref, z_in, b_ref, a_ref, dc_ref, wkb_ref, wka_ref, v_ref, a_out, b_out):
    v_ref[0 : 2 * na] = z_in[...]
    for r in range(8):
        for at in range(na):
            lower, upper = got_faces(par_ref, (at, r), a_ref, b_ref)
            v_ref[at, r, 0] = v_ref[at, r, 0] + lower
            v_ref[na + at, r, 7] = v_ref[na + at, r, 7] + upper

    lane = lane_index()
    cross = lambda j: jnp.broadcast_to(dc_ref[1:2, j * LANES : (j + 1) * LANES], (LANES, LANES))

    def near_rows(j):
        rows = []
        for s in range(8):
            inner = pltpu.roll(v_ref[j, 0, s], LANES - 1, 1)
            rows.append(v_ref[j, 7, s] + jnp.where(lane == RIM - 1, inner, 0.0))
        return jnp.concatenate([v_ref[j, 0:7].reshape(448, LANES)] + rows + [cross(j)], 0)

    def far_rows(j):
        rows = []
        for s in range(8):
            inner = pltpu.roll(v_ref[j, 7, s], 1, 1)
            rows.append(v_ref[j, 0, s] + jnp.where(lane == LANES - RIM, inner, 0.0))
        return jnp.concatenate(rows + [v_ref[j, 1:8].reshape(448, LANES), cross(j)], 0)

    behind, ahead = send_rims(near_rows, far_rows, na)
    behind = jnp.where(par_ref[3] > 0, jnp.concatenate([behind, wkb_ref[...]], 1), 0.0)
    ahead = jnp.where(par_ref[4] > 0, jnp.concatenate([ahead, wka_ref[...]], 1), 0.0)
    even = par_ref[5] == 0
    a_out[...] = jnp.where(even, ahead, behind)
    b_out[...] = jnp.where(even, behind, ahead)


def send_faces(par_ref, at, lower, upper, a_ref, b_ref):
    even = par_ref[0] == 0
    lower = jnp.where(par_ref[1] > 0, lower, 0.0)
    upper = jnp.where(par_ref[2] > 0, upper, 0.0)
    a_ref[at] = jnp.where(even, upper, lower)
    b_ref[at] = jnp.where(even, lower, upper)


def got_faces(par_ref, at, a_ref, b_ref):
    even = par_ref[0] == 0
    a, b = a_ref[at], b_ref[at]
    return jnp.where(even, b, a), jnp.where(even, a, b)


def axial_row(l, far, near):
    ghost = len(far) - 1
    lane = lane_index()
    half = LANES // 2
    roll = pltpu.roll
    right = [roll(x, 1, 1) for x in far]
    left = [roll(x, LANES - 1, 1) for x in near]
    new_far, new_near = [], []
    for at in range(ghost):
        if at > 0:
            carry = right[at - 1]
        else:
            carry = roll(far[ghost], half + 1, 1) if l == 0 else right[ghost]
        new_near.append(near[at] + jnp.where(lane == 0, carry, right[at]))
        if at < ghost - 1:
            carry = left[at + 1]
        else:
            carry = left[ghost] if l == 0 else roll(near[ghost], half - 1, 1)
        new_far.append(far[at] + jnp.where(lane == LANES - 1, carry, left[at]))
    carry = right[ghost - 1] if l == 0 else roll(far[ghost - 1], half + 1, 1)
    new_near.append(near[ghost] + jnp.where(lane == half * l, carry, right[ghost]))
    carry = roll(near[0], half - 1, 1) if l == 0 else left[0]
    new_far.append(far[ghost] + jnp.where(lane == half * (l + 1) - 1, carry, left[ghost]))
    return new_far, new_near


def assemble_axial(na, y):
    ghost = 2 * na
    low = lane_index() < LANES // 2
    for s in range(8):
        rims = []
        for l in range(2):
            tiles = list(range(l * na, l * na + na)) + [ghost]
            far, near = axial_row(l, [y[j, 7, s] for j in tiles], [y[j, 0, s] for j in tiles])
            for n, j in enumerate(tiles[:-1]):
                y[j, 7, s] = far[n]
                y[j, 0, s] = near[n]
            rims.append((far[-1], near[-1]))
        y[ghost, 7, s] = jnp.where(low, rims[0][0], rims[1][0])
        y[ghost, 0, s] = jnp.where(low, rims[0][1], rims[1][1])


def assemble_lateral(na, y):
    ghost = 2 * na
    half = LANES // 2
    low = lane_index() < half
    for r in range(8):
        for at in range(na):
            shared = y[at, r, 7] + y[na + at, r, 0]
            y[at, r, 7] = shared
            y[na + at, r, 0] = shared
        upper = y[ghost, r, 7]
        lower = y[ghost, r, 0]
        y[ghost, r, 7] = upper + jnp.where(low, pltpu.roll(lower, half, 1), 0.0)
        y[ghost, r, 0] = lower + jnp.where(low, 0.0, pltpu.roll(upper, half, 1))


def turn(x, by):
    return x if by % LANES == 0 else pltpu.roll(x, by % LANES, 1)


def pack_rim(planes, l):
    lane = lane_index()
    half = LANES // 2
    out = None
    for r, x in enumerate(planes):
        at = 2 * RIM * r
        near = turn(x, at - half * l)
        far = turn(x, at + RIM - (half * (l + 1) - RIM))
        near = jnp.where((lane >= at) & (lane < at + RIM), near, 0.0)
        both = jnp.where((lane >= at + RIM) & (lane < at + 2 * RIM), far, near)
        out = both if out is None else out + both
    return out


def unpack_rim(x, r, l):
    lane = lane_index()
    half = LANES // 2
    at = 2 * RIM * r
    near = turn(x, half * l - at)
    far = turn(x, half * (l + 1) - RIM - (at + RIM))
    near = jnp.where((lane >= half * l) & (lane < half * l + RIM), near, 0.0)
    return jnp.where((lane >= half * (l + 1) - RIM) & (lane < half * (l + 1)), far, near)


def add_faces(na, par_ref, v, a_ref, b_ref):
    ghost = 2 * na
    for at in range(na):
        for r in range(8):
            lower, upper = got_faces(par_ref, at * 8 + r, a_ref, b_ref)
            v[at, r, 0] = v[at, r, 0] + lower
            v[na + at, r, 7] = v[na + at, r, 7] + upper
    lower, upper = got_faces(par_ref, na * 8, a_ref, b_ref)
    for r in range(8):
        v[ghost, r, 0] = v[ghost, r, 0] + unpack_rim(lower, r, 0)
        v[ghost, r, 7] = v[ghost, r, 7] + unpack_rim(upper, r, 1)


def owners(l2s, me, total, chan):
    elements = l2s.shape[1]
    if elements & (elements - 1) == 0:
        owner = lax.shift_right_logical(l2s, elements.bit_length() - 1)
        slot = l2s & (elements - 1)
    else:
        owner = l2s // elements
        slot = l2s - owner * elements
    ahead = owner - me
    ahead = jnp.where(ahead < 0, ahead + total, ahead)
    group = jnp.where(ahead == 1, 1, jnp.where(ahead == total - 1, 2, jnp.where(ahead == chan, 3, 0)))
    return slot, group


def fluid_kernel(
    na, planes, chan, total, me_ref, par_ref, u_ref, l2s_ref, k_ref, p_ref, q_ref, wr_ref,
    out_ref, cond_ref, s1_ref, s2_ref, s3_ref, z_ref, fa_ref, fb_ref, t_ref, uf_ref
):
    i = pl.program_id(0)
    k = k_ref[...]
    curve_matrix = time_step * viscosity * (DERIV @ DERIV)
    slope_matrix = time_step * DERIV
    for c in range(3):
        for s in range(8):
            line = [u_ref[c, r, s].astype(f32) for r in range(8)]
            for r in range(8):
                uf_ref[c, r, s] = line[r]
            parts = halves_of(line)
            slope = combined(slope_matrix, parts, -1)
            curve = combined(curve_matrix, parts, 1)
            for r in range(8):
                t_ref[c, r, s] = curve[r] - uf_ref[0, r, s] * slope[r]
    for p in range(2):
        speed = [None] * 32
        for c in range(3):
            x = uf_ref[c, 4 * p : 4 * p + 4].reshape(2, 128, LANES)
            x = jnp.concatenate([x[0], x[1]], 1).astype(bf16)
            y = jnp.dot(k, jnp.concatenate([x, x], 0), preferred_element_type=f32)
            for h in range(2):
                part = y[:, h * LANES : (h + 1) * LANES].reshape(3, 2, 8, 8, LANES)
                for q in range(2):
                    r = 4 * p + 2 * h + q
                    for s in range(8):
                        change = t_ref[c, r, s] - uf_ref[1, r, s] * part[0, q, s] - uf_ref[2, r, s] * part[1, q, s]
                        new = (part[2, q, s] + change).astype(bf16)
                        out_ref[c, r, s] = new
                        new = new.astype(f32)
                        n = (2 * h + q) * 8 + s
                        speed[n] = new * new if speed[n] is None else speed[n] + new * new
        for n, value in enumerate(speed):
            t_ref[0, 4 * p + n // 8, n % 8] = 1.0 + 0.5 * value
    cond_ref[i] = t_ref[0].reshape(512, LANES).astype(bf16)
    source_planes(na, planes, par_ref, p_ref, q_ref, wr_ref, z_ref, fa_ref, fb_ref)

    @pl.when(i == pl.num_programs(0) - 1)
    def _():
        elements = l2s_ref.shape[-1]
        cond = jnp.concatenate([cond_ref[n] for n in range(cond_ref.shape[0])], 1)
        slot, group = owners(l2s_ref[...], me_ref[0], total, chan)
        kinds = lax.broadcasted_iota(jnp.int32, (16, elements), 0)
        marks = (kinds == group).astype(f32).astype(bf16)
        before = lax.broadcasted_iota(jnp.int32, (elements, elements), 0) < lax.broadcasted_iota(
            jnp.int32, (elements, elements), 1
        )
        rank = jnp.dot(marks, before.astype(f32).astype(bf16), preferred_element_type=f32).astype(jnp.int32)
        high = lax.shift_right_logical(slot, 5)
        codes = jnp.concatenate(
            [jnp.broadcast_to(high, (8, elements)), jnp.broadcast_to(slot - high * 32, (8, elements))], 0
        )
        tagged = jnp.concatenate([cond, codes.astype(f32).astype(bf16)], 0)
        room = s1_ref.shape[-1]
        position = lax.broadcasted_iota(jnp.int32, (room, elements), 0)
        even = me_ref[0] % 2 == 0
        one, two = rank[1:2], rank[2:3]
        sends = (
            (jnp.where(even, 1, 2), jnp.where(even, one, two), s1_ref),
            (jnp.where(even, 2, 1), jnp.where(even, two, one), s2_ref),
            (3, rank[3:4], s3_ref),
        )
        for g, order, ref in sends:
            take = ((position == order) & (group == g)).astype(f32).astype(bf16)
            ref[...] = lax.dot_general(tagged, take, NT, preferred_element_type=f32).astype(bf16)


def keep_kernel(chan, total, me_ref, cond_ref, l2s_ref, own_ref):
    elements = l2s_ref.shape[-1]
    cond = jnp.concatenate([cond_ref[n] for n in range(cond_ref.shape[0])], 1)
    slot, group = owners(l2s_ref[...], me_ref[0], total, chan)
    place = lax.broadcasted_iota(jnp.int32, (elements, elements), 0)
    keep = ((place == slot) & (group == 0)).astype(f32).astype(bf16)
    own_ref[...] = lax.dot_general(cond, keep, NT, preferred_element_type=f32).astype(bf16)


def unpack_kernel(na, own_ref, r1_ref, r2_ref, r3_ref, dc_ref, wt_ref, wk_ref, behind_ref, ahead_ref):
    rows = weight_rows(wt_ref[...] * KRYLOV_SCALE)
    got = jnp.concatenate([r[0:512] for r in (r1_ref, r2_ref, r3_ref)], 1)
    tags = [r[512:528].astype(f32) for r in (r1_ref, r2_ref, r3_ref)]
    slots = [(t[0:1] * 32.0 + t[8:9]).astype(jnp.int32) for t in tags]
    slot = jnp.concatenate(slots, 1)
    for j in range(2 * na):
        place = lax.broadcasted_iota(jnp.int32, (LANES, slot.shape[1]), 0) + j * LANES
        put = (place == slot).astype(f32).astype(bf16)
        cols = slice(j * LANES, (j + 1) * LANES)
        moved = own_ref[:, cols].astype(f32) + lax.dot_general(got, put, NT, preferred_element_type=f32)
        kappa = (moved * dc_ref[0:1, cols]).reshape(8, 8, 8, LANES)
        for r in range(8):
            for s in range(8):
                wk_ref[j, r, s] = rows[r][s] * kappa[r, s]
    rows = lambda j: wk_ref[j].reshape(512, LANES)
    behind_ref[...], ahead_ref[...] = send_rims(rows, rows, na)


def lines_t(k_ref, blocks):
    out = []
    for p in range(0, len(blocks), 2):
        pair = jnp.concatenate(blocks[p : p + 2], 1)
        high = pair.astype(bf16)
        low = (pair - high.astype(f32)).astype(bf16)
        y = jnp.dot(k_ref[...], jnp.concatenate([high, low], 0), preferred_element_type=f32)
        y = y[:128] + y[128:]
        out += [y[:, n * LANES : (n + 1) * LANES].reshape(2, 8, 8, LANES) for n in range(len(blocks[p : p + 2]))]
    return out


def blocks_of(x):
    x = x.reshape(4, 128, LANES)
    return [x[n] for n in range(4)]


def squares(v, j, other, iw_ref):
    sums = {}
    for r in range(8):
        for s in range(8):
            key = (0 if r == 0 else 2 if r == 7 else 1, 0 if s == 0 else 2 if s == 7 else 1)
            x = v[j, r, s]
            pair = (x * x,) if other is None else (x * x, x * other[j, r, s])
            old = sums.get((key, r))
            sums[(key, r)] = pair if old is None else tuple(a + b for a, b in zip(old, pair))
    total = None
    for (key, _), pair in sums.items():
        weight = iw_ref[j, key[0] * 3 + key[1]]
        pair = tuple(weight * a for a in pair)
        total = pair if total is None else tuple(a + b for a, b in zip(total, pair))
    return total


def gradient_r(v, j, g):
    for s in range(8):
        for r, value in enumerate(along(DERIV, [v[j, r, s] for r in range(8)])):
            g[r, s] = value


def fluxes(v, j, wk, c, g, f1, f2):
    gradient_r(v, j, g)
    for r in range(8):
        second = along(DERIV, [v[j, r, s] for s in range(8)])
        k = wk(r)
        for s in range(8):
            first = g[r, s]
            f2[j, r, s] = k[s] * (second[s] + c * first)
            f1[j, r, s] = k[s] * (first + c * second[s])


def lateral_faces(na, par_ref, v, wk, f1, f2, base, kf_ref, kb_ref, a_ref, b_ref):
    rows = [[(l * na + at, 7 * l) for at in range(na)] + [(2 * na, 7 * l)] for l in range(2)]
    flat = rows[0] + rows[1]

    def lines(k_ref, xs):
        blocks = []
        for n in range(0, len(xs), 2):
            blocks.append(jnp.concatenate([x.reshape(64, LANES) for x in xs[n : n + 2]], 0))
        out = []
        for part in lines_t(k_ref, blocks):
            part = part.reshape(2, 8, 8, LANES)
            out += [part[0], part[1]]
        return out

    thirds = lines(kf_ref, [v[j, :, s] for j, s in flat])
    scaled = []
    for (j, s), third in zip(flat, thirds):
        scaled.append(jnp.stack([wk(j, r, s) * third[r] for r in range(8)]))
    thirds = lines(kb_ref, scaled)
    faces = []
    for (j, s), third in zip(flat, thirds):
        first = along(DERIV.T, [f1[j, r, s] for r in range(8)])
        face = []
        for r in range(8):
            second = sum(float(DERIV[i, s]) * f2[j, r, i] for i in range(8) if DERIV[i, s] != 0.0)
            face.append(second + (base[r] * float(GLL_W[s])) * v[j, r, s] + first[r] + third[r])
        faces.append(face)
    for l in range(2):
        row = faces[l * (na + 1) : (l + 1) * (na + 1)]
        far, near = axial_row(l, [x[7] for x in row], [x[0] for x in row])
        for x, last, start in zip(row, far, near):
            x[7], x[0] = last, start
    for at in range(na):
        for r in range(8):
            send_faces(par_ref, at * 8 + r, faces[at][r], faces[na + 1 + at][r], a_ref, b_ref)
    send_faces(par_ref, na * 8, pack_rim(faces[na], 0), pack_rim(faces[2 * na + 1], 1), a_ref, b_ref)


def mass_rows(wt, base):
    for r in range(8):
        base[r] = wt * float(GLL_W[r] * coolant_throughput * KRYLOV_SCALE)


def flux_kernel(na, first, *refs):
    refs = list(refs)
    take = lambda n: [refs.pop(0) for _ in range(n)]
    ghost = 2 * na
    if first:
        par_ref, _, wk_ref, b_in, a_in, dc_ref = take(6)
    else:
        par_ref, _, b_in, a_in, wk_ref, wkg_ref, cr_ref = take(7)
    wt_ref, kf_ref, kb_ref, v, f1, f2, a_out, b_out = take(8)
    if first:
        wkg_ref, cr_ref = take(2)
    g, base = refs
    if first:
        even = par_ref[5] == 0
        a, b = a_in[...], b_in[...]
        rims = place_rims(jnp.where(even, a, b), jnp.where(even, b, a))
        v[ghost] = rims[0:512].reshape(8, 8, 8, LANES)
        wkg_ref[...] = rims[640:1152].reshape(8, 8, 8, LANES)
        for j in range(ghost):
            cr_ref[j] = jnp.broadcast_to(dc_ref[1:2, j * LANES : (j + 1) * LANES], (8, LANES))
        cr_ref[ghost] = rims[512:520]
        assemble_axial(na, v)
    else:
        add_faces(na, par_ref, v, a_in, b_in)
    mass_rows(wt_ref[...], base)
    for j in range(ghost + 1):
        if j < ghost:
            wk = lambda r: wk_ref[j, r]
        else:
            wk = lambda r: wkg_ref[r]
        fluxes(v, j, wk, cr_ref[j], g.at[j % 2], f1, f2)
    face_wk = lambda j, r, s: wk_ref[j, r, s] if j < ghost else wkg_ref[r, s]
    lateral_faces(na, par_ref, v, face_wk, f1, f2, base, kf_ref, kb_ref, a_out, b_out)


def rest_kernel(na, first, *refs):
    refs = list(refs)
    prev = None if first else refs.pop(0)
    v, f1, f2, wk_ref, wkg_ref, wt_ref, iw_ref, kf_ref, kb_ref, y, dots, base, f3 = refs
    ghost = 2 * na
    mass_rows(wt_ref[...], base)
    totals = None
    for j in range(ghost + 1):
        if j < ghost:
            sums = squares(v, j, prev, iw_ref)
            totals = sums if totals is None else [a + b for a, b in zip(totals, sums)]
        for p, part in enumerate(lines_t(kf_ref, blocks_of(v[j]))):
            for q in range(2):
                r = 2 * p + q
                f3[j % 2, r] = (wk_ref[j, r] if j < ghost else wkg_ref[r]) * part[q]
        parts = lines_t(kb_ref, blocks_of(f3[j % 2]))
        for r in range(8):
            for s, value in enumerate(along(DERIV.T, [f2[j, r, s] for s in range(8)])):
                y[j, r, s] = value + (base[r] * float(GLL_W[s])) * v[j, r, s]
        for s in range(8):
            for r, value in enumerate(along(DERIV.T, [f1[j, r, s] for r in range(8)])):
                y[j, r, s] = y[j, r, s] + value + parts[r // 2][r % 2, s]
    for k, value in enumerate(totals):
        dots[k] = jnp.broadcast_to(jnp.sum(jnp.sum(value, 0, keepdims=True), 1, keepdims=True), (8, LANES))
    assemble_axial(na, y)
    assemble_lateral(na, y)


def last_kernel(na, par_ref, _, b_in, a_in, wk_ref, cr_ref, prev, wt_ref, iw_ref, kf_ref, d0, d1, d2, d3, v, all_dots, g, base):
    ghost = 2 * na
    add_faces(na, par_ref, v, a_in, b_in)
    mass_rows(wt_ref[...], base)
    totals = None
    for j in range(ghost):
        gj = g.at[j % 2]
        third = lines_t(kf_ref, blocks_of(v[j]))
        sums = list(squares(v, j, prev, iw_ref))
        gradient_r(v, j, gj)
        c = 2.0 * cr_ref[j]
        total = None
        for r in range(8):
            line = [v[j, r, s] for s in range(8)]
            second = along(DERIV, line)
            row = None
            for s in range(8):
                one, two, three = gj[r, s], second[s], third[r // 2][r % 2, s]
                term = (base[r] * float(GLL_W[s])) * (line[s] * line[s])
                term = term + wk_ref[j, r, s] * (one * (one + c * two) + two * two + three * three)
                row = term if row is None else row + term
            total = row if total is None else total + row
        sums.append(total)
        totals = sums if totals is None else [a + b for a, b in zip(totals, sums)]
    lane = lane_index(1)
    rows = [d0[0], d1[1], d1[0], d2[1], d2[0], d3[1], d3[0], totals[1], totals[0], totals[2]]
    out = jnp.zeros((1, LANES), f32)
    for k, row in enumerate(rows):
        if k < 2 * ITERS - 3:
            row = row[0:1]
        else:
            row = jnp.sum(jnp.sum(row, 0, keepdims=True), 1, keepdims=True)
        out = jnp.where(lane == k, row, out)
    all_dots[...] = jnp.broadcast_to(out[None], all_dots.shape)


def solve_moments(m_ref, coef_ref):
    sums = jnp.sum(m_ref[:, 0, :], 0, keepdims=True)
    lane = lane_index(1)
    m = [jnp.sum(jnp.where(lane == k, sums, 0.0), 1, keepdims=True) for k in range(2 * ITERS)]
    n = ITERS
    low = [[None] * n for _ in range(n)]
    diag = [None] * n
    for j in range(n):
        acc = [m[i + j + 1] for i in range(n)]
        for k in range(j):
            scaled = low[j][k] * diag[k]
            for i in range(j, n):
                acc[i] = acc[i] - low[i][k] * scaled
        diag[j] = acc[j]
        for i in range(j + 1, n):
            low[i][j] = acc[i] / acc[j]
    z = []
    for i in range(n):
        value = m[i]
        for k in range(i):
            value = value - low[i][k] * z[k]
        z.append(value)
    c = [z[i] / diag[i] for i in range(n)]
    for i in reversed(range(n)):
        for k in range(i + 1, n):
            c[i] = c[i] - low[k][i] * c[k]
    for k, x in enumerate(c):
        coef_ref[k] = jnp.broadcast_to(x * KRYLOV_SCALE, (8, LANES))


def combine_kernel(na, planes, m_ref, v0, v1, v2, v3, v4, out_ref, coef_ref):
    i = pl.program_id(0)

    @pl.when(i == 0)
    def _():
        solve_moments(m_ref, coef_ref)

    c = [coef_ref[k] for k in range(ITERS)]
    step = 2 * na
    for n in range(planes):
        r = i * planes + n
        for s in range(8):
            base = (n * 8 + s) * 8 * step
            for l in range(2):
                for at in range(na):
                    x = None
                    for coef, v in zip(c, (v0, v1, v2, v3, v4)):
                        term = coef * v[l * na + at, r, s]
                        x = term if x is None else x + term
                    out_ref[pl.ds(base + at * 2 + l, 8, stride=step), :] = x


def slab_swap(x, start):
    n, m = lax.axis_size("slab"), lax.axis_size("chan")
    pairs = [(i * m + c, (i + 1) * m + c) for i in range(start, n - 1, 2) for c in range(m)]
    busy = {i for pair in pairs for i in pair}
    pairs += [(i, i + 1) for i in range(0, n * m, 2) if i not in busy]
    return lax.ppermute(x, ("slab", "chan"), pairs + [(j, i) for i, j in pairs])


def swap(x, axis, start):
    n = lax.axis_size(axis)
    pairs = [((start + i) % n, (start + i + 1) % n) for i in range(0, n, 2)]
    return lax.ppermute(x, axis, pairs + [(j, i) for i, j in pairs])


def around(x, by):
    n = lax.axis_size("slab") * lax.axis_size("chan")
    return lax.ppermute(x, ("slab", "chan"), [(i, (i + by) % n) for i in range(n)])


def swap_around(x, start):
    n = lax.axis_size("slab") * lax.axis_size("chan")
    pairs = [((start + i) % n, (start + i + 1) % n) for i in range(0, n, 2)]
    return lax.ppermute(x, ("slab", "chan"), pairs + [(j, i) for i, j in pairs])


def product_weights(count_l, count_a):
    slab, chan = lax.axis_index("slab"), lax.axis_index("chan")
    axial = slab * count_a + jnp.arange(count_a)
    lateral = chan * count_l + jnp.arange(count_l)
    last_a = lax.axis_size("slab") * count_a - 1
    last_l = lax.axis_size("chan") * count_l - 1
    half = lambda cond: jnp.where(cond, 0.5, 1.0).astype(f32)
    along_a = jnp.stack([half(axial > 0), jnp.ones(count_a, f32), half(axial < last_a)])
    along_l = jnp.stack([half(lateral > 0), jnp.ones(count_l, f32), half(lateral < last_l)])
    weights = along_a[:, None, None, :] * along_l[None, :, :, None]
    weights = weights.reshape(9, -1, LANES).transpose(1, 0, 2)
    return jnp.broadcast_to(weights[:, :, None, :], weights.shape[:2] + (8, LANES))


def on_device(
    stream_speed_field,
    liquid_to_solid_element,
    previous_panel_warmth,
    pointwise_energy_source,
    coked_element_flags,
    coking_thickness_plies,
):
    count_l, count_a = coked_element_flags.shape
    assert count_l == 2 and count_a % LANES == 0
    elements = count_l * count_a
    na = count_a // LANES
    tiles = count_l * na
    chan = lax.axis_size("chan")
    total = lax.axis_size("slab") * chan
    slab_at, chan_at = lax.axis_index("slab"), lax.axis_index("chan")
    me = (slab_at * chan + chan_at).astype(jnp.int32).reshape(1)
    position = [
        chan_at % 2,
        chan_at > 0,
        chan_at < chan - 1,
        slab_at > 0,
        slab_at < lax.axis_size("slab") - 1,
        slab_at % 2,
    ]
    position = jnp.stack([jnp.asarray(x, jnp.int32) for x in position])

    wt = jnp.asarray(np.broadcast_to(GLL_W[:, None], (8, LANES)), f32)
    wr = jnp.asarray(np.broadcast_to((GLL_W[:, None] * GLL_W)[:, :, None], (8, 8, LANES)), f32)
    kf, kb = (jnp.asarray(k) for k in line_matrices())
    kfluid = jnp.asarray(fluid_matrix())

    layers = coking_thickness_plies.astype(f32)
    flags = coked_element_flags.astype(f32)
    damping = jnp.where(coked_element_flags == 1, 1.0 / (1.0 + layer_damp * layers), jnp.ones_like(layers))
    cross = cross_gain * flags * layers / (layers + 1.0)
    dc = jnp.stack([damping.reshape(elements), cross.reshape(elements)])
    iw = product_weights(count_l, count_a)

    def as_rows(x):
        x = x.reshape(8, 8, 8, count_l, na, LANES).transpose(0, 1, 2, 4, 3, 5)
        return x.reshape(512 * tiles, LANES)

    field = (tiles, 8, 8, 8, LANES)
    whole = (tiles + 1, 8, 8, 8, LANES)
    shape = lambda s, d=f32: jax.ShapeDtypeStruct(s, d)
    kept = vmem
    split = elements // LANES
    width = LANES
    room = elements // 4
    in_hbm = lambda x: pltpu.with_memory_space_constraint(x, pltpu.HBM)
    here = lambda: pl.BlockSpec(memory_space=pltpu.VMEM)
    scalars = pl.BlockSpec(memory_space=pltpu.SMEM)
    steps = 4
    rows = 512 * tiles // steps
    l2s = liquid_to_solid_element.reshape(1, elements)
    out = pl.pallas_call(
        functools.partial(fluid_kernel, na, 8 // split, chan, total),
        grid=(split,),
        in_specs=[
            scalars,
            scalars,
            pl.BlockSpec((3, 8, 8, 8, width), lambda i: (0, 0, 0, 0, i)),
            pl.BlockSpec((1, elements), lambda i: (0, 0)),
            pl.BlockSpec(kfluid.shape, lambda i: (0, 0)),
        ]
        + [pl.BlockSpec((512 * tiles // split, LANES), lambda i: (i, 0))] * 2
        + [pl.BlockSpec((8, 8, LANES), lambda i: (0, 0, 0))],
        out_specs=[pl.BlockSpec((3, 8, 8, 8, width), lambda i: (0, 0, 0, 0, i))] + [here()] * 7,
        out_shape=[shape(stream_speed_field.shape, bf16), kept((split, 512, width), bf16)]
        + [kept((528, room), bf16)] * 3
        + [kept(field), kept((na, 8, 8, LANES)), kept((na, 8, 8, LANES))],
        scratch_shapes=[pltpu.VMEM((3, 8, 8, 8, width), f32)] * 2,
        compiler_params=pltpu.CompilerParams(vmem_limit_bytes=24 * 1024 * 1024),
    )(
        me,
        position,
        in_hbm(stream_speed_field),
        in_hbm(l2s),
        in_hbm(kfluid),
        in_hbm(as_rows(previous_panel_warmth)),
        in_hbm(as_rows(pointwise_energy_source)),
        in_hbm(wr),
    )
    stepped, cond, out_even, out_odd, out_far, z, a, b = out
    received = [around(out_far, chan), swap_around(out_odd, 1), swap_around(out_even, 0)]
    (own,) = call(
        functools.partial(keep_kernel, chan, total), [kept((512, elements), bf16)], me, cond, l2s, smem=1
    )
    a, b, own = lax.optimization_barrier((a, b, own))
    b, a = swap(b, "chan", 1), swap(a, "chan", 0)
    wk, wk_behind, wk_ahead = call(
        functools.partial(unpack_kernel, na),
        [kept(field), kept((2 * RIM, 512)), kept((2 * RIM, 512))],
        own,
        *received,
        dc,
        wt,
    )
    y, a, b = call(
        functools.partial(rim_kernel, na),
        [kept(whole), kept((2 * RIM, 1152)), kept((2 * RIM, 1152))],
        position,
        z,
        b,
        a,
        dc,
        wk_behind,
        wk_ahead,
        smem=1,
    )
    b, a = slab_swap(b, 1), slab_swap(a, 0)

    basis, products = [], []
    face = (8 * na + 1, 8, LANES)
    for number in range(ITERS - 1):
        first = number == 0
        outs = [kept(whole)] * 3 + [kept(face)] * 2
        if first:
            args = (y, wk, b, a, dc)
            outs += [kept((8, 8, 8, LANES)), kept((tiles + 1, 8, LANES))]
        else:
            args = (y, b, a, wk, wkg, cr)
        got = call(
            functools.partial(flux_kernel, na, first),
            outs,
            position,
            *args,
            wt,
            kf,
            kb,
            smem=1,
            scratch=[pltpu.VMEM((2, 8, 8, 8, LANES), f32), pltpu.VMEM((8, 8, LANES), f32)],
            input_output_aliases={1: 0},
        )
        if first:
            wkg, cr = got[5:]
        v, f1, f2, a, b = got[:5]
        b, a = swap(b, "chan", 1), swap(a, "chan", 0)
        y, dots = call(
            functools.partial(rest_kernel, na, first),
            [kept(whole), kept((2, 8, LANES))],
            *basis[-1:],
            v,
            f1,
            f2,
            wk,
            wkg,
            wt,
            iw,
            kf,
            kb,
            scratch=[pltpu.VMEM((8, 8, LANES), f32), pltpu.VMEM((2, 8, 8, 8, LANES), f32)],
        )
        basis.append(v)
        products.append(dots)
    v, sums = call(
        functools.partial(last_kernel, na),
        [kept(whole), kept((total, 1, LANES))],
        position,
        y,
        b,
        a,
        wk,
        cr,
        basis[-1],
        wt,
        iw,
        kf,
        *products,
        smem=1,
        input_output_aliases={1: 0},
        scratch=[pltpu.VMEM((2, 8, 8, 8, LANES), f32), pltpu.VMEM((8, 8, LANES), f32)],
    )
    basis.append(v)
    sums = lax.all_to_all(sums, ("slab", "chan"), 0, 0)
    x = pl.pallas_call(
        functools.partial(combine_kernel, na, 8 // steps),
        grid=(steps,),
        in_specs=[here()] * 6,
        out_specs=pl.BlockSpec((rows, LANES), lambda i: (i, 0)),
        out_shape=shape((512 * tiles, LANES)),
        scratch_shapes=[pltpu.VMEM((ITERS, 8, LANES), f32)],
        compiler_params=pltpu.CompilerParams(vmem_limit_bytes=12 * 1024 * 1024),
    )(sums, *basis)
    x = x.reshape(8, 8, 8, na, count_l, LANES).transpose(0, 1, 2, 4, 3, 5)
    return stepped, x.reshape(8, 8, 8, count_l, count_a)


def solution(mesh):
    in_specs = (
        P(None, None, None, None, ("slab", "chan")),
        P(("slab", "chan")),
        P(None, None, None, "chan", "slab"),
        P(None, None, None, "chan", "slab"),
        P("chan", "slab"),
        P("chan", "slab"),
    )
    out_specs = (P(None, None, None, None, ("slab", "chan")), P(None, None, None, "chan", "slab"))
    return jax.shard_map(
        on_device, mesh=mesh, in_specs=in_specs, out_specs=out_specs, check_vma=False
    )
```

```python
import functools

import jax
import jax.numpy as jnp
import numpy as np
from jax import lax
from jax.experimental import pallas as pl
from jax.experimental.pallas import tpu as pltpu
from jax.sharding import PartitionSpec as P

ITERS = 5
LANES = 128
RIM = 4
KRYLOV_SCALE = 1.0 / 256.0

highest = lax.Precision.HIGHEST
f32 = jnp.float32
bf16 = jnp.bfloat16
coolant_throughput = 0.05
time_step = 0.01
viscosity = 0.02
cross_gain = 0.4
layer_damp = 0.25

NT = (((1,), (1,)), ((), ()))
TN = (((0,), (0,)), ((), ()))


def gll_tables():
    points = np.array(
        [
            -1.0,
            -0.8717401485096066,
            -0.5917001814331423,
            -0.2092992179024789,
            0.2092992179024789,
            0.5917001814331423,
            0.8717401485096066,
            1.0,
        ]
    )
    weights = np.array(
        [
            1.0 / 28.0,
            0.2107042271435061,
            0.3411226924835044,
            0.4124587946587038,
            0.4124587946587038,
            0.3411226924835044,
            0.2107042271435061,
            1.0 / 28.0,
        ]
    )
    lower_poly = np.ones(8)
    upper_poly = points.copy()
    for degree in range(1, 7):
        next_poly = ((2 * degree + 1) * points * upper_poly - degree * lower_poly) / (degree + 1)
        lower_poly = upper_poly
        upper_poly = next_poly
    gaps_matrix = points[:, None] - points[None, :] + np.eye(8)
    derivative = upper_poly[:, None] / (upper_poly[None, :] * gaps_matrix)
    derivative = derivative * (1.0 - np.eye(8))
    derivative[0, 0] = -14.0
    derivative[7, 7] = 14.0
    return derivative, weights


DERIV, GLL_W = gll_tables()
DERIV = DERIV.astype(np.float32).astype(np.float64)
GLL_W = GLL_W.astype(np.float32).astype(np.float64)


def split_hi_lo(matrix):
    high = np.asarray(matrix, np.float32).astype(jnp.bfloat16)
    low = (np.asarray(matrix, np.float64) - high.astype(np.float64)).astype(np.float32)
    return high, low.astype(jnp.bfloat16)


def line_matrices():
    out = []
    for matrix in (DERIV, DERIV.T):
        high, low = split_hi_lo(np.kron(np.eye(16), matrix))
        upper = np.concatenate([high, high], 1)
        out.append(np.concatenate([upper, np.concatenate([low, np.zeros_like(low)], 1)], 0))
    return out


def fluid_matrix():
    eye8 = np.eye(8)
    square = DERIV @ DERIV
    second = time_step * np.kron(DERIV, eye8)
    third = time_step * np.kron(eye8, DERIV)
    curve = np.eye(64) + time_step * viscosity * (np.kron(square, eye8) + np.kron(eye8, square))
    return np.concatenate([np.concatenate(split_hi_lo(np.kron(np.eye(2), m)), 1) for m in (second, third, curve)], 0)


def halves_of(line):
    return [line[j] + line[7 - j] for j in range(4)], [line[j] - line[7 - j] for j in range(4)]


def combined(matrix, parts, sign):
    even, odd = parts
    result = [None] * 8
    for i in range(4):
        p = sum(float(0.5 * (matrix[i, j] + matrix[i, 7 - j])) * even[j] for j in range(4))
        q = sum(float(0.5 * (matrix[i, j] - matrix[i, 7 - j])) * odd[j] for j in range(4))
        result[i] = p + q
        result[7 - i] = q - p if sign < 0 else p - q
    return result


def along(matrix, line):
    return combined(matrix, halves_of(line), -1)


def lane_index(rows=8):
    return lax.broadcasted_iota(jnp.int32, (rows, LANES), 1)


def vmem(shape, dtype=f32):
    return pltpu.VMEM(shape, dtype)


def call(kernel, out_shape, *args, smem=0, hbm=0, scratch=(), limit=12, **kw):
    specs = [pl.BlockSpec(memory_space=pltpu.SMEM)] * smem
    specs += [pl.BlockSpec(memory_space=pltpu.HBM)] * hbm
    specs += [pl.BlockSpec(memory_space=pltpu.VMEM)] * (len(args) - smem - hbm)
    outs = [pl.BlockSpec(memory_space=pltpu.VMEM) for _ in out_shape]
    return pl.pallas_call(
        kernel,
        in_specs=specs,
        out_specs=outs,
        out_shape=out_shape,
        scratch_shapes=scratch,
        compiler_params=pltpu.CompilerParams(vmem_limit_bytes=limit * 1024 * 1024),
        **kw,
    )(*args)


def weight_rows(wt):
    return [[float(GLL_W[r] * GLL_W[s]) * wt for s in range(8)] for r in range(8)]


def in_three(x):
    high = x.astype(bf16)
    rest = x - high.astype(f32)
    middle = rest.astype(bf16)
    return [high, middle, (rest - middle.astype(f32)).astype(bf16)]


def sel_matrix(l, first_lane):
    row = lax.broadcasted_iota(jnp.int32, (2 * RIM, LANES), 0)
    lane = lax.broadcasted_iota(jnp.int32, (2 * RIM, LANES), 1)
    inside = (row >= l * RIM) & (row < (l + 1) * RIM)
    return ((row - l * RIM + first_lane == lane) & inside).astype(f32)


def place_matrix(first_lane):
    row = lax.broadcasted_iota(jnp.int32, (2 * RIM, LANES), 0)
    lane = lax.broadcasted_iota(jnp.int32, (2 * RIM, LANES), 1)
    target = jnp.where(row < RIM, row + first_lane, row - RIM + first_lane + LANES // 2)
    return (target == lane).astype(f32)


def send_rims(near_rows, far_rows, na):
    def pick(tile_rows, tiles, first_lane):
        out = None
        for l, j in enumerate(tiles):
            terms = jnp.concatenate(in_three(tile_rows(j)), 1)
            sel = jnp.concatenate([sel_matrix(l, first_lane)] * 3, 1).astype(bf16)
            part = lax.dot_general(sel, terms, NT, preferred_element_type=f32)
            out = part if out is None else out + part
        return out

    return pick(near_rows, (0, na), 0), pick(far_rows, (na - 1, 2 * na - 1), LANES - RIM)


def place_rims(from_ahead, from_behind):
    terms = [x.astype(f32) for x in in_three(from_ahead) + in_three(from_behind)]
    places = [place_matrix(0)] * 3 + [place_matrix(LANES // 2 - RIM)] * 3
    terms = jnp.concatenate(terms, 0).astype(bf16)
    places = jnp.concatenate(places, 0).astype(bf16)
    return lax.dot_general(terms, places, TN, preferred_element_type=f32)


def source_planes(na, planes, par_ref, p_ref, q_ref, wr_ref, z_ref, a_ref, b_ref):
    step = 2 * na
    for n in range(planes):
        r = pl.program_id(0) * planes + n
        wr = wr_ref[r]
        ends = {}
        for s in range(8):
            base = (n * 8 + s) * 8 * step
            for l in range(2):
                for at in range(na):
                    pick = pl.ds(base + at * 2 + l, 8, stride=step)
                    value = (wr * float(GLL_W[s])) * (coolant_throughput * p_ref[pick, :] + q_ref[pick, :])
                    if (l, s) in ((0, 0), (0, 7), (1, 0), (1, 7)):
                        ends[l, s, at] = value
                    else:
                        z_ref[l * na + at, n, s] = value
        for at in range(na):
            shared = ends[0, 7, at] + ends[1, 0, at]
            z_ref[at, n, 7] = shared
            z_ref[na + at, n, 0] = shared
            lower, upper = ends[0, 0, at], ends[1, 7, at]
            z_ref[at, n, 0] = lower
            z_ref[na + at, n, 7] = upper
            send_faces(par_ref, (at, r), lower, upper, a_ref, b_ref)


def rim_kernel(na, par_ref, z_in, b_ref, a_ref, dc_ref, wkb_ref, wka_ref, v_ref, a_out, b_out):
    v_ref[0 : 2 * na] = z_in[...]
    for r in range(8):
        for at in range(na):
            lower, upper = got_faces(par_ref, (at, r), a_ref, b_ref)
            v_ref[at, r, 0] = v_ref[at, r, 0] + lower
            v_ref[na + at, r, 7] = v_ref[na + at, r, 7] + upper

    lane = lane_index()
    cross = lambda j: jnp.broadcast_to(dc_ref[1:2, j * LANES : (j + 1) * LANES], (LANES, LANES))

    def near_rows(j):
        rows = []
        for s in range(8):
            inner = pltpu.roll(v_ref[j, 0, s], LANES - 1, 1)
            rows.append(v_ref[j, 7, s] + jnp.where(lane == RIM - 1, inner, 0.0))
        return jnp.concatenate([v_ref[j, 0:7].reshape(448, LANES)] + rows + [cross(j)], 0)

    def far_rows(j):
        rows = []
        for s in range(8):
            inner = pltpu.roll(v_ref[j, 7, s], 1, 1)
            rows.append(v_ref[j, 0, s] + jnp.where(lane == LANES - RIM, inner, 0.0))
        return jnp.concatenate(rows + [v_ref[j, 1:8].reshape(448, LANES), cross(j)], 0)

    behind, ahead = send_rims(near_rows, far_rows, na)
    behind = jnp.where(par_ref[3] > 0, jnp.concatenate([behind, wkb_ref[...]], 1), 0.0)
    ahead = jnp.where(par_ref[4] > 0, jnp.concatenate([ahead, wka_ref[...]], 1), 0.0)
    even = par_ref[5] == 0
    a_out[...] = jnp.where(even, ahead, behind)
    b_out[...] = jnp.where(even, behind, ahead)


def send_faces(par_ref, at, lower, upper, a_ref, b_ref):
    even = par_ref[0] == 0
    lower = jnp.where(par_ref[1] > 0, lower, 0.0)
    upper = jnp.where(par_ref[2] > 0, upper, 0.0)
    a_ref[at] = jnp.where(even, upper, lower)
    b_ref[at] = jnp.where(even, lower, upper)


def got_faces(par_ref, at, a_ref, b_ref):
    even = par_ref[0] == 0
    a, b = a_ref[at], b_ref[at]
    return jnp.where(even, b, a), jnp.where(even, a, b)


def axial_row(l, far, near):
    ghost = len(far) - 1
    lane = lane_index()
    half = LANES // 2
    roll = pltpu.roll
    right = [roll(x, 1, 1) for x in far]
    left = [roll(x, LANES - 1, 1) for x in near]
    new_far, new_near = [], []
    for at in range(ghost):
        if at > 0:
            carry = right[at - 1]
        else:
            carry = roll(far[ghost], half + 1, 1) if l == 0 else right[ghost]
        new_near.append(near[at] + jnp.where(lane == 0, carry, right[at]))
        if at < ghost - 1:
            carry = left[at + 1]
        else:
            carry = left[ghost] if l == 0 else roll(near[ghost], half - 1, 1)
        new_far.append(far[at] + jnp.where(lane == LANES - 1, carry, left[at]))
    carry = right[ghost - 1] if l == 0 else roll(far[ghost - 1], half + 1, 1)
    new_near.append(near[ghost] + jnp.where(lane == half * l, carry, right[ghost]))
    carry = roll(near[0], half - 1, 1) if l == 0 else left[0]
    new_far.append(far[ghost] + jnp.where(lane == half * (l + 1) - 1, carry, left[ghost]))
    return new_far, new_near


def assemble_axial(na, y):
    ghost = 2 * na
    low = lane_index() < LANES // 2
    for s in range(8):
        rims = []
        for l in range(2):
            tiles = list(range(l * na, l * na + na)) + [ghost]
            far, near = axial_row(l, [y[j, 7, s] for j in tiles], [y[j, 0, s] for j in tiles])
            for n, j in enumerate(tiles[:-1]):
                y[j, 7, s] = far[n]
                y[j, 0, s] = near[n]
            rims.append((far[-1], near[-1]))
        y[ghost, 7, s] = jnp.where(low, rims[0][0], rims[1][0])
        y[ghost, 0, s] = jnp.where(low, rims[0][1], rims[1][1])


def assemble_lateral(na, y):
    ghost = 2 * na
    half = LANES // 2
    low = lane_index() < half
    for r in range(8):
        for at in range(na):
            shared = y[at, r, 7] + y[na + at, r, 0]
            y[at, r, 7] = shared
            y[na + at, r, 0] = shared
        upper = y[ghost, r, 7]
        lower = y[ghost, r, 0]
        y[ghost, r, 7] = upper + jnp.where(low, pltpu.roll(lower, half, 1), 0.0)
        y[ghost, r, 0] = lower + jnp.where(low, 0.0, pltpu.roll(upper, half, 1))


def turn(x, by):
    return x if by % LANES == 0 else pltpu.roll(x, by % LANES, 1)


def pack_rim(planes, l):
    lane = lane_index()
    half = LANES // 2
    out = None
    for r, x in enumerate(planes):
        at = 2 * RIM * r
        near = turn(x, at - half * l)
        far = turn(x, at + RIM - (half * (l + 1) - RIM))
        near = jnp.where((lane >= at) & (lane < at + RIM), near, 0.0)
        both = jnp.where((lane >= at + RIM) & (lane < at + 2 * RIM), far, near)
        out = both if out is None else out + both
    return out


def unpack_rim(x, r, l):
    lane = lane_index()
    half = LANES // 2
    at = 2 * RIM * r
    near = turn(x, half * l - at)
    far = turn(x, half * (l + 1) - RIM - (at + RIM))
    near = jnp.where((lane >= half * l) & (lane < half * l + RIM), near, 0.0)
    return jnp.where((lane >= half * (l + 1) - RIM) & (lane < half * (l + 1)), far, near)


def add_faces(na, par_ref, v, a_ref, b_ref):
    ghost = 2 * na
    for at in range(na):
        for r in range(8):
            lower, upper = got_faces(par_ref, at * 8 + r, a_ref, b_ref)
            v[at, r, 0] = v[at, r, 0] + lower
            v[na + at, r, 7] = v[na + at, r, 7] + upper
    lower, upper = got_faces(par_ref, na * 8, a_ref, b_ref)
    for r in range(8):
        v[ghost, r, 0] = v[ghost, r, 0] + unpack_rim(lower, r, 0)
        v[ghost, r, 7] = v[ghost, r, 7] + unpack_rim(upper, r, 1)


def owners(l2s, me, total, chan):
    elements = l2s.shape[1]
    if elements & (elements - 1) == 0:
        owner = lax.shift_right_logical(l2s, elements.bit_length() - 1)
        slot = l2s & (elements - 1)
    else:
        owner = l2s // elements
        slot = l2s - owner * elements
    ahead = owner - me
    ahead = jnp.where(ahead < 0, ahead + total, ahead)
    group = jnp.where(ahead == 1, 1, jnp.where(ahead == total - 1, 2, jnp.where(ahead == chan, 3, 0)))
    return slot, group


def fluid_kernel(
    na, planes, chan, total, me_ref, par_ref, u_ref, l2s_ref, k_ref, p_ref, q_ref, wr_ref,
    out_ref, cond_ref, s1_ref, s2_ref, s3_ref, z_ref, fa_ref, fb_ref, t_ref, uf_ref
):
    i = pl.program_id(0)
    k = k_ref[...]
    curve_matrix = time_step * viscosity * (DERIV @ DERIV)
    slope_matrix = time_step * DERIV
    for c in range(3):
        for s in range(8):
            line = [u_ref[c, r, s].astype(f32) for r in range(8)]
            for r in range(8):
                uf_ref[c, r, s] = line[r]
            parts = halves_of(line)
            slope = combined(slope_matrix, parts, -1)
            curve = combined(curve_matrix, parts, 1)
            for r in range(8):
                t_ref[c, r, s] = curve[r] - uf_ref[0, r, s] * slope[r]
    for p in range(2):
        speed = [None] * 32
        for c in range(3):
            x = uf_ref[c, 4 * p : 4 * p + 4].reshape(2, 128, LANES)
            x = jnp.concatenate([x[0], x[1]], 1).astype(bf16)
            y = jnp.dot(k, jnp.concatenate([x, x], 0), preferred_element_type=f32)
            for h in range(2):
                part = y[:, h * LANES : (h + 1) * LANES].reshape(3, 2, 8, 8, LANES)
                for q in range(2):
                    r = 4 * p + 2 * h + q
                    for s in range(8):
                        change = t_ref[c, r, s] - uf_ref[1, r, s] * part[0, q, s] - uf_ref[2, r, s] * part[1, q, s]
                        new = (part[2, q, s] + change).astype(bf16)
                        out_ref[c, r, s] = new
                        new = new.astype(f32)
                        n = (2 * h + q) * 8 + s
                        speed[n] = new * new if speed[n] is None else speed[n] + new * new
        for n, value in enumerate(speed):
            t_ref[0, 4 * p + n // 8, n % 8] = 1.0 + 0.5 * value
    cond_ref[i] = t_ref[0].reshape(512, LANES).astype(bf16)
    source_planes(na, planes, par_ref, p_ref, q_ref, wr_ref, z_ref, fa_ref, fb_ref)

    @pl.when(i == pl.num_programs(0) - 1)
    def _():
        elements = l2s_ref.shape[-1]
        cond = jnp.concatenate([cond_ref[n] for n in range(cond_ref.shape[0])], 1)
        slot, group = owners(l2s_ref[...], me_ref[0], total, chan)
        kinds = lax.broadcasted_iota(jnp.int32, (16, elements), 0)
        marks = (kinds == group).astype(f32).astype(bf16)
        before = lax.broadcasted_iota(jnp.int32, (elements, elements), 0) < lax.broadcasted_iota(
            jnp.int32, (elements, elements), 1
        )
        rank = jnp.dot(marks, before.astype(f32).astype(bf16), preferred_element_type=f32).astype(jnp.int32)
        high = lax.shift_right_logical(slot, 5)
        codes = jnp.concatenate(
            [jnp.broadcast_to(high, (8, elements)), jnp.broadcast_to(slot - high * 32, (8, elements))], 0
        )
        tagged = jnp.concatenate([cond, codes.astype(f32).astype(bf16)], 0)
        room = s1_ref.shape[-1]
        position = lax.broadcasted_iota(jnp.int32, (room, elements), 0)
        even = me_ref[0] % 2 == 0
        one, two = rank[1:2], rank[2:3]
        sends = (
            (jnp.where(even, 1, 2), jnp.where(even, one, two), s1_ref),
            (jnp.where(even, 2, 1), jnp.where(even, two, one), s2_ref),
            (3, rank[3:4], s3_ref),
        )
        for g, order, ref in sends:
            take = ((position == order) & (group == g)).astype(f32).astype(bf16)
            ref[...] = lax.dot_general(tagged, take, NT, preferred_element_type=f32).astype(bf16)


def keep_kernel(chan, total, me_ref, cond_ref, l2s_ref, own_ref):
    elements = l2s_ref.shape[-1]
    cond = jnp.concatenate([cond_ref[n] for n in range(cond_ref.shape[0])], 1)
    slot, group = owners(l2s_ref[...], me_ref[0], total, chan)
    place = lax.broadcasted_iota(jnp.int32, (elements, elements), 0)
    keep = ((place == slot) & (group == 0)).astype(f32).astype(bf16)
    own_ref[...] = lax.dot_general(cond, keep, NT, preferred_element_type=f32).astype(bf16)


def unpack_kernel(
    na, z_hbm, own_ref, r1_ref, r2_ref, r3_ref, dc_ref, wt_ref, wk_ref, behind_ref, ahead_ref, z_ref, sems
):
    copies = [pltpu.make_async_copy(z_hbm.at[j], z_ref.at[j], sems.at[j]) for j in range(2 * na)]
    for copy in copies:
        copy.start()
    rows = weight_rows(wt_ref[...] * KRYLOV_SCALE)
    got = jnp.concatenate([r[0:512] for r in (r1_ref, r2_ref, r3_ref)], 1)
    tags = [r[512:528].astype(f32) for r in (r1_ref, r2_ref, r3_ref)]
    slots = [(t[0:1] * 32.0 + t[8:9]).astype(jnp.int32) for t in tags]
    slot = jnp.concatenate(slots, 1)
    for j in range(2 * na):
        place = lax.broadcasted_iota(jnp.int32, (LANES, slot.shape[1]), 0) + j * LANES
        put = (place == slot).astype(f32).astype(bf16)
        cols = slice(j * LANES, (j + 1) * LANES)
        moved = own_ref[:, cols].astype(f32) + lax.dot_general(got, put, NT, preferred_element_type=f32)
        kappa = (moved * dc_ref[0:1, cols]).reshape(8, 8, 8, LANES)
        for r in range(8):
            for s in range(8):
                wk_ref[j, r, s] = rows[r][s] * kappa[r, s]
    rows = lambda j: wk_ref[j].reshape(512, LANES)
    behind_ref[...], ahead_ref[...] = send_rims(rows, rows, na)
    for copy in copies:
        copy.wait()


def lines_t(k_ref, blocks):
    out = []
    for p in range(0, len(blocks), 2):
        pair = jnp.concatenate(blocks[p : p + 2], 1)
        high = pair.astype(bf16)
        low = (pair - high.astype(f32)).astype(bf16)
        y = jnp.dot(k_ref[...], jnp.concatenate([high, low], 0), preferred_element_type=f32)
        y = y[:128] + y[128:]
        out += [y[:, n * LANES : (n + 1) * LANES].reshape(2, 8, 8, LANES) for n in range(len(blocks[p : p + 2]))]
    return out


def blocks_of(x):
    x = x.reshape(4, 128, LANES)
    return [x[n] for n in range(4)]


def squares(v, j, other, iw_ref):
    sums = {}
    for r in range(8):
        for s in range(8):
            key = (0 if r == 0 else 2 if r == 7 else 1, 0 if s == 0 else 2 if s == 7 else 1)
            x = v[j, r, s]
            pair = (x * x,) if other is None else (x * x, x * other[j, r, s])
            old = sums.get((key, r))
            sums[(key, r)] = pair if old is None else tuple(a + b for a, b in zip(old, pair))
    total = None
    for (key, _), pair in sums.items():
        weight = iw_ref[j, key[0] * 3 + key[1]]
        pair = tuple(weight * a for a in pair)
        total = pair if total is None else tuple(a + b for a, b in zip(total, pair))
    return total


def gradient_r(v, j, g):
    for s in range(8):
        for r, value in enumerate(along(DERIV, [v[j, r, s] for r in range(8)])):
            g[r, s] = value


def fluxes(v, j, wk, c, g, f1, f2):
    gradient_r(v, j, g)
    for r in range(8):
        second = along(DERIV, [v[j, r, s] for s in range(8)])
        k = wk(r)
        for s in range(8):
            first = g[r, s]
            f2[j, r, s] = k[s] * (second[s] + c * first)
            f1[j, r, s] = k[s] * (first + c * second[s])


def lateral_faces(na, par_ref, v, wk, f1, f2, base, kf_ref, kb_ref, a_ref, b_ref):
    rows = [[(l * na + at, 7 * l) for at in range(na)] + [(2 * na, 7 * l)] for l in range(2)]
    flat = rows[0] + rows[1]

    def lines(k_ref, xs):
        blocks = []
        for n in range(0, len(xs), 2):
            blocks.append(jnp.concatenate([x.reshape(64, LANES) for x in xs[n : n + 2]], 0))
        out = []
        for part in lines_t(k_ref, blocks):
            part = part.reshape(2, 8, 8, LANES)
            out += [part[0], part[1]]
        return out

    thirds = lines(kf_ref, [v[j, :, s] for j, s in flat])
    scaled = []
    for (j, s), third in zip(flat, thirds):
        scaled.append(jnp.stack([wk(j, r, s) * third[r] for r in range(8)]))
    thirds = lines(kb_ref, scaled)
    faces = []
    for (j, s), third in zip(flat, thirds):
        first = along(DERIV.T, [f1[j, r, s] for r in range(8)])
        face = []
        for r in range(8):
            second = sum(float(DERIV[i, s]) * f2[j, r, i] for i in range(8) if DERIV[i, s] != 0.0)
            face.append(second + (base[r] * float(GLL_W[s])) * v[j, r, s] + first[r] + third[r])
        faces.append(face)
    for l in range(2):
        row = faces[l * (na + 1) : (l + 1) * (na + 1)]
        far, near = axial_row(l, [x[7] for x in row], [x[0] for x in row])
        for x, last, start in zip(row, far, near):
            x[7], x[0] = last, start
    for at in range(na):
        for r in range(8):
            send_faces(par_ref, at * 8 + r, faces[at][r], faces[na + 1 + at][r], a_ref, b_ref)
    send_faces(par_ref, na * 8, pack_rim(faces[na], 0), pack_rim(faces[2 * na + 1], 1), a_ref, b_ref)


def mass_rows(wt, base):
    for r in range(8):
        base[r] = wt * float(GLL_W[r] * coolant_throughput * KRYLOV_SCALE)


def flux_kernel(na, first, *refs):
    refs = list(refs)
    take = lambda n: [refs.pop(0) for _ in range(n)]
    ghost = 2 * na
    if first:
        par_ref, _, wk_ref, b_in, a_in, dc_ref = take(6)
    else:
        par_ref, _, b_in, a_in, wk_ref, wkg_ref, cr_ref = take(7)
    wt_ref, kf_ref, kb_ref, v, f1, f2, a_out, b_out = take(8)
    if first:
        wkg_ref, cr_ref = take(2)
    g, base = refs
    if first:
        even = par_ref[5] == 0
        a, b = a_in[...], b_in[...]
        rims = place_rims(jnp.where(even, a, b), jnp.where(even, b, a))
        v[ghost] = rims[0:512].reshape(8, 8, 8, LANES)
        wkg_ref[...] = rims[640:1152].reshape(8, 8, 8, LANES)
        for j in range(ghost):
            cr_ref[j] = jnp.broadcast_to(dc_ref[1:2, j * LANES : (j + 1) * LANES], (8, LANES))
        cr_ref[ghost] = rims[512:520]
        assemble_axial(na, v)
    else:
        add_faces(na, par_ref, v, a_in, b_in)
    mass_rows(wt_ref[...], base)
    for j in range(ghost + 1):
        if j < ghost:
            wk = lambda r: wk_ref[j, r]
        else:
            wk = lambda r: wkg_ref[r]
        fluxes(v, j, wk, cr_ref[j], g.at[j % 2], f1, f2)
    face_wk = lambda j, r, s: wk_ref[j, r, s] if j < ghost else wkg_ref[r, s]
    lateral_faces(na, par_ref, v, face_wk, f1, f2, base, kf_ref, kb_ref, a_out, b_out)


def rest_kernel(na, first, *refs):
    refs = list(refs)
    prev = None if first else refs.pop(0)
    v, f1, f2, wk_ref, wkg_ref, wt_ref, iw_ref, kf_ref, kb_ref, y, dots, base, f3 = refs
    ghost = 2 * na
    mass_rows(wt_ref[...], base)
    totals = None
    for j in range(ghost + 1):
        if j < ghost:
            sums = squares(v, j, prev, iw_ref)
            totals = sums if totals is None else [a + b for a, b in zip(totals, sums)]
        for p, part in enumerate(lines_t(kf_ref, blocks_of(v[j]))):
            for q in range(2):
                r = 2 * p + q
                f3[j % 2, r] = (wk_ref[j, r] if j < ghost else wkg_ref[r]) * part[q]
        parts = lines_t(kb_ref, blocks_of(f3[j % 2]))
        for r in range(8):
            for s, value in enumerate(along(DERIV.T, [f2[j, r, s] for s in range(8)])):
                y[j, r, s] = value + (base[r] * float(GLL_W[s])) * v[j, r, s]
        for s in range(8):
            for r, value in enumerate(along(DERIV.T, [f1[j, r, s] for r in range(8)])):
                y[j, r, s] = y[j, r, s] + value + parts[r // 2][r % 2, s]
    for k, value in enumerate(totals):
        dots[k] = jnp.broadcast_to(jnp.sum(jnp.sum(value, 0, keepdims=True), 1, keepdims=True), (8, LANES))
    assemble_axial(na, y)
    assemble_lateral(na, y)


def last_kernel(na, par_ref, _, b_in, a_in, wk_ref, cr_ref, prev, wt_ref, iw_ref, kf_ref, d0, d1, d2, d3, v, all_dots, g, base):
    ghost = 2 * na
    add_faces(na, par_ref, v, a_in, b_in)
    mass_rows(wt_ref[...], base)
    totals = None
    for j in range(ghost):
        gj = g.at[j % 2]
        third = lines_t(kf_ref, blocks_of(v[j]))
        sums = list(squares(v, j, prev, iw_ref))
        gradient_r(v, j, gj)
        c = 2.0 * cr_ref[j]
        total = None
        for r in range(8):
            line = [v[j, r, s] for s in range(8)]
            second = along(DERIV, line)
            row = None
            for s in range(8):
                one, two, three = gj[r, s], second[s], third[r // 2][r % 2, s]
                term = (base[r] * float(GLL_W[s])) * (line[s] * line[s])
                term = term + wk_ref[j, r, s] * (one * (one + c * two) + two * two + three * three)
                row = term if row is None else row + term
            total = row if total is None else total + row
        sums.append(total)
        totals = sums if totals is None else [a + b for a, b in zip(totals, sums)]
    lane = lane_index(1)
    rows = [d0[0], d1[1], d1[0], d2[1], d2[0], d3[1], d3[0], totals[1], totals[0], totals[2]]
    out = jnp.zeros((1, LANES), f32)
    for k, row in enumerate(rows):
        if k < 2 * ITERS - 3:
            row = row[0:1]
        else:
            row = jnp.sum(jnp.sum(row, 0, keepdims=True), 1, keepdims=True)
        out = jnp.where(lane == k, row, out)
    all_dots[...] = jnp.broadcast_to(out[None], all_dots.shape)


def solve_moments(m_ref, coef_ref):
    sums = jnp.sum(m_ref[:, 0, :], 0, keepdims=True)
    lane = lane_index(1)
    m = [jnp.sum(jnp.where(lane == k, sums, 0.0), 1, keepdims=True) for k in range(2 * ITERS)]
    n = ITERS
    low = [[None] * n for _ in range(n)]
    diag = [None] * n
    for j in range(n):
        acc = [m[i + j + 1] for i in range(n)]
        for k in range(j):
            scaled = low[j][k] * diag[k]
            for i in range(j, n):
                acc[i] = acc[i] - low[i][k] * scaled
        diag[j] = acc[j]
        for i in range(j + 1, n):
            low[i][j] = acc[i] / acc[j]
    z = []
    for i in range(n):
        value = m[i]
        for k in range(i):
            value = value - low[i][k] * z[k]
        z.append(value)
    c = [z[i] / diag[i] for i in range(n)]
    for i in reversed(range(n)):
        for k in range(i + 1, n):
            c[i] = c[i] - low[k][i] * c[k]
    for k, x in enumerate(c):
        coef_ref[k] = jnp.broadcast_to(x * KRYLOV_SCALE, (8, LANES))


def combine_kernel(na, planes, m_ref, v0, v1, v2, v3, v4, out_ref, coef_ref):
    i = pl.program_id(0)

    @pl.when(i == 0)
    def _():
        solve_moments(m_ref, coef_ref)

    c = [coef_ref[k] for k in range(ITERS)]
    step = 2 * na
    for n in range(planes):
        r = i * planes + n
        for s in range(8):
            base = (n * 8 + s) * 8 * step
            for l in range(2):
                for at in range(na):
                    x = None
                    for coef, v in zip(c, (v0, v1, v2, v3, v4)):
                        term = coef * v[l * na + at, r, s]
                        x = term if x is None else x + term
                    out_ref[pl.ds(base + at * 2 + l, 8, stride=step), :] = x


def slab_swap(x, start):
    n, m = lax.axis_size("slab"), lax.axis_size("chan")
    pairs = [(i * m + c, (i + 1) * m + c) for i in range(start, n - 1, 2) for c in range(m)]
    busy = {i for pair in pairs for i in pair}
    pairs += [(i, i + 1) for i in range(0, n * m, 2) if i not in busy]
    return lax.ppermute(x, ("slab", "chan"), pairs + [(j, i) for i, j in pairs])


def swap(x, axis, start):
    n = lax.axis_size(axis)
    pairs = [((start + i) % n, (start + i + 1) % n) for i in range(0, n, 2)]
    return lax.ppermute(x, axis, pairs + [(j, i) for i, j in pairs])


def around(x, by):
    n = lax.axis_size("slab") * lax.axis_size("chan")
    return lax.ppermute(x, ("slab", "chan"), [(i, (i + by) % n) for i in range(n)])


def swap_around(x, start):
    n = lax.axis_size("slab") * lax.axis_size("chan")
    pairs = [((start + i) % n, (start + i + 1) % n) for i in range(0, n, 2)]
    return lax.ppermute(x, ("slab", "chan"), pairs + [(j, i) for i, j in pairs])


def product_weights(count_l, count_a):
    slab, chan = lax.axis_index("slab"), lax.axis_index("chan")
    axial = slab * count_a + jnp.arange(count_a)
    lateral = chan * count_l + jnp.arange(count_l)
    last_a = lax.axis_size("slab") * count_a - 1
    last_l = lax.axis_size("chan") * count_l - 1
    half = lambda cond: jnp.where(cond, 0.5, 1.0).astype(f32)
    along_a = jnp.stack([half(axial > 0), jnp.ones(count_a, f32), half(axial < last_a)])
    along_l = jnp.stack([half(lateral > 0), jnp.ones(count_l, f32), half(lateral < last_l)])
    weights = along_a[:, None, None, :] * along_l[None, :, :, None]
    weights = weights.reshape(9, -1, LANES).transpose(1, 0, 2)
    return jnp.broadcast_to(weights[:, :, None, :], weights.shape[:2] + (8, LANES))


def on_device(
    stream_speed_field,
    liquid_to_solid_element,
    previous_panel_warmth,
    pointwise_energy_source,
    coked_element_flags,
    coking_thickness_plies,
):
    count_l, count_a = coked_element_flags.shape
    assert count_l == 2 and count_a % LANES == 0
    elements = count_l * count_a
    na = count_a // LANES
    tiles = count_l * na
    chan = lax.axis_size("chan")
    total = lax.axis_size("slab") * chan
    slab_at, chan_at = lax.axis_index("slab"), lax.axis_index("chan")
    me = (slab_at * chan + chan_at).astype(jnp.int32).reshape(1)
    position = [
        chan_at % 2,
        chan_at > 0,
        chan_at < chan - 1,
        slab_at > 0,
        slab_at < lax.axis_size("slab") - 1,
        slab_at % 2,
    ]
    position = jnp.stack([jnp.asarray(x, jnp.int32) for x in position])

    wt = jnp.asarray(np.broadcast_to(GLL_W[:, None], (8, LANES)), f32)
    wr = jnp.asarray(np.broadcast_to((GLL_W[:, None] * GLL_W)[:, :, None], (8, 8, LANES)), f32)
    kf, kb = (jnp.asarray(k) for k in line_matrices())
    kfluid = jnp.asarray(fluid_matrix())

    layers = coking_thickness_plies.astype(f32)
    flags = coked_element_flags.astype(f32)
    damping = jnp.where(coked_element_flags == 1, 1.0 / (1.0 + layer_damp * layers), jnp.ones_like(layers))
    cross = cross_gain * flags * layers / (layers + 1.0)
    dc = jnp.stack([damping.reshape(elements), cross.reshape(elements)])
    iw = product_weights(count_l, count_a)

    def as_rows(x):
        x = x.reshape(8, 8, 8, count_l, na, LANES).transpose(0, 1, 2, 4, 3, 5)
        return x.reshape(512 * tiles, LANES)

    field = (tiles, 8, 8, 8, LANES)
    whole = (tiles + 1, 8, 8, 8, LANES)
    shape = lambda s, d=f32: jax.ShapeDtypeStruct(s, d)
    kept = vmem
    split = elements // LANES
    width = LANES
    room = elements // 4
    in_hbm = lambda x: pltpu.with_memory_space_constraint(x, pltpu.HBM)
    here = lambda: pl.BlockSpec(memory_space=pltpu.VMEM)
    scalars = pl.BlockSpec(memory_space=pltpu.SMEM)
    steps = 4
    rows = 512 * tiles // steps
    l2s = liquid_to_solid_element.reshape(1, elements)
    out = pl.pallas_call(
        functools.partial(fluid_kernel, na, 8 // split, chan, total),
        grid=(split,),
        in_specs=[
            scalars,
            scalars,
            pl.BlockSpec((3, 8, 8, 8, width), lambda i: (0, 0, 0, 0, i)),
            pl.BlockSpec((1, elements), lambda i: (0, 0)),
            pl.BlockSpec(kfluid.shape, lambda i: (0, 0)),
        ]
        + [pl.BlockSpec((512 * tiles // split, LANES), lambda i: (i, 0))] * 2
        + [pl.BlockSpec((8, 8, LANES), lambda i: (0, 0, 0))],
        out_specs=[pl.BlockSpec((3, 8, 8, 8, width), lambda i: (0, 0, 0, 0, i))]
        + [here()] * 4
        + [pl.BlockSpec((tiles, 8 // split, 8, 8, LANES), lambda i: (0, i, 0, 0, 0))]
        + [here()] * 2,
        out_shape=[shape(stream_speed_field.shape, bf16), kept((split, 512, width), bf16)]
        + [kept((528, room), bf16)] * 3
        + [pltpu.HBM(field, f32), kept((na, 8, 8, LANES)), kept((na, 8, 8, LANES))],
        scratch_shapes=[pltpu.VMEM((3, 8, 8, 8, width), f32)] * 2,
        compiler_params=pltpu.CompilerParams(vmem_limit_bytes=24 * 1024 * 1024),
    )(
        me,
        position,
        in_hbm(stream_speed_field),
        in_hbm(l2s),
        in_hbm(kfluid),
        in_hbm(as_rows(previous_panel_warmth)),
        in_hbm(as_rows(pointwise_energy_source)),
        in_hbm(wr),
    )
    stepped, cond, out_even, out_odd, out_far, z, a, b = out
    received = [around(out_far, chan), swap_around(out_odd, 1), swap_around(out_even, 0)]
    (own,) = call(
        functools.partial(keep_kernel, chan, total), [kept((512, elements), bf16)], me, cond, l2s, smem=1
    )
    a, b, own = lax.optimization_barrier((a, b, own))
    b, a = swap(b, "chan", 1), swap(a, "chan", 0)
    wk, wk_behind, wk_ahead, z = call(
        functools.partial(unpack_kernel, na),
        [kept(field), kept((2 * RIM, 512)), kept((2 * RIM, 512)), kept(field)],
        in_hbm(z),
        own,
        *received,
        dc,
        wt,
        hbm=1,
        scratch=[pltpu.SemaphoreType.DMA((tiles,))],
    )
    y, a, b = call(
        functools.partial(rim_kernel, na),
        [kept(whole), kept((2 * RIM, 1152)), kept((2 * RIM, 1152))],
        position,
        z,
        b,
        a,
        dc,
        wk_behind,
        wk_ahead,
        smem=1,
    )
    b, a = slab_swap(b, 1), slab_swap(a, 0)

    basis, products = [], []
    face = (8 * na + 1, 8, LANES)
    for number in range(ITERS - 1):
        first = number == 0
        outs = [kept(whole)] * 3 + [kept(face)] * 2
        if first:
            args = (y, wk, b, a, dc)
            outs += [kept((8, 8, 8, LANES)), kept((tiles + 1, 8, LANES))]
        else:
            args = (y, b, a, wk, wkg, cr)
        got = call(
            functools.partial(flux_kernel, na, first),
            outs,
            position,
            *args,
            wt,
            kf,
            kb,
            smem=1,
            scratch=[pltpu.VMEM((2, 8, 8, 8, LANES), f32), pltpu.VMEM((8, 8, LANES), f32)],
            input_output_aliases={1: 0},
        )
        if first:
            wkg, cr = got[5:]
        v, f1, f2, a, b = got[:5]
        b, a = swap(b, "chan", 1), swap(a, "chan", 0)
        y, dots = call(
            functools.partial(rest_kernel, na, first),
            [kept(whole), kept((2, 8, LANES))],
            *basis[-1:],
            v,
            f1,
            f2,
            wk,
            wkg,
            wt,
            iw,
            kf,
            kb,
            scratch=[pltpu.VMEM((8, 8, LANES), f32), pltpu.VMEM((2, 8, 8, 8, LANES), f32)],
        )
        basis.append(v)
        products.append(dots)
    v, sums = call(
        functools.partial(last_kernel, na),
        [kept(whole), kept((total, 1, LANES))],
        position,
        y,
        b,
        a,
        wk,
        cr,
        basis[-1],
        wt,
        iw,
        kf,
        *products,
        smem=1,
        input_output_aliases={1: 0},
        scratch=[pltpu.VMEM((2, 8, 8, 8, LANES), f32), pltpu.VMEM((8, 8, LANES), f32)],
    )
    basis.append(v)
    sums = lax.all_to_all(sums, ("slab", "chan"), 0, 0)
    x = pl.pallas_call(
        functools.partial(combine_kernel, na, 8 // steps),
        grid=(steps,),
        in_specs=[here()] * 6,
        out_specs=pl.BlockSpec((rows, LANES), lambda i: (i, 0)),
        out_shape=shape((512 * tiles, LANES)),
        scratch_shapes=[pltpu.VMEM((ITERS, 8, LANES), f32)],
        compiler_params=pltpu.CompilerParams(vmem_limit_bytes=12 * 1024 * 1024),
    )(sums, *basis)
    x = x.reshape(8, 8, 8, na, count_l, LANES).transpose(0, 1, 2, 4, 3, 5)
    return stepped, x.reshape(8, 8, 8, count_l, count_a)


def solution(mesh):
    in_specs = (
        P(None, None, None, None, ("slab", "chan")),
        P(("slab", "chan")),
        P(None, None, None, "chan", "slab"),
        P(None, None, None, "chan", "slab"),
        P("chan", "slab"),
        P("chan", "slab"),
    )
    out_specs = (P(None, None, None, None, ("slab", "chan")), P(None, None, None, "chan", "slab"))
    return jax.shard_map(
        on_device, mesh=mesh, in_specs=in_specs, out_specs=out_specs, check_vma=False
    )
```

```python
import functools

import jax
import jax.numpy as jnp
import numpy as np
from jax import lax
from jax.experimental import pallas as pl
from jax.experimental.pallas import tpu as pltpu
from jax.sharding import PartitionSpec as P

ITERS = 5
LANES = 128
RIM = 4
KRYLOV_SCALE = 1.0 / 256.0

highest = lax.Precision.HIGHEST
f32 = jnp.float32
bf16 = jnp.bfloat16
coolant_throughput = 0.05
time_step = 0.01
viscosity = 0.02
cross_gain = 0.4
layer_damp = 0.25

NT = (((1,), (1,)), ((), ()))
TN = (((0,), (0,)), ((), ()))


def gll_tables():
    points = np.array(
        [
            -1.0,
            -0.8717401485096066,
            -0.5917001814331423,
            -0.2092992179024789,
            0.2092992179024789,
            0.5917001814331423,
            0.8717401485096066,
            1.0,
        ]
    )
    weights = np.array(
        [
            1.0 / 28.0,
            0.2107042271435061,
            0.3411226924835044,
            0.4124587946587038,
            0.4124587946587038,
            0.3411226924835044,
            0.2107042271435061,
            1.0 / 28.0,
        ]
    )
    lower_poly = np.ones(8)
    upper_poly = points.copy()
    for degree in range(1, 7):
        next_poly = ((2 * degree + 1) * points * upper_poly - degree * lower_poly) / (degree + 1)
        lower_poly = upper_poly
        upper_poly = next_poly
    gaps_matrix = points[:, None] - points[None, :] + np.eye(8)
    derivative = upper_poly[:, None] / (upper_poly[None, :] * gaps_matrix)
    derivative = derivative * (1.0 - np.eye(8))
    derivative[0, 0] = -14.0
    derivative[7, 7] = 14.0
    return derivative, weights


DERIV, GLL_W = gll_tables()
DERIV = DERIV.astype(np.float32).astype(np.float64)
GLL_W = GLL_W.astype(np.float32).astype(np.float64)


def split_hi_lo(matrix):
    high = np.asarray(matrix, np.float32).astype(jnp.bfloat16)
    low = (np.asarray(matrix, np.float64) - high.astype(np.float64)).astype(np.float32)
    return high, low.astype(jnp.bfloat16)


def line_matrices():
    out = []
    for matrix in (DERIV, DERIV.T):
        high, low = split_hi_lo(np.kron(np.eye(16), matrix))
        upper = np.concatenate([high, high], 1)
        out.append(np.concatenate([upper, np.concatenate([low, np.zeros_like(low)], 1)], 0))
    return out


def fluid_matrix():
    eye8 = np.eye(8)
    square = DERIV @ DERIV
    second = time_step * np.kron(DERIV, eye8)
    third = time_step * np.kron(eye8, DERIV)
    curve = np.eye(64) + time_step * viscosity * (np.kron(square, eye8) + np.kron(eye8, square))
    return np.concatenate([np.concatenate(split_hi_lo(np.kron(np.eye(2), m)), 1) for m in (second, third, curve)], 0)


def halves_of(line):
    return [line[j] + line[7 - j] for j in range(4)], [line[j] - line[7 - j] for j in range(4)]


def combined(matrix, parts, sign):
    even, odd = parts
    result = [None] * 8
    for i in range(4):
        p = sum(float(0.5 * (matrix[i, j] + matrix[i, 7 - j])) * even[j] for j in range(4))
        q = sum(float(0.5 * (matrix[i, j] - matrix[i, 7 - j])) * odd[j] for j in range(4))
        result[i] = p + q
        result[7 - i] = q - p if sign < 0 else p - q
    return result


def along(matrix, line):
    return combined(matrix, halves_of(line), -1)


def lane_index(rows=8):
    return lax.broadcasted_iota(jnp.int32, (rows, LANES), 1)


def vmem(shape, dtype=f32):
    return pltpu.VMEM(shape, dtype)


def call(kernel, out_shape, *args, smem=0, hbm=0, scratch=(), limit=12, **kw):
    specs = [pl.BlockSpec(memory_space=pltpu.SMEM)] * smem
    specs += [pl.BlockSpec(memory_space=pltpu.HBM)] * hbm
    specs += [pl.BlockSpec(memory_space=pltpu.VMEM)] * (len(args) - smem - hbm)
    outs = [pl.BlockSpec(memory_space=pltpu.VMEM) for _ in out_shape]
    return pl.pallas_call(
        kernel,
        in_specs=specs,
        out_specs=outs,
        out_shape=out_shape,
        scratch_shapes=scratch,
        compiler_params=pltpu.CompilerParams(vmem_limit_bytes=limit * 1024 * 1024),
        **kw,
    )(*args)


def weight_rows(wt):
    return [[float(GLL_W[r] * GLL_W[s]) * wt for s in range(8)] for r in range(8)]


def in_three(x):
    high = x.astype(bf16)
    rest = x - high.astype(f32)
    middle = rest.astype(bf16)
    return [high, middle, (rest - middle.astype(f32)).astype(bf16)]


def sel_matrix(l, first_lane):
    row = lax.broadcasted_iota(jnp.int32, (2 * RIM, LANES), 0)
    lane = lax.broadcasted_iota(jnp.int32, (2 * RIM, LANES), 1)
    inside = (row >= l * RIM) & (row < (l + 1) * RIM)
    return ((row - l * RIM + first_lane == lane) & inside).astype(f32)


def place_matrix(first_lane):
    row = lax.broadcasted_iota(jnp.int32, (2 * RIM, LANES), 0)
    lane = lax.broadcasted_iota(jnp.int32, (2 * RIM, LANES), 1)
    target = jnp.where(row < RIM, row + first_lane, row - RIM + first_lane + LANES // 2)
    return (target == lane).astype(f32)


def send_rims(near_rows, far_rows, na):
    def pick(tile_rows, tiles, first_lane):
        out = None
        for l, j in enumerate(tiles):
            terms = jnp.concatenate(in_three(tile_rows(j)), 1)
            sel = jnp.concatenate([sel_matrix(l, first_lane)] * 3, 1).astype(bf16)
            part = lax.dot_general(sel, terms, NT, preferred_element_type=f32)
            out = part if out is None else out + part
        return out

    return pick(near_rows, (0, na), 0), pick(far_rows, (na - 1, 2 * na - 1), LANES - RIM)


def place_rims(from_ahead, from_behind):
    terms = [x.astype(f32) for x in in_three(from_ahead) + in_three(from_behind)]
    places = [place_matrix(0)] * 3 + [place_matrix(LANES // 2 - RIM)] * 3
    terms = jnp.concatenate(terms, 0).astype(bf16)
    places = jnp.concatenate(places, 0).astype(bf16)
    return lax.dot_general(terms, places, TN, preferred_element_type=f32)


def source_planes(na, planes, par_ref, p_ref, q_ref, wr_ref, z_ref, a_ref, b_ref):
    step = 2 * na
    for n in range(planes):
        r = pl.program_id(0) * planes + n
        wr = wr_ref[r]
        ends = {}
        for s in range(8):
            base = (n * 8 + s) * 8 * step
            for l in range(2):
                for at in range(na):
                    pick = pl.ds(base + at * 2 + l, 8, stride=step)
                    value = (wr * float(GLL_W[s])) * (coolant_throughput * p_ref[pick, :] + q_ref[pick, :])
                    if (l, s) in ((0, 0), (0, 7), (1, 0), (1, 7)):
                        ends[l, s, at] = value
                    else:
                        z_ref[l * na + at, n, s] = value
        for at in range(na):
            shared = ends[0, 7, at] + ends[1, 0, at]
            z_ref[at, n, 7] = shared
            z_ref[na + at, n, 0] = shared
            lower, upper = ends[0, 0, at], ends[1, 7, at]
            z_ref[at, n, 0] = lower
            z_ref[na + at, n, 7] = upper
            send_faces(par_ref, (at, r), lower, upper, a_ref, b_ref)


def rim_kernel(na, par_ref, z_in, b_ref, a_ref, dc_ref, wkb_ref, wka_ref, v_ref, a_out, b_out):
    v_ref[0 : 2 * na] = z_in[...]
    for r in range(8):
        for at in range(na):
            lower, upper = got_faces(par_ref, (at, r), a_ref, b_ref)
            v_ref[at, r, 0] = v_ref[at, r, 0] + lower
            v_ref[na + at, r, 7] = v_ref[na + at, r, 7] + upper

    lane = lane_index()
    cross = lambda j: jnp.broadcast_to(dc_ref[1:2, j * LANES : (j + 1) * LANES], (LANES, LANES))

    def near_rows(j):
        rows = []
        for s in range(8):
            inner = pltpu.roll(v_ref[j, 0, s], LANES - 1, 1)
            rows.append(v_ref[j, 7, s] + jnp.where(lane == RIM - 1, inner, 0.0))
        return jnp.concatenate([v_ref[j, 0:7].reshape(448, LANES)] + rows + [cross(j)], 0)

    def far_rows(j):
        rows = []
        for s in range(8):
            inner = pltpu.roll(v_ref[j, 7, s], 1, 1)
            rows.append(v_ref[j, 0, s] + jnp.where(lane == LANES - RIM, inner, 0.0))
        return jnp.concatenate(rows + [v_ref[j, 1:8].reshape(448, LANES), cross(j)], 0)

    behind, ahead = send_rims(near_rows, far_rows, na)
    behind = jnp.where(par_ref[3] > 0, jnp.concatenate([behind, wkb_ref[...]], 1), 0.0)
    ahead = jnp.where(par_ref[4] > 0, jnp.concatenate([ahead, wka_ref[...]], 1), 0.0)
    even = par_ref[5] == 0
    a_out[...] = jnp.where(even, ahead, behind)
    b_out[...] = jnp.where(even, behind, ahead)


def send_faces(par_ref, at, lower, upper, a_ref, b_ref):
    even = par_ref[0] == 0
    lower = jnp.where(par_ref[1] > 0, lower, 0.0)
    upper = jnp.where(par_ref[2] > 0, upper, 0.0)
    a_ref[at] = jnp.where(even, upper, lower)
    b_ref[at] = jnp.where(even, lower, upper)


def got_faces(par_ref, at, a_ref, b_ref):
    even = par_ref[0] == 0
    a, b = a_ref[at], b_ref[at]
    return jnp.where(even, b, a), jnp.where(even, a, b)


def axial_row(l, far, near):
    ghost = len(far) - 1
    lane = lane_index()
    half = LANES // 2
    roll = pltpu.roll
    right = [roll(x, 1, 1) for x in far]
    left = [roll(x, LANES - 1, 1) for x in near]
    new_far, new_near = [], []
    for at in range(ghost):
        if at > 0:
            carry = right[at - 1]
        else:
            carry = roll(far[ghost], half + 1, 1) if l == 0 else right[ghost]
        new_near.append(near[at] + jnp.where(lane == 0, carry, right[at]))
        if at < ghost - 1:
            carry = left[at + 1]
        else:
            carry = left[ghost] if l == 0 else roll(near[ghost], half - 1, 1)
        new_far.append(far[at] + jnp.where(lane == LANES - 1, carry, left[at]))
    carry = right[ghost - 1] if l == 0 else roll(far[ghost - 1], half + 1, 1)
    new_near.append(near[ghost] + jnp.where(lane == half * l, carry, right[ghost]))
    carry = roll(near[0], half - 1, 1) if l == 0 else left[0]
    new_far.append(far[ghost] + jnp.where(lane == half * (l + 1) - 1, carry, left[ghost]))
    return new_far, new_near


def assemble_axial(na, y):
    ghost = 2 * na
    low = lane_index() < LANES // 2
    for s in range(8):
        rims = []
        for l in range(2):
            tiles = list(range(l * na, l * na + na)) + [ghost]
            far, near = axial_row(l, [y[j, 7, s] for j in tiles], [y[j, 0, s] for j in tiles])
            for n, j in enumerate(tiles[:-1]):
                y[j, 7, s] = far[n]
                y[j, 0, s] = near[n]
            rims.append((far[-1], near[-1]))
        y[ghost, 7, s] = jnp.where(low, rims[0][0], rims[1][0])
        y[ghost, 0, s] = jnp.where(low, rims[0][1], rims[1][1])


def assemble_lateral(na, y):
    ghost = 2 * na
    half = LANES // 2
    low = lane_index() < half
    for r in range(8):
        for at in range(na):
            shared = y[at, r, 7] + y[na + at, r, 0]
            y[at, r, 7] = shared
            y[na + at, r, 0] = shared
        upper = y[ghost, r, 7]
        lower = y[ghost, r, 0]
        y[ghost, r, 7] = upper + jnp.where(low, pltpu.roll(lower, half, 1), 0.0)
        y[ghost, r, 0] = lower + jnp.where(low, 0.0, pltpu.roll(upper, half, 1))


def turn(x, by):
    return x if by % LANES == 0 else pltpu.roll(x, by % LANES, 1)


def pack_rim(planes, l):
    lane = lane_index()
    half = LANES // 2
    out = None
    for r, x in enumerate(planes):
        at = 2 * RIM * r
        near = turn(x, at - half * l)
        far = turn(x, at + RIM - (half * (l + 1) - RIM))
        near = jnp.where((lane >= at) & (lane < at + RIM), near, 0.0)
        both = jnp.where((lane >= at + RIM) & (lane < at + 2 * RIM), far, near)
        out = both if out is None else out + both
    return out


def unpack_rim(x, r, l):
    lane = lane_index()
    half = LANES // 2
    at = 2 * RIM * r
    near = turn(x, half * l - at)
    far = turn(x, half * (l + 1) - RIM - (at + RIM))
    near = jnp.where((lane >= half * l) & (lane < half * l + RIM), near, 0.0)
    return jnp.where((lane >= half * (l + 1) - RIM) & (lane < half * (l + 1)), far, near)


def add_faces(na, par_ref, v, a_ref, b_ref):
    ghost = 2 * na
    for at in range(na):
        for r in range(8):
            lower, upper = got_faces(par_ref, at * 8 + r, a_ref, b_ref)
            v[at, r, 0] = v[at, r, 0] + lower
            v[na + at, r, 7] = v[na + at, r, 7] + upper
    lower, upper = got_faces(par_ref, na * 8, a_ref, b_ref)
    for r in range(8):
        v[ghost, r, 0] = v[ghost, r, 0] + unpack_rim(lower, r, 0)
        v[ghost, r, 7] = v[ghost, r, 7] + unpack_rim(upper, r, 1)


def owners(l2s, me, total, chan):
    elements = l2s.shape[1]
    if elements & (elements - 1) == 0:
        owner = lax.shift_right_logical(l2s, elements.bit_length() - 1)
        slot = l2s & (elements - 1)
    else:
        owner = l2s // elements
        slot = l2s - owner * elements
    ahead = owner - me
    ahead = jnp.where(ahead < 0, ahead + total, ahead)
    group = jnp.where(ahead == 1, 1, jnp.where(ahead == total - 1, 2, jnp.where(ahead == chan, 3, 0)))
    return slot, group


def fluid_kernel(
    na, planes, chan, total, me_ref, par_ref, u_ref, l2s_ref, k_ref, p_ref, q_ref, wr_ref,
    out_ref, cond_ref, s1_ref, s2_ref, s3_ref, z_ref, fa_ref, fb_ref, t_ref, uf_ref
):
    i = pl.program_id(0)
    k = k_ref[...]
    curve_matrix = time_step * viscosity * (DERIV @ DERIV)
    slope_matrix = time_step * DERIV
    for c in range(3):
        for s in range(8):
            line = [u_ref[c, r, s].astype(f32) for r in range(8)]
            for r in range(8):
                uf_ref[c, r, s] = line[r]
            parts = halves_of(line)
            slope = combined(slope_matrix, parts, -1)
            curve = combined(curve_matrix, parts, 1)
            for r in range(8):
                t_ref[c, r, s] = curve[r] - uf_ref[0, r, s] * slope[r]
    for p in range(2):
        speed = [None] * 32
        for c in range(3):
            x = uf_ref[c, 4 * p : 4 * p + 4].reshape(2, 128, LANES)
            x = jnp.concatenate([x[0], x[1]], 1).astype(bf16)
            y = jnp.dot(k, jnp.concatenate([x, x], 0), preferred_element_type=f32)
            for h in range(2):
                part = y[:, h * LANES : (h + 1) * LANES].reshape(3, 2, 8, 8, LANES)
                for q in range(2):
                    r = 4 * p + 2 * h + q
                    for s in range(8):
                        change = t_ref[c, r, s] - uf_ref[1, r, s] * part[0, q, s] - uf_ref[2, r, s] * part[1, q, s]
                        new = (part[2, q, s] + change).astype(bf16)
                        out_ref[c, r, s] = new
                        new = new.astype(f32)
                        n = (2 * h + q) * 8 + s
                        speed[n] = new * new if speed[n] is None else speed[n] + new * new
        for n, value in enumerate(speed):
            t_ref[0, 4 * p + n // 8, n % 8] = 1.0 + 0.5 * value
    cond_ref[i] = t_ref[0].reshape(512, LANES).astype(bf16)
    source_planes(na, planes, par_ref, p_ref, q_ref, wr_ref, z_ref, fa_ref, fb_ref)

    @pl.when(i == pl.num_programs(0) - 1)
    def _():
        elements = l2s_ref.shape[-1]
        cond = jnp.concatenate([cond_ref[n] for n in range(cond_ref.shape[0])], 1)
        slot, group = owners(l2s_ref[...], me_ref[0], total, chan)
        kinds = lax.broadcasted_iota(jnp.int32, (16, elements), 0)
        marks = (kinds == group).astype(f32).astype(bf16)
        before = lax.broadcasted_iota(jnp.int32, (elements, elements), 0) < lax.broadcasted_iota(
            jnp.int32, (elements, elements), 1
        )
        rank = jnp.dot(marks, before.astype(f32).astype(bf16), preferred_element_type=f32).astype(jnp.int32)
        high = lax.shift_right_logical(slot, 5)
        codes = jnp.concatenate(
            [jnp.broadcast_to(high, (8, elements)), jnp.broadcast_to(slot - high * 32, (8, elements))], 0
        )
        tagged = jnp.concatenate([cond, codes.astype(f32).astype(bf16)], 0)
        room = s1_ref.shape[-1]
        position = lax.broadcasted_iota(jnp.int32, (room, elements), 0)
        even = me_ref[0] % 2 == 0
        one, two = rank[1:2], rank[2:3]
        sends = (
            (jnp.where(even, 1, 2), jnp.where(even, one, two), s1_ref),
            (jnp.where(even, 2, 1), jnp.where(even, two, one), s2_ref),
            (3, rank[3:4], s3_ref),
        )
        for g, order, ref in sends:
            take = ((position == order) & (group == g)).astype(f32).astype(bf16)
            ref[...] = lax.dot_general(tagged, take, NT, preferred_element_type=f32).astype(bf16)


def keep_kernel(chan, total, me_ref, cond_ref, l2s_ref, own_ref):
    elements = l2s_ref.shape[-1]
    cond = jnp.concatenate([cond_ref[n] for n in range(cond_ref.shape[0])], 1)
    slot, group = owners(l2s_ref[...], me_ref[0], total, chan)
    place = lax.broadcasted_iota(jnp.int32, (elements, elements), 0)
    keep = ((place == slot) & (group == 0)).astype(f32).astype(bf16)
    own_ref[...] = lax.dot_general(cond, keep, NT, preferred_element_type=f32).astype(bf16)


def unpack_kernel(
    na, z_hbm, own_ref, r1_ref, r2_ref, r3_ref, dc_ref, wt_ref, wk_ref, behind_ref, ahead_ref, z_ref, sems
):
    copies = [pltpu.make_async_copy(z_hbm.at[j], z_ref.at[j], sems.at[j]) for j in range(2 * na)]
    for copy in copies:
        copy.start()
    rows = weight_rows(wt_ref[...] * KRYLOV_SCALE)
    got = jnp.concatenate([r[0:512] for r in (r1_ref, r2_ref, r3_ref)], 1)
    tags = [r[512:528].astype(f32) for r in (r1_ref, r2_ref, r3_ref)]
    slots = [(t[0:1] * 32.0 + t[8:9]).astype(jnp.int32) for t in tags]
    slot = jnp.concatenate(slots, 1)
    for j in range(2 * na):
        place = lax.broadcasted_iota(jnp.int32, (LANES, slot.shape[1]), 0) + j * LANES
        put = (place == slot).astype(f32).astype(bf16)
        cols = slice(j * LANES, (j + 1) * LANES)
        moved = own_ref[:, cols].astype(f32) + lax.dot_general(got, put, NT, preferred_element_type=f32)
        kappa = (moved * dc_ref[0:1, cols]).reshape(8, 8, 8, LANES)
        for r in range(8):
            for s in range(8):
                wk_ref[j, r, s] = rows[r][s] * kappa[r, s]
    rows = lambda j: wk_ref[j].reshape(512, LANES)
    behind_ref[...], ahead_ref[...] = send_rims(rows, rows, na)
    for copy in copies:
        copy.wait()


def lines_t(k_ref, blocks):
    out = []
    for p in range(0, len(blocks), 2):
        pair = jnp.concatenate(blocks[p : p + 2], 1)
        high = pair.astype(bf16)
        low = (pair - high.astype(f32)).astype(bf16)
        y = jnp.dot(k_ref[...], jnp.concatenate([high, low], 0), preferred_element_type=f32)
        y = y[:128] + y[128:]
        out += [y[:, n * LANES : (n + 1) * LANES].reshape(2, 8, 8, LANES) for n in range(len(blocks[p : p + 2]))]
    return out


def blocks_of(x):
    x = x.reshape(4, 128, LANES)
    return [x[n] for n in range(4)]


def squares(v, j, other, iw_ref):
    sums = {}
    for r in range(8):
        for s in range(8):
            key = (0 if r == 0 else 2 if r == 7 else 1, 0 if s == 0 else 2 if s == 7 else 1)
            x = v[j, r, s]
            pair = (x * x,) if other is None else (x * x, x * other[j, r, s])
            old = sums.get((key, r))
            sums[(key, r)] = pair if old is None else tuple(a + b for a, b in zip(old, pair))
    total = None
    for (key, _), pair in sums.items():
        weight = iw_ref[j, key[0] * 3 + key[1]]
        pair = tuple(weight * a for a in pair)
        total = pair if total is None else tuple(a + b for a, b in zip(total, pair))
    return total


def gradient_r(v, j, g):
    for s in range(8):
        for r, value in enumerate(along(DERIV, [v[j, r, s] for r in range(8)])):
            g[r, s] = value


def fluxes(v, j, wk, c, g, f1, f2):
    gradient_r(v, j, g)
    for r in range(8):
        second = along(DERIV, [v[j, r, s] for s in range(8)])
        k = wk(r)
        for s in range(8):
            first = g[r, s]
            f2[j, r, s] = k[s] * (second[s] + c * first)
            f1[j, r, s] = k[s] * (first + c * second[s])


def lateral_faces(na, par_ref, v, wk, f1, f2, base, kf_ref, kb_ref, a_ref, b_ref):
    rows = [[(l * na + at, 7 * l) for at in range(na)] + [(2 * na, 7 * l)] for l in range(2)]
    flat = rows[0] + rows[1]

    def lines(k_ref, xs):
        blocks = []
        for n in range(0, len(xs), 2):
            blocks.append(jnp.concatenate([x.reshape(64, LANES) for x in xs[n : n + 2]], 0))
        out = []
        for part in lines_t(k_ref, blocks):
            part = part.reshape(2, 8, 8, LANES)
            out += [part[0], part[1]]
        return out

    thirds = lines(kf_ref, [v[j, :, s] for j, s in flat])
    scaled = []
    for (j, s), third in zip(flat, thirds):
        scaled.append(jnp.stack([wk(j, r, s) * third[r] for r in range(8)]))
    thirds = lines(kb_ref, scaled)
    faces = []
    for (j, s), third in zip(flat, thirds):
        first = along(DERIV.T, [f1[j, r, s] for r in range(8)])
        face = []
        for r in range(8):
            second = sum(float(DERIV[i, s]) * f2[j, r, i] for i in range(8) if DERIV[i, s] != 0.0)
            face.append(second + (base[r] * float(GLL_W[s])) * v[j, r, s] + first[r] + third[r])
        faces.append(face)
    for l in range(2):
        row = faces[l * (na + 1) : (l + 1) * (na + 1)]
        far, near = axial_row(l, [x[7] for x in row], [x[0] for x in row])
        for x, last, start in zip(row, far, near):
            x[7], x[0] = last, start
    for at in range(na):
        for r in range(8):
            send_faces(par_ref, at * 8 + r, faces[at][r], faces[na + 1 + at][r], a_ref, b_ref)
    send_faces(par_ref, na * 8, pack_rim(faces[na], 0), pack_rim(faces[2 * na + 1], 1), a_ref, b_ref)


def mass_rows(wt, base):
    for r in range(8):
        base[r] = wt * float(GLL_W[r] * coolant_throughput * KRYLOV_SCALE)


def flux_kernel(na, first, *refs):
    refs = list(refs)
    take = lambda n: [refs.pop(0) for _ in range(n)]
    ghost = 2 * na
    if first:
        par_ref, _, wk_ref, b_in, a_in, dc_ref = take(6)
    else:
        par_ref, _, b_in, a_in, wk_ref, wkg_ref, cr_ref = take(7)
    wt_ref, kf_ref, kb_ref, v, f1, f2, a_out, b_out = take(8)
    if first:
        wkg_ref, cr_ref = take(2)
    g, base = refs
    if first:
        even = par_ref[5] == 0
        a, b = a_in[...], b_in[...]
        rims = place_rims(jnp.where(even, a, b), jnp.where(even, b, a))
        v[ghost] = rims[0:512].reshape(8, 8, 8, LANES)
        wkg_ref[...] = rims[640:1152].reshape(8, 8, 8, LANES)
        for j in range(ghost):
            cr_ref[j] = jnp.broadcast_to(dc_ref[1:2, j * LANES : (j + 1) * LANES], (8, LANES))
        cr_ref[ghost] = rims[512:520]
        assemble_axial(na, v)
    else:
        add_faces(na, par_ref, v, a_in, b_in)
    mass_rows(wt_ref[...], base)
    for j in range(ghost + 1):
        if j < ghost:
            wk = lambda r: wk_ref[j, r]
        else:
            wk = lambda r: wkg_ref[r]
        fluxes(v, j, wk, cr_ref[j], g.at[j % 2], f1, f2)
    face_wk = lambda j, r, s: wk_ref[j, r, s] if j < ghost else wkg_ref[r, s]
    lateral_faces(na, par_ref, v, face_wk, f1, f2, base, kf_ref, kb_ref, a_out, b_out)


def rest_kernel(na, first, *refs):
    refs = list(refs)
    prev = None if first else refs.pop(0)
    v, f1, f2, wk_ref, wkg_ref, wt_ref, iw_ref, kf_ref, kb_ref, y, dots, base, f3 = refs
    ghost = 2 * na
    mass_rows(wt_ref[...], base)
    totals = None
    for j in range(ghost + 1):
        if j < ghost:
            sums = squares(v, j, prev, iw_ref)
            totals = sums if totals is None else [a + b for a, b in zip(totals, sums)]
        for p, part in enumerate(lines_t(kf_ref, blocks_of(v[j]))):
            for q in range(2):
                r = 2 * p + q
                f3[j % 2, r] = (wk_ref[j, r] if j < ghost else wkg_ref[r]) * part[q]
        parts = lines_t(kb_ref, blocks_of(f3[j % 2]))
        for r in range(8):
            for s, value in enumerate(along(DERIV.T, [f2[j, r, s] for s in range(8)])):
                y[j, r, s] = value + (base[r] * float(GLL_W[s])) * v[j, r, s]
        for s in range(8):
            for r, value in enumerate(along(DERIV.T, [f1[j, r, s] for r in range(8)])):
                y[j, r, s] = y[j, r, s] + value + parts[r // 2][r % 2, s]
    for k, value in enumerate(totals):
        dots[k] = jnp.broadcast_to(jnp.sum(jnp.sum(value, 0, keepdims=True), 1, keepdims=True), (8, LANES))
    assemble_axial(na, y)
    assemble_lateral(na, y)


def last_kernel(na, par_ref, _, b_in, a_in, wk_ref, cr_ref, prev, wt_ref, iw_ref, kf_ref, d0, d1, d2, d3, v, all_dots, g, base):
    ghost = 2 * na
    add_faces(na, par_ref, v, a_in, b_in)
    mass_rows(wt_ref[...], base)
    totals = None
    for j in range(ghost):
        gj = g.at[j % 2]
        third = lines_t(kf_ref, blocks_of(v[j]))
        sums = list(squares(v, j, prev, iw_ref))
        gradient_r(v, j, gj)
        c = 2.0 * cr_ref[j]
        total = None
        for r in range(8):
            line = [v[j, r, s] for s in range(8)]
            second = along(DERIV, line)
            row = None
            for s in range(8):
                one, two, three = gj[r, s], second[s], third[r // 2][r % 2, s]
                term = (base[r] * float(GLL_W[s])) * (line[s] * line[s])
                term = term + wk_ref[j, r, s] * (one * (one + c * two) + two * two + three * three)
                row = term if row is None else row + term
            total = row if total is None else total + row
        sums.append(total)
        totals = sums if totals is None else [a + b for a, b in zip(totals, sums)]
    lane = lane_index(1)
    rows = [d0[0], d1[1], d1[0], d2[1], d2[0], d3[1], d3[0], totals[1], totals[0], totals[2]]
    out = jnp.zeros((1, LANES), f32)
    for k, row in enumerate(rows):
        if k < 2 * ITERS - 3:
            row = row[0:1]
        else:
            row = jnp.sum(jnp.sum(row, 0, keepdims=True), 1, keepdims=True)
        out = jnp.where(lane == k, row, out)
    all_dots[...] = jnp.broadcast_to(out[None], all_dots.shape)


def solve_moments(m_ref, coef_ref):
    sums = jnp.sum(m_ref[:, 0, :], 0, keepdims=True)
    lane = lane_index(1)
    m = [jnp.sum(jnp.where(lane == k, sums, 0.0), 1, keepdims=True) for k in range(2 * ITERS)]
    n = ITERS
    low = [[None] * n for _ in range(n)]
    diag = [None] * n
    for j in range(n):
        acc = [m[i + j + 1] for i in range(n)]
        for k in range(j):
            scaled = low[j][k] * diag[k]
            for i in range(j, n):
                acc[i] = acc[i] - low[i][k] * scaled
        diag[j] = acc[j]
        for i in range(j + 1, n):
            low[i][j] = acc[i] / acc[j]
    z = []
    for i in range(n):
        value = m[i]
        for k in range(i):
            value = value - low[i][k] * z[k]
        z.append(value)
    c = [z[i] / diag[i] for i in range(n)]
    for i in reversed(range(n)):
        for k in range(i + 1, n):
            c[i] = c[i] - low[k][i] * c[k]
    for k, x in enumerate(c):
        coef_ref[k] = jnp.broadcast_to(x * KRYLOV_SCALE, (8, LANES))


def combine_kernel(na, planes, m_ref, v0, v1, v2, v3, v4, out_ref, coef_ref):
    i = pl.program_id(0)

    @pl.when(i == 0)
    def _():
        solve_moments(m_ref, coef_ref)

    c = [coef_ref[k] for k in range(ITERS)]
    step = 2 * na
    for n in range(planes):
        r = i * planes + n
        for s in range(8):
            base = (n * 8 + s) * 8 * step
            for l in range(2):
                for at in range(na):
                    x = None
                    for coef, v in zip(c, (v0, v1, v2, v3, v4)):
                        term = coef * v[l * na + at, r, s]
                        x = term if x is None else x + term
                    out_ref[pl.ds(base + at * 2 + l, 8, stride=step), :] = x


def slab_swap(x, start):
    n, m = lax.axis_size("slab"), lax.axis_size("chan")
    pairs = [(i * m + c, (i + 1) * m + c) for i in range(start, n - 1, 2) for c in range(m)]
    busy = {i for pair in pairs for i in pair}
    pairs += [(i, i + 1) for i in range(0, n * m, 2) if i not in busy]
    return lax.ppermute(x, ("slab", "chan"), pairs + [(j, i) for i, j in pairs])


def swap(x, axis, start):
    n = lax.axis_size(axis)
    pairs = [((start + i) % n, (start + i + 1) % n) for i in range(0, n, 2)]
    return lax.ppermute(x, axis, pairs + [(j, i) for i, j in pairs])


def around(x, by):
    n = lax.axis_size("slab") * lax.axis_size("chan")
    return lax.ppermute(x, ("slab", "chan"), [(i, (i + by) % n) for i in range(n)])


def swap_around(x, start):
    n = lax.axis_size("slab") * lax.axis_size("chan")
    pairs = [((start + i) % n, (start + i + 1) % n) for i in range(0, n, 2)]
    return lax.ppermute(x, ("slab", "chan"), pairs + [(j, i) for i, j in pairs])


def product_weights(count_l, count_a):
    slab, chan = lax.axis_index("slab"), lax.axis_index("chan")
    axial = slab * count_a + jnp.arange(count_a)
    lateral = chan * count_l + jnp.arange(count_l)
    last_a = lax.axis_size("slab") * count_a - 1
    last_l = lax.axis_size("chan") * count_l - 1
    half = lambda cond: jnp.where(cond, 0.5, 1.0).astype(f32)
    along_a = jnp.stack([half(axial > 0), jnp.ones(count_a, f32), half(axial < last_a)])
    along_l = jnp.stack([half(lateral > 0), jnp.ones(count_l, f32), half(lateral < last_l)])
    weights = along_a[:, None, None, :] * along_l[None, :, :, None]
    weights = weights.reshape(9, -1, LANES).transpose(1, 0, 2)
    return jnp.broadcast_to(weights[:, :, None, :], weights.shape[:2] + (8, LANES))


def on_device(
    stream_speed_field,
    liquid_to_solid_element,
    previous_panel_warmth,
    pointwise_energy_source,
    coked_element_flags,
    coking_thickness_plies,
):
    count_l, count_a = coked_element_flags.shape
    assert count_l == 2 and count_a % LANES == 0
    elements = count_l * count_a
    na = count_a // LANES
    tiles = count_l * na
    chan = lax.axis_size("chan")
    total = lax.axis_size("slab") * chan
    slab_at, chan_at = lax.axis_index("slab"), lax.axis_index("chan")
    me = (slab_at * chan + chan_at).astype(jnp.int32).reshape(1)
    position = [
        chan_at % 2,
        chan_at > 0,
        chan_at < chan - 1,
        slab_at > 0,
        slab_at < lax.axis_size("slab") - 1,
        slab_at % 2,
    ]
    position = jnp.stack([jnp.asarray(x, jnp.int32) for x in position])

    wt = jnp.asarray(np.broadcast_to(GLL_W[:, None], (8, LANES)), f32)
    wr = jnp.asarray(np.broadcast_to((GLL_W[:, None] * GLL_W)[:, :, None], (8, 8, LANES)), f32)
    kf, kb = (jnp.asarray(k) for k in line_matrices())
    kfluid = jnp.asarray(fluid_matrix())

    layers = coking_thickness_plies.astype(f32)
    flags = coked_element_flags.astype(f32)
    damping = jnp.where(coked_element_flags == 1, 1.0 / (1.0 + layer_damp * layers), jnp.ones_like(layers))
    cross = cross_gain * flags * layers / (layers + 1.0)
    dc = jnp.stack([damping.reshape(elements), cross.reshape(elements)])
    iw = product_weights(count_l, count_a)

    def as_rows(x):
        x = x.reshape(8, 8, 8, count_l, na, LANES).transpose(0, 1, 2, 4, 3, 5)
        return x.reshape(512 * tiles, LANES)

    field = (tiles, 8, 8, 8, LANES)
    whole = (tiles + 1, 8, 8, 8, LANES)
    shape = lambda s, d=f32: jax.ShapeDtypeStruct(s, d)
    kept = vmem
    split = elements // LANES
    width = LANES
    room = elements // 4
    in_hbm = lambda x: pltpu.with_memory_space_constraint(x, pltpu.HBM)
    here = lambda: pl.BlockSpec(memory_space=pltpu.VMEM)
    scalars = pl.BlockSpec(memory_space=pltpu.SMEM)
    steps = 4
    rows = 512 * tiles // steps
    l2s = liquid_to_solid_element.reshape(1, elements)
    out = pl.pallas_call(
        functools.partial(fluid_kernel, na, 8 // split, chan, total),
        grid=(split,),
        in_specs=[
            scalars,
            scalars,
            pl.BlockSpec((3, 8, 8, 8, width), lambda i: (0, 0, 0, 0, i)),
            pl.BlockSpec((1, elements), lambda i: (0, 0)),
            pl.BlockSpec(kfluid.shape, lambda i: (0, 0)),
        ]
        + [pl.BlockSpec((512 * tiles // split, LANES), lambda i: (i, 0))] * 2
        + [pl.BlockSpec((8, 8, LANES), lambda i: (0, 0, 0))],
        out_specs=[pl.BlockSpec((3, 8, 8, 8, width), lambda i: (0, 0, 0, 0, i))]
        + [here()] * 4
        + [pl.BlockSpec((tiles, 8 // split, 8, 8, LANES), lambda i: (0, i, 0, 0, 0))]
        + [here()] * 2,
        out_shape=[shape(stream_speed_field.shape, bf16), kept((split, 512, width), bf16)]
        + [kept((528, room), bf16)] * 3
        + [pltpu.HBM(field, f32), kept((na, 8, 8, LANES)), kept((na, 8, 8, LANES))],
        scratch_shapes=[pltpu.VMEM((3, 8, 8, 8, width), f32)] * 2,
        compiler_params=pltpu.CompilerParams(vmem_limit_bytes=24 * 1024 * 1024),
    )(
        me,
        position,
        in_hbm(stream_speed_field),
        in_hbm(l2s),
        in_hbm(kfluid),
        in_hbm(as_rows(previous_panel_warmth)),
        in_hbm(as_rows(pointwise_energy_source)),
        in_hbm(wr),
    )
    stepped, cond, out_even, out_odd, out_far, z, a, b = out
    received = [around(out_far, chan), swap_around(out_odd, 1), swap_around(out_even, 0)]
    (own,) = call(
        functools.partial(keep_kernel, chan, total), [kept((512, elements), bf16)], me, cond, l2s, smem=1
    )
    a, b, own = lax.optimization_barrier((a, b, own))
    b, a = swap(b, "chan", 1), swap(a, "chan", 0)
    wk, wk_behind, wk_ahead, z = call(
        functools.partial(unpack_kernel, na),
        [kept(field), kept((2 * RIM, 512)), kept((2 * RIM, 512)), kept(field)],
        in_hbm(z),
        own,
        *received,
        dc,
        wt,
        hbm=1,
        scratch=[pltpu.SemaphoreType.DMA((tiles,))],
    )
    y, a, b = call(
        functools.partial(rim_kernel, na),
        [kept(whole), kept((2 * RIM, 1152)), kept((2 * RIM, 1152))],
        position,
        z,
        b,
        a,
        dc,
        wk_behind,
        wk_ahead,
        smem=1,
    )
    b, a = slab_swap(b, 1), slab_swap(a, 0)

    basis, products = [], []
    face = (8 * na + 1, 8, LANES)
    for number in range(ITERS - 1):
        first = number == 0
        outs = [kept(whole)] * 3 + [kept(face)] * 2
        if first:
            args = (y, wk, b, a, dc)
            outs += [kept((8, 8, 8, LANES)), kept((tiles + 1, 8, LANES))]
        else:
            args = (y, b, a, wk, wkg, cr)
        got = call(
            functools.partial(flux_kernel, na, first),
            outs,
            position,
            *args,
            wt,
            kf,
            kb,
            smem=1,
            scratch=[pltpu.VMEM((2, 8, 8, 8, LANES), f32), pltpu.VMEM((8, 8, LANES), f32)],
            input_output_aliases={1: 0},
        )
        if first:
            wkg, cr = got[5:]
        v, f1, f2, a, b = got[:5]
        b, a = swap(b, "chan", 1), swap(a, "chan", 0)
        y, dots = call(
            functools.partial(rest_kernel, na, first),
            [kept(whole), kept((2, 8, LANES))],
            *basis[-1:],
            v,
            f1,
            f2,
            wk,
            wkg,
            wt,
            iw,
            kf,
            kb,
            scratch=[pltpu.VMEM((8, 8, LANES), f32), pltpu.VMEM((2, 8, 8, 8, LANES), f32)],
        )
        basis.append(v)
        products.append(dots)
    v, sums = call(
        functools.partial(last_kernel, na),
        [kept(whole), kept((total, 1, LANES))],
        position,
        y,
        b,
        a,
        wk,
        cr,
        basis[-1],
        wt,
        iw,
        kf,
        *products,
        smem=1,
        input_output_aliases={1: 0},
        scratch=[pltpu.VMEM((2, 8, 8, 8, LANES), f32), pltpu.VMEM((8, 8, LANES), f32)],
    )
    basis.append(v)
    sums = lax.all_to_all(sums, ("slab", "chan"), 0, 0)
    x = pl.pallas_call(
        functools.partial(combine_kernel, na, 1),
        grid=(8,),
        in_specs=[here()] * 6,
        out_specs=pl.BlockSpec((64 * tiles, LANES), lambda i: (i, 0)),
        out_shape=shape((512 * tiles, LANES)),
        scratch_shapes=[pltpu.VMEM((ITERS, 8, LANES), f32)],
        compiler_params=pltpu.CompilerParams(vmem_limit_bytes=12 * 1024 * 1024),
    )(sums, *basis)
    x = x.reshape(8, 8, 8, na, count_l, LANES).transpose(0, 1, 2, 4, 3, 5)
    return stepped, x.reshape(8, 8, 8, count_l, count_a)


def solution(mesh):
    in_specs = (
        P(None, None, None, None, ("slab", "chan")),
        P(("slab", "chan")),
        P(None, None, None, "chan", "slab"),
        P(None, None, None, "chan", "slab"),
        P("chan", "slab"),
        P("chan", "slab"),
    )
    out_specs = (P(None, None, None, None, ("slab", "chan")), P(None, None, None, "chan", "slab"))
    return jax.shard_map(
        on_device, mesh=mesh, in_specs=in_specs, out_specs=out_specs, check_vma=False
    )
```
